32 devices in a mesh: dp: 4 (over x, core), seq: 8 (over z, y).
Axes of the slice: x: 2, y: 2, z: 4, core: 2. Of those that a mesh axis runs over, the one named last changes fastest.
Arguments:
- tokens: bfloat16 [8192, 1536], P(('dp', 'seq')), may hold values from -6 to 6
- lengths: int32 [4, 8], P('dp'), may hold values from 1 to 1024, 1920 in all within a row
- cotangent: bfloat16 [8192, 1536], P(('dp', 'seq')), may hold values from -6 to 6
- gain_attn: bfloat16 [1536], P('seq'), may hold values from 0.25 to 1.75
- w_query: bfloat16 [1536, 1536], P('seq'), may hold values from -0.15625 to 0.15625
- w_key: bfloat16 [1536, 768], P('seq'), may hold values from -0.15625 to 0.15625
- w_value: bfloat16 [1536, 768], P('seq'), may hold values from -0.15625 to 0.15625
- w_out: bfloat16 [1536, 1536], P('seq'), may hold values from -0.625 to 0.625
- gain_mlp: bfloat16 [1536], P('seq'), may hold values from 0.25 to 1.75
- w_gate: bfloat16 [1536, 4096], P('seq'), may hold values from -0.15625 to 0.15625
- w_up: bfloat16 [1536, 4096], P('seq'), may hold values from -0.15625 to 0.15625
- w_down: bfloat16 [4096, 1536], P('seq'), may hold values from -0.09375 to 0.09375
Outputs:
- output: bfloat16 [8192, 1536], P(('dp', 'seq'))
- grad_tokens: float32 [8192, 1536], P(('dp', 'seq'))
- grad_gain_attn: float32 [1536], P('seq')
- grad_query: float32 [1536, 1536], P('seq')
- grad_key: float32 [1536, 768], P('seq')
- grad_value: float32 [1536, 768], P('seq')
- grad_out: float32 [1536, 1536], P('seq')
- grad_gain_mlp: float32 [1536], P('seq')
- grad_gate: float32 [1536, 4096], P('seq')
- grad_up: float32 [1536, 4096], P('seq')
- grad_down: float32 [4096, 1536], P('seq')
The draws below stay inside these ranges and needn't reach their ends.
Inputs may be any that keep to these rules, and one draw needn't show every extreme that they name: Each group's lengths sum to 1920; the last 128 tokens of a group are padding; one length equals 1024.
All inputs are finite; a program needn't handle non-finite values.
Results may differ from the reference program's by a relative error of at most 0.017.
Values may be sent and summed in bfloat16 or wider, within the bound.
No kernel may reach another device: no remote copies, remote signals or barrier semaphores. Data moves between devices by JAX's collectives and lax.ppermute only.
A program may use at most 320 MiB of HBM per device.

```python
import math
import jax
import jax.numpy as jnp
import numpy as np
from jax import lax

D = 1536
HEADS = 16
KV_HEADS = 8
HEAD = 96
FF = 4096
WINDOW = 512
DOCS = 8
GROUP = 2048
TOKENS = 8192
LONGEST = 1024
FILLED = 1920
N_DP = 4


def steps_of(key, dims, shards, low, top_value):
    def one(dim, blocks):
        draws = jax.random.uniform(jax.random.fold_in(jax.random.fold_in(key, 6), dim), (blocks,), jnp.float32, low / len(shards), top_value / len(shards))
        return jnp.repeat(jnp.exp(draws), dims[dim] // blocks).reshape((-1,) + (1,) * (len(dims) - dim - 1))

    level = one(*shards[0])
    for cut in shards[1:]:
        level = level * one(*cut)
    return level


def length_profile(count, total, limit, slope):
    portions = [(1 << 20) // math.isqrt(standing ** slope) + 1 for standing in range(2, count + 1)]
    rest, holding = total - limit - (count - 1), [1] * (count - 1)
    while rest > 0:
        movable = [i for i in range(count - 1) if holding[i] < limit]
        mass, left = sum([portions[i] for i in movable]), rest
        for i in movable:
            extra = min(limit - holding[i], max(1, left * portions[i] // mass), rest)
            holding[i] = holding[i] + extra
            rest = rest - extra
    return np.array([limit] + holding)


def uneven_parts(key, amount, total, limit, lean):
    if amount == 2:
        one = jax.random.randint(key, (), max(1, total - limit), min(limit, total - 1) + 1)
        return jnp.stack([one, total - one])
    sizes = jnp.asarray(length_profile(amount, total, limit, lean), jnp.int32)
    couples = (amount - 1) // 2
    donor, receiver = sizes[1:1 + 2 * couples:2], sizes[2:2 + 2 * couples:2]
    room = jnp.minimum(donor - 1, limit - receiver)
    moved = jax.random.randint(jax.random.fold_in(key, 1), (couples,), 0, 1 << 20) % (room + 1)
    sizes = sizes.at[1:1 + 2 * couples:2].set(donor - moved).at[2:2 + 2 * couples:2].set(receiver + moved)
    return sizes[jax.random.permutation(jax.random.fold_in(key, 2), amount)]


def centred(key, shape, deviation, limit, cuts=(), kind=jnp.bfloat16):
    array = deviation * jax.random.normal(key, shape, jnp.float32)
    if cuts:
        array = array * steps_of(key, shape, cuts, -0.22, 0.18)
    return jnp.clip(array, -limit, limit).astype(kind)


def setup_inputs(seed: int = 0) -> dict:
    streams_of = jax.random.split(jax.random.key(seed), 13)
    tokens = centred(streams_of[0], (TOKENS, D), 1.0, 6.0, ((0, 32),))
    lengths = jax.vmap(lambda own: uneven_parts(own, DOCS, FILLED, LONGEST, 2))(jax.random.split(streams_of[1], N_DP)).reshape((N_DP, DOCS)).astype(jnp.int32)
    cotangent = centred(streams_of[2], (TOKENS, D), 1.0, 6.0, ((0, 32),))
    gain_attn = jnp.clip(1.0 + 0.15 * jax.random.normal(streams_of[3], (D,), jnp.float32), 0.25, 1.75).astype(jnp.bfloat16)
    w_query = centred(streams_of[4], (D, D), D ** -0.5, 0.15625, ((0, 8),))
    w_key = centred(streams_of[5], (D, KV_HEADS * HEAD), D ** -0.5, 0.15625, ((0, 8),))
    w_value = centred(streams_of[6], (D, KV_HEADS * HEAD), D ** -0.5, 0.15625, ((0, 8),))
    w_out = centred(streams_of[7], (D, D), (D // 16) ** -0.5, 0.625, ((0, 8),))
    gain_mlp = jnp.clip(1.0 + 0.15 * jax.random.normal(streams_of[8], (D,), jnp.float32), 0.25, 1.75).astype(jnp.bfloat16)
    w_gate = centred(streams_of[9], (D, FF), D ** -0.5, 0.15625, ((0, 8),))
    w_up = centred(streams_of[10], (D, FF), D ** -0.5, 0.15625, ((0, 8),))
    w_down = centred(streams_of[11], (FF, D), FF ** -0.5, 0.09375, ((0, 8),))
    return {"tokens": tokens, "lengths": lengths, "cotangent": cotangent, "gain_attn": gain_attn, "w_query": w_query, "w_key": w_key, "w_value": w_value, "w_out": w_out, "gain_mlp": gain_mlp, "w_gate": w_gate, "w_up": w_up, "w_down": w_down}


EPS = 1e-05
THETA = 100000.0
HIGH = lax.Precision.HIGHEST

@jax.custom_vjp
def low(v):
    return lax.optimization_barrier(v.astype(jnp.bfloat16)).astype(jnp.float32)

@jax.custom_vjp
def low_back(v):
    return v

def low_keep(v):
    return (low(v), None)

def low_pass(kept, grad):
    return (grad,)

def back_keep(v):
    return (v, None)

def back_low(kept, grad):
    return (low(grad),)
low.defvjp(low_keep, low_pass)
low_back.defvjp(back_keep, back_low)

def rms_norm(values, gain):
    return values * lax.rsqrt(lax.optimization_barrier(jnp.mean(values * values, axis=-1, keepdims=True)) + EPS) * gain

def rotate_half(values):
    middle = values.shape[-1] // 2
    return jnp.concatenate([-values[..., middle:], values[..., :middle]], axis=-1)

def rotary(values, cosine, sine):
    return values * cosine + rotate_half(values) * sine

def layout(lengths):
    index = jnp.arange(GROUP, dtype=jnp.int32)
    ends = jnp.cumsum(lengths, axis=1).astype(jnp.int32)
    before = index[None, :, None] >= ends[:, None, :]
    segment = lax.optimization_barrier(jnp.sum(before.astype(jnp.int32), axis=2)).astype(jnp.int32)
    offset = lax.optimization_barrier(jnp.sum(jnp.where(before, lengths[:, None, :], 0), axis=2)).astype(jnp.int32)
    position = index[None, :] - offset
    segment = jnp.where(segment < DOCS, segment, -1).astype(jnp.int32)
    return (segment, position)

def rope_tables(position):
    inverse_freq = THETA ** (-jnp.arange(0, HEAD, 2, dtype=jnp.float32) / HEAD)
    angles = position.astype(jnp.float32)[..., None] * inverse_freq
    angles = jnp.concatenate([angles, angles], axis=-1)
    return (jnp.cos(angles)[..., None, :], jnp.sin(angles)[..., None, :])

def attend_group(query, key, value, segment):
    groups = HEADS // KV_HEADS
    factor = 1.0 / math.sqrt(HEAD)
    key_pad = jnp.concatenate([jnp.zeros((WINDOW, KV_HEADS * HEAD), jnp.float32), key], axis=0)
    value_pad = jnp.concatenate([jnp.zeros((WINDOW, KV_HEADS * HEAD), jnp.float32), value], axis=0)
    seg_pad = jnp.concatenate([jnp.full((WINDOW,), -3, jnp.int32), segment], axis=0)
    distance = WINDOW + jnp.arange(WINDOW, dtype=jnp.int32)[:, None] - jnp.arange(2 * WINDOW, dtype=jnp.int32)[None, :]

    def one_block(number):
        first_row = number * WINDOW
        query_block = lax.dynamic_slice_in_dim(query, first_row, WINDOW).reshape(WINDOW, KV_HEADS, groups, HEAD)
        key_block = lax.dynamic_slice_in_dim(key_pad, first_row, 2 * WINDOW).reshape(2 * WINDOW, KV_HEADS, HEAD)
        value_block = lax.dynamic_slice_in_dim(value_pad, first_row, 2 * WINDOW).reshape(2 * WINDOW, KV_HEADS, HEAD)
        seg_query = lax.dynamic_slice_in_dim(segment, first_row, WINDOW)
        seg_key = lax.dynamic_slice_in_dim(seg_pad, first_row, 2 * WINDOW)
        allowed = (distance == 0) | (seg_query[:, None] == seg_key[None, :]) & (seg_key[None, :] >= 0) & (distance > 0) & (distance < WINDOW)
        scores = low_back(jnp.einsum('qgrd,kgd->grqk', query_block, key_block, precision=HIGH) * factor)
        scores = jnp.where(allowed, scores, -1e+30)
        peak_score = lax.optimization_barrier(jnp.max(scores, axis=-1, keepdims=True))
        exponent = jnp.exp(scores - peak_score)
        probabilities = low(exponent / lax.optimization_barrier(jnp.sum(exponent, axis=-1, keepdims=True)))
        context = jnp.einsum('grqk,kgd->qgrd', probabilities, value_block, precision=HIGH)
        return context.reshape(WINDOW, HEADS * HEAD)
    blocks = lax.map(jax.checkpoint(one_block), jnp.arange(GROUP // WINDOW, dtype=jnp.int32))
    return blocks.reshape(GROUP, HEADS * HEAD)

def group_layer(params, tokens_group, cosine, sine, segment):
    gain_attn, w_query, w_key, w_value, w_out, gain_mlp, w_gate, w_up, w_down = params
    normed = low(rms_norm(tokens_group, gain_attn))
    query = low_back(jnp.dot(normed, w_query, precision=HIGH)).reshape(GROUP, HEADS, HEAD)
    query = low(rotary(query, cosine, sine)).reshape(GROUP, HEADS * HEAD)
    key = low_back(jnp.dot(normed, w_key, precision=HIGH)).reshape(GROUP, KV_HEADS, HEAD)
    key = low(rotary(key, cosine, sine)).reshape(GROUP, KV_HEADS * HEAD)
    value = low(low_back(jnp.dot(normed, w_value, precision=HIGH)))
    context = low(low_back(attend_group(query, key, value, segment)))
    attended = low_back(jnp.dot(context, w_out, precision=HIGH))
    middle = tokens_group + attended
    normed_mlp = low(rms_norm(middle, gain_mlp))
    gate = low_back(jnp.dot(normed_mlp, w_gate, precision=HIGH))
    up_proj = low_back(jnp.dot(normed_mlp, w_up, precision=HIGH))
    hidden = low(jax.nn.silu(gate) * up_proj)
    return middle + low_back(jnp.dot(hidden, w_down, precision=HIGH))

def reference(tokens, lengths, cotangent, gain_attn, w_query, w_key, w_value, w_out, gain_mlp, w_gate, w_up, w_down):
    segment, position = layout(lengths)
    cosine, sine = rope_tables(position)
    params = (gain_attn.astype(jnp.float32), w_query.astype(jnp.float32), w_key.astype(jnp.float32), w_value.astype(jnp.float32), w_out.astype(jnp.float32), gain_mlp.astype(jnp.float32), w_gate.astype(jnp.float32), w_up.astype(jnp.float32), w_down.astype(jnp.float32))

    def forward(inputs, weights):

        def one_group(items):
            return group_layer(weights, items[0], items[1], items[2], items[3])
        result = lax.map(jax.checkpoint(one_group), (inputs.reshape(N_DP, GROUP, D), cosine, sine, segment))
        return result.reshape(TOKENS, D)
    output, pullback = jax.vjp(forward, tokens.astype(jnp.float32), params)
    grad_tokens, grads = pullback(cotangent.astype(jnp.float32))
    return (output.astype(jnp.bfloat16), grad_tokens, grads[0], grads[1], grads[2], grads[3], grads[4], grads[5], grads[6], grads[7], grads[8])
```

```python
import math

import jax
import jax.numpy as jnp
from jax import lax
from jax.sharding import PartitionSpec as P

HEADS = 16
KV_HEADS = 8
HEAD = 96
WINDOW = 512


EPS = 1e-05
THETA = 100000.0
BOTH = ("dp", "seq")
BF = jnp.bfloat16
F32 = jnp.float32


def send(block, target):
    n_dp, n_seq = lax.axis_size("dp"), lax.axis_size("seq")
    route = []
    for d in range(n_dp):
        for s in range(n_seq):
            to = target(d, s)
            if to is not None and 0 <= to[1] < n_seq:
                route.append((d * n_seq + s, to[0] * n_seq + to[1]))
    return lax.ppermute(block, BOTH, route)


def gather_dp(block):
    core = send(block, lambda d, s: (d ^ 1, s))
    far = send(block, lambda d, s: (d ^ 2, s))
    both = send(far, lambda d, s: (d ^ 1, s))
    return [block, core, far, both]


def scatter_dp(blocks):
    to_core = jnp.stack([blocks[1], blocks[3]]).astype(BF)
    core = send(to_core, lambda d, s: (d ^ 1, s)).astype(F32)
    far = send((blocks[2] + core[1]).astype(BF), lambda d, s: (d ^ 2, s))
    return blocks[0] + core[0] + far.astype(F32)


def ring(s, k):
    return ((s // 2 + k) % 4) * 2 + s % 2


def gather_seq(block):
    n_seq = lax.axis_size("seq")
    if n_seq != 8:
        return lax.all_gather(block, "seq", axis=0)
    me = lax.axis_index("seq")
    full = jnp.zeros((n_seq,) + block.shape, block.dtype)
    for k in (0, 1, 3, 2):
        mine = block if k == 0 else send(block, lambda d, s, k=k: (d, ring(s, k)))
        other = send(mine, lambda d, s: (d, s ^ 1))
        full = lax.dynamic_update_index_in_dim(full, mine, ring(me, -k), 0)
        full = lax.dynamic_update_index_in_dim(full, other, ring(me, -k) ^ 1, 0)
    return full


def scatter_seq(blocks):
    n_seq = lax.axis_size("seq")
    if n_seq != 8:
        return lax.psum_scatter(blocks.astype(F32), "seq", scatter_dimension=0)
    me = lax.axis_index("seq")
    pairs = blocks.reshape((4, 2) + blocks.shape[1:])
    y = me % 2
    other = lax.dynamic_index_in_dim(pairs, 1 - y, 1, keepdims=False).astype(BF)
    own = lax.dynamic_index_in_dim(pairs, y, 1, keepdims=False).astype(F32)
    summed = own + send(other, lambda d, s: (d, s ^ 1)).astype(F32)
    z = me // 2
    total = lax.dynamic_index_in_dim(summed, z, 0, keepdims=False)
    for k in (1, 3, 2):
        piece = lax.dynamic_index_in_dim(summed, (z + k) % 4, 0, keepdims=False).astype(BF)
        total = total + send(piece, lambda d, s, k=k: (d, ring(s, k))).astype(F32)
    return total


def gather_out(w_out):
    n_seq, n_dp = lax.axis_size("seq"), lax.axis_size("dp")
    d, me = lax.axis_index("dp"), lax.axis_index("seq")
    if n_seq != 8 or n_dp != 4:
        full = lax.all_gather(w_out, "seq", axis=0, tiled=True)
        rows = full.shape[0] // n_dp
        return lax.dynamic_slice_in_dim(full, d * rows, rows, 0)
    mine = jnp.where(me // 2 == d, w_out, jnp.zeros_like(w_out))
    for k in (1, 3, 2):
        mine = mine + send(w_out, lambda d, s, k=k: (d, ring(s, k)) if s // 2 == d else None)
    other = send(mine, lambda d, s: (d, s ^ 1))
    y = me % 2
    return jnp.concatenate([jnp.where(y == 0, mine, other), jnp.where(y == 0, other, mine)], axis=0)


def scatter_out(grad):
    n_seq, n_dp = lax.axis_size("seq"), lax.axis_size("dp")
    d, me = lax.axis_index("dp"), lax.axis_index("seq")
    if n_seq != 8 or n_dp != 4:
        rows = grad.shape[0]
        full = jnp.zeros((rows * n_dp, grad.shape[1]), F32)
        full = lax.dynamic_update_slice_in_dim(full, grad, d * rows, 0)
        shard = lax.psum_scatter(full, "seq", scatter_dimension=0, tiled=True)
        return lax.psum(shard.astype(BF), "dp").astype(F32)
    pairs = grad.reshape((2, -1) + grad.shape[1:])
    y, z = me % 2, me // 2
    other = lax.dynamic_index_in_dim(pairs, 1 - y, 0, keepdims=False).astype(BF)
    own = lax.dynamic_index_in_dim(pairs, y, 0, keepdims=False)
    summed = own + send(other, lambda d, s: (d, s ^ 1)).astype(F32)
    total = summed
    low = summed.astype(BF)
    for k in (1, 3, 2):
        total = total + send(
            low, lambda d, s, k=k: (d, ring(s, k)) if (s // 2 + k) % 4 == d else None
        ).astype(F32)
    total = jnp.where(z == d, total, 0.0).astype(BF)
    total = total + send(total, lambda d, s: (d ^ 1, s))
    total = total + send(total, lambda d, s: (d ^ 2, s))
    return total.astype(F32)


def order_dp(blocks):
    d = lax.axis_index("dp")
    full = jnp.zeros((len(blocks),) + blocks[0].shape, blocks[0].dtype)
    for k, block in enumerate(blocks):
        full = lax.dynamic_update_index_in_dim(full, block, d ^ k, 0)
    return full


def rotate_half(values):
    middle = values.shape[-1] // 2
    return jnp.concatenate([-values[..., middle:], values[..., :middle]], axis=-1)


def rotate_back(values):
    middle = values.shape[-1] // 2
    return jnp.concatenate([values[..., middle:], -values[..., :middle]], axis=-1)


def rope_tables(position):
    inverse_freq = THETA ** (-jnp.arange(0, HEAD, 2, dtype=jnp.float32) / HEAD)
    angles = position.astype(jnp.float32)[..., None] * inverse_freq
    angles = jnp.concatenate([angles, angles], axis=-1)
    return (jnp.cos(angles)[..., None, :], jnp.sin(angles)[..., None, :])


def layout_rows(lengths, index):
    ends = jnp.cumsum(lengths, axis=1)
    before = index[None, :, None] >= ends[:, None, :]
    segment = jnp.sum(before.astype(jnp.int32), axis=2)
    offset = jnp.sum(jnp.where(before, lengths[:, None, :], 0), axis=2)
    segment = jnp.where(segment < lengths.shape[1], segment, -1)
    segment = jnp.where(index[None, :] < 0, -3, segment)
    return (segment, index[None, :] - offset)


def on_device(
    tokens,
    lengths,
    cotangent,
    gain_attn,
    w_query,
    w_key,
    w_value,
    w_out,
    gain_mlp,
    w_gate,
    w_up,
    w_down,
):
    n_dp, n_seq = lax.axis_size("dp"), lax.axis_size("seq")
    d = lax.axis_index("dp")
    rows, width = tokens.shape
    hops = (WINDOW + rows - 1) // rows
    kv = KV_HEADS // n_dp
    groups = HEADS // KV_HEADS
    q_w, k_w = kv * groups * HEAD, kv * HEAD
    shard = w_query.shape[0]
    ff_shard = w_down.shape[0]
    ff_part = ff_shard // n_dp
    factor = 1.0 / math.sqrt(HEAD)

    gains = jnp.zeros((16, q_w + 2 * k_w), BF)
    gains = gains.at[0, :shard].set(gain_attn).at[1, :shard].set(gain_mlp)
    part_qkv = jnp.concatenate(
        [
            lax.dynamic_slice_in_dim(w_query, d * q_w, q_w, 1),
            lax.dynamic_slice_in_dim(w_key, d * k_w, k_w, 1),
            lax.dynamic_slice_in_dim(w_value, d * k_w, k_w, 1),
        ],
        axis=1,
    )
    part_qkv = jnp.concatenate([part_qkv, gains], axis=0)

    def ff_columns(w):
        w = w.reshape(shard, n_seq, n_dp, ff_part)
        return lax.dynamic_index_in_dim(w, d, 2, keepdims=False).reshape(shard, -1)

    part_gu = jnp.concatenate([ff_columns(w_gate), ff_columns(w_up)], axis=1)
    part_down = lax.dynamic_slice_in_dim(w_down, d * ff_part, ff_part, 0)

    own_rows = gather_dp(tokens)
    lens = jnp.concatenate(gather_dp(lengths), axis=0)
    inputs = jnp.concatenate(own_rows, axis=0)
    got_qkv = gather_seq(part_qkv)
    full_out = gather_out(w_out)
    full_gu = gather_seq(part_gu).reshape(width, -1)
    full_down = gather_seq(part_down).reshape(-1, width)
    upstream_low = jnp.concatenate(gather_dp(cotangent), axis=0)
    full_qkv = got_qkv[:, :shard].reshape(width, -1)
    full_gain_attn = got_qkv[:, shard, :shard].reshape(-1).astype(F32)
    full_gain_mlp = got_qkv[:, shard + 1, :shard].reshape(-1).astype(F32)

    first_row = lax.axis_index("seq") * rows
    local_index = first_row + jnp.arange(rows, dtype=jnp.int32)
    key_index = first_row - hops * rows + jnp.arange((hops + 1) * rows, dtype=jnp.int32)
    segment_query, position = layout_rows(lens, local_index)
    segment_key, _ = layout_rows(lens, key_index)
    distance = local_index[:, None] - key_index[None, :]
    allowed = (distance == 0)[None] | (segment_query[:, :, None] == segment_key[:, None, :]) & (
        segment_key[:, None, :] >= 0
    ) & ((distance > 0) & (distance < WINDOW))[None]
    allowed = allowed[:, None, None]
    cosine, sine = rope_tables(position)

    wide = inputs.astype(F32)
    inverse_attn = lax.rsqrt(jnp.mean(wide * wide, axis=-1, keepdims=True) + EPS)
    normed = (wide * inverse_attn * full_gain_attn).astype(BF)
    qkv = jnp.dot(normed, full_qkv, preferred_element_type=F32).reshape(n_dp, rows, -1)
    query_raw = qkv[..., :q_w].reshape(n_dp, rows, kv * groups, HEAD)
    key_raw = qkv[..., q_w : q_w + k_w].reshape(n_dp, rows, kv, HEAD)
    query = (query_raw * cosine + rotate_half(query_raw) * sine).astype(BF)
    query = query.reshape(n_dp, rows, kv, groups, HEAD)
    key = (key_raw * cosine + rotate_half(key_raw) * sine).astype(BF).reshape(n_dp, rows, k_w)
    value = qkv[..., q_w + k_w :].astype(BF)
    kv_local = jnp.concatenate([key, value], axis=-1)
    pieces = [kv_local]
    for step in range(1, hops + 1):
        pieces = [send(kv_local, lambda d, s, step=step: (d, s + step))] + pieces
    kv_all = jnp.concatenate(pieces, axis=1)
    keys = kv_all[..., :k_w].reshape(n_dp, -1, kv, HEAD)
    values = kv_all[..., k_w:].reshape(n_dp, -1, kv, HEAD)
    scores = jnp.einsum("bqgrd,bkgd->bgrqk", query, keys, preferred_element_type=F32) * factor
    scores = jnp.where(allowed, scores, -1e30)
    peak = jnp.max(scores, axis=-1, keepdims=True)
    exponent = jnp.exp(scores - peak)
    row_total = jnp.sum(exponent, axis=-1, keepdims=True)
    probs = exponent / row_total
    probs_low = probs.astype(BF)
    context = jnp.einsum("bgrqk,bkgd->bqgrd", probs_low, values, preferred_element_type=F32)
    context = context.astype(BF).reshape(n_dp * rows, q_w)
    attended = jnp.dot(context, full_out, preferred_element_type=F32).reshape(n_dp, rows, width)
    middle = tokens.astype(F32) + scatter_dp([attended[k] for k in range(n_dp)])

    inverse_mlp = lax.rsqrt(jnp.mean(middle * middle, axis=-1, keepdims=True) + EPS)
    normed_mlp_own = (middle * inverse_mlp * full_gain_mlp).astype(BF)
    normed_mlp = jnp.concatenate(gather_dp(normed_mlp_own), axis=0)
    gu = jnp.dot(normed_mlp, full_gu, preferred_element_type=F32)
    gate, up = jnp.split(gu, 2, axis=1)
    sigmoid = jax.nn.sigmoid(gate)
    silu = gate * sigmoid
    hidden = (silu * up).astype(BF)
    down = jnp.dot(hidden, full_down, preferred_element_type=F32).reshape(n_dp, rows, width)

    grad_hidden = jnp.einsum("td,fd->tf", upstream_low, full_down, preferred_element_type=F32)
    grad_gate = (grad_hidden * up * sigmoid * (1.0 + gate * (1.0 - sigmoid))).astype(BF)
    grad_up = (grad_hidden * silu).astype(BF)
    grad_gu = jnp.concatenate([grad_gate, grad_up], axis=1)
    grad_normed_mlp = jnp.einsum("tf,df->td", grad_gu, full_gu, preferred_element_type=F32)
    grad_normed_mlp = scatter_dp([part for part in grad_normed_mlp.reshape(n_dp, rows, width)])
    upstream = cotangent.astype(F32)
    scaled = grad_normed_mlp * full_gain_mlp
    grad_gain_mlp = jnp.sum(grad_normed_mlp * middle * inverse_mlp, axis=0)
    grad_middle = (
        upstream
        + inverse_mlp * scaled
        - middle * inverse_mlp**3 * jnp.mean(scaled * middle, axis=-1, keepdims=True)
    )
    grad_attended = jnp.concatenate(gather_dp(grad_middle.astype(BF)), axis=0)

    def shared(total):
        return order_dp(gather_dp(total.astype(BF))).astype(F32)

    grad_w_down = jnp.einsum("tf,td->fd", hidden, upstream_low, preferred_element_type=F32)
    out_down = shared(scatter_seq(grad_w_down.reshape(n_seq, ff_part, width)))
    out_down = out_down.reshape(ff_shard, width)
    grad_w_gu = jnp.einsum("td,tf->df", normed_mlp, grad_gu, preferred_element_type=F32)
    out_gu = shared(scatter_seq(grad_w_gu.reshape(n_seq, shard, -1)))
    out_gu = out_gu.reshape(n_dp, shard, 2, n_seq, ff_part).transpose(2, 1, 3, 0, 4)
    out_gu = out_gu.reshape(2, shard, -1)

    out_out = scatter_out(
        jnp.einsum("ta,td->ad", context, grad_attended, preferred_element_type=F32)
    )
    grad_context = jnp.einsum("td,ad->ta", grad_attended, full_out, preferred_element_type=F32)
    grad_context = grad_context.astype(BF).reshape(n_dp, rows, kv, groups, HEAD)
    grad_probs = jnp.einsum("bqgrd,bkgd->bgrqk", grad_context, values, preferred_element_type=F32)
    delta = jnp.sum(probs * grad_probs, axis=-1, keepdims=True)
    grad_scores = (probs * (grad_probs - delta)).astype(BF)
    grad_query = (
        jnp.einsum("bgrqk,bkgd->bqgrd", grad_scores, keys, preferred_element_type=F32) * factor
    )
    grad_keys = (
        jnp.einsum("bgrqk,bqgrd->bkgd", grad_scores, query, preferred_element_type=F32) * factor
    ).reshape(n_dp, -1, k_w)
    grad_values = jnp.einsum(
        "bgrqk,bqgrd->bkgd", probs_low, grad_context, preferred_element_type=F32
    ).reshape(n_dp, -1, k_w)
    grad_kv = jnp.concatenate([grad_keys, grad_values], axis=-1)
    grad_kv_local = grad_kv[:, hops * rows :]
    for step in range(1, hops + 1):
        at = (hops - step) * rows
        grad_kv_local = grad_kv_local + send(
            grad_kv[:, at : at + rows].astype(BF), lambda d, s, step=step: (d, s - step)
        ).astype(F32)
    grad_query = grad_query.reshape(n_dp, rows, kv * groups, HEAD)
    grad_query = grad_query * cosine + rotate_back(grad_query * sine)
    grad_key = grad_kv_local[..., :k_w].reshape(n_dp, rows, kv, HEAD)
    grad_key = grad_key * cosine + rotate_back(grad_key * sine)
    grad_qkv = jnp.concatenate(
        [
            grad_query.astype(BF).reshape(n_dp * rows, q_w),
            grad_key.astype(BF).reshape(n_dp * rows, k_w),
            grad_kv_local[..., k_w:].astype(BF).reshape(n_dp * rows, k_w),
        ],
        axis=1,
    )
    grad_normed = jnp.einsum("ta,da->td", grad_qkv, full_qkv, preferred_element_type=F32)
    grad_gain_attn = jnp.sum(grad_normed * wide * inverse_attn, axis=0)
    grad_w_qkv = jnp.einsum("td,ta->da", normed, grad_qkv, preferred_element_type=F32)
    gain_rows = jnp.zeros((n_seq, 16, q_w + 2 * k_w), F32)
    gain_rows = gain_rows.at[:, 0, :shard].set(grad_gain_attn.reshape(n_seq, shard))
    gain_rows = gain_rows.at[:, 1, :shard].set(grad_gain_mlp.reshape(n_seq, shard))
    grad_w_qkv = jnp.concatenate([grad_w_qkv.reshape(n_seq, shard, -1), gain_rows], axis=1)
    out_qkv = shared(scatter_seq(grad_w_qkv))
    out_gains = jnp.sum(out_qkv[:, shard : shard + 2, :shard], axis=0)
    out_qkv = out_qkv[:, :shard].transpose(1, 0, 2)

    own = scatter_dp([part for part in grad_normed.reshape(n_dp, rows, width)])
    own_wide, own_inverse = wide[:rows], inverse_attn[:rows]
    scaled = own * full_gain_attn
    grad_tokens = (
        grad_middle
        + own_inverse * scaled
        - own_wide * own_inverse**3 * jnp.mean(scaled * own_wide, axis=-1, keepdims=True)
    )
    output = (middle + scatter_dp([down[k] for k in range(n_dp)])).astype(BF)
    return (
        output,
        grad_tokens,
        out_gains[0],
        out_qkv[..., :q_w].reshape(shard, -1),
        out_qkv[..., q_w : q_w + k_w].reshape(shard, -1),
        out_qkv[..., q_w + k_w :].reshape(shard, -1),
        out_out,
        out_gains[1],
        out_gu[0],
        out_gu[1],
        out_down,
    )


def solution(mesh):
    return jax.shard_map(
        on_device,
        mesh=mesh,
        in_specs=(
            P(("dp", "seq"), None),
            P("dp", None),
            P(("dp", "seq"), None),
            P("seq"),
            P("seq", None),
            P("seq", None),
            P("seq", None),
            P("seq", None),
            P("seq"),
            P("seq", None),
            P("seq", None),
            P("seq", None),
        ),
        out_specs=(
            P(("dp", "seq"), None),
            P(("dp", "seq"), None),
            P("seq"),
            P("seq", None),
            P("seq", None),
            P("seq", None),
            P("seq", None),
            P("seq"),
            P("seq", None),
            P("seq", None),
            P("seq", None),
        ),
        check_vma=False,
    )
```

```python
import math

import jax
import jax.numpy as jnp
from jax import lax
from jax.experimental import pallas as pl
from jax.experimental.pallas import tpu as pltpu
from jax.sharding import PartitionSpec as P

HEADS = 16
KV_HEADS = 8
HEAD = 96
WINDOW = 512


EPS = 1e-05
THETA = 100000.0
BOTH = ("dp", "seq")
BF = jnp.bfloat16
F32 = jnp.float32


def send(block, target):
    n_dp, n_seq = lax.axis_size("dp"), lax.axis_size("seq")
    route = []
    for d in range(n_dp):
        for s in range(n_seq):
            to = target(d, s)
            if to is not None and 0 <= to[1] < n_seq:
                route.append((d * n_seq + s, to[0] * n_seq + to[1]))
    return lax.ppermute(block, BOTH, route)


def after(value, *others):
    return lax.optimization_barrier((value,) + others)[0]


def across_core(d, s):
    return (d ^ 1, s)


def across_x(d, s):
    return (d ^ 2, s)


def across_y(d, s):
    return (d, s ^ 1)


def gather_plane(block, *meanwhile):
    half = block.shape[0] // 2
    from_x = send(block, across_x)
    from_y = send(block, across_y)
    if meanwhile:
        from_x, from_y = lax.optimization_barrier((from_x, from_y, *meanwhile))[:2]
    first = send(from_x[:half], across_y)
    second = send(from_y[half:], across_x)
    return [block, from_y, from_x, first, second]


def scatter_plane(partial, *meanwhile):
    rows = partial.shape[0] // 4
    half = rows // 2
    own, own_y, far, far_y = [partial[i * rows : (i + 1) * rows] for i in range(4)]
    first = send(far_y[:half], across_y)
    second = send(far_y[half:], across_x)

    def plus(a, b):
        return (a.astype(F32) + b.astype(F32)).astype(BF)

    far = jnp.concatenate([plus(far[:half], first), far[half:]], axis=0)
    own_y = jnp.concatenate([own_y[:half], plus(own_y[half:], second)], axis=0)
    from_x, from_y = send(far, across_x), send(own_y, across_y)
    if meanwhile:
        from_x, from_y = lax.optimization_barrier((from_x, from_y, *meanwhile))[:2]
    return own.astype(F32) + from_x.astype(F32) + from_y.astype(F32)


def with_core(block):
    return [block, send(block, across_core)]


def sum_core(mine, other):
    return (mine.astype(F32) + send(other.astype(BF), across_core).astype(F32)).astype(BF)


def along_z(blocks):
    n_seq = lax.axis_size("seq")
    lines = [list(range(y, n_seq, 2)) for y in range(2)]
    return lax.all_to_all(blocks, "seq", 0, 0, axis_index_groups=lines)


def gather_z(block):
    return along_z(jnp.broadcast_to(block[None], (lax.axis_size("seq") // 2,) + block.shape))


def scatter_z(blocks):
    return jnp.sum(along_z(blocks).astype(F32), axis=0)


def line_gather_z(block):
    n_z = lax.axis_size("seq") // 2
    if n_z > 8:
        return gather_z(block)
    z = lax.axis_index("seq") // 2
    up, down = [block], [block]
    for _ in range(1, n_z):
        up.append(send(up[-1], lambda d, s: (d, s + 2)))
        down.append(send(down[-1], lambda d, s: (d, s - 2)))
    full = jnp.zeros((n_z,) + block.shape, block.dtype)
    full = lax.dynamic_update_index_in_dim(full, block, z, 0)
    for r in range(1, n_z):
        full = lax.dynamic_update_index_in_dim(full, up[r] + down[n_z - r], (z - r) % n_z, 0)
    return full


def line_scatter_z(blocks):
    n_z = lax.axis_size("seq") // 2
    if n_z > 8:
        return scatter_z(blocks)
    z = lax.axis_index("seq") // 2

    def own(index):
        index = jnp.clip(index, 0, n_z - 1)
        return lax.dynamic_index_in_dim(blocks, index, 0, keepdims=False)

    up, down = own(n_z - 1), own(0)
    for r in range(1, n_z):
        up = send(up, lambda d, s: (d, s + 2)).astype(F32)
        down = send(down, lambda d, s: (d, s - 2)).astype(F32)
        if r < n_z - 1:
            up = (up + own(n_z - 1 - r + z).astype(F32)).astype(BF)
            down = (down + own(z + r - n_z + 1).astype(F32)).astype(BF)
    return own(z).astype(F32) + up + down


def pair_y(mine, other):
    y = lax.axis_index("seq") % 2
    return jnp.stack([jnp.where(y == 0, mine, other), jnp.where(y == 0, other, mine)])


def turned(d, s):
    return (s // 2, 2 * d + s % 2)


def fold(rows, wide):
    count, columns = rows.shape
    whole = columns // wide
    parts = [rows[:, i * wide : (i + 1) * wide] for i in range(whole)]
    rest = rows[:, whole * wide :]
    if rest.shape[1]:
        times = wide // rest.shape[1]
        step = count // times
        parts.append(
            jnp.concatenate([rest[i * step : (i + 1) * step] for i in range(times)], axis=1)
        )
    return jnp.concatenate(parts, axis=0)


def unfold(folded, columns):
    total, wide = folded.shape
    count = total * wide // columns
    whole = columns // wide
    parts = [folded[i * count : (i + 1) * count] for i in range(whole)]
    if columns % wide:
        rest, narrow = folded[whole * count :], columns % wide
        parts.append(
            jnp.concatenate(
                [rest[:, i * narrow : (i + 1) * narrow] for i in range(wide // narrow)], axis=0
            )
        )
    return jnp.concatenate(parts, axis=1)


def gather_dp(block):
    core = send(block, across_core)
    far = send(block, across_x)
    return [block, core, far, send(far, across_core)]


def order_dp(blocks):
    d = lax.axis_index("dp")
    pairs = [
        (jnp.where(d % 2 == 0, a, b), jnp.where(d % 2 == 0, b, a))
        for a, b in (blocks[:2], blocks[2:])
    ]
    low, high = pairs
    return [jnp.where(d < 2, a, b) for a, b in zip(low, high)] + [
        jnp.where(d < 2, b, a) for a, b in zip(low, high)
    ]


def rope_tables(position):
    lane = jnp.arange(128, dtype=jnp.float32) % (HEAD // 2)
    angles = position.astype(jnp.float32)[..., None] * THETA ** (-2.0 * lane / HEAD)
    return jnp.cos(angles), jnp.sin(angles)


VMEM_BYTES = 60 * 1024 * 1024


def call(kernel, out_shape, flops, moved, **rest):
    return pl.pallas_call(
        kernel,
        out_shape=out_shape,
        compiler_params=pltpu.CompilerParams(vmem_limit_bytes=VMEM_BYTES),
        cost_estimate=pl.CostEstimate(flops=flops, bytes_accessed=moved, transcendentals=0),
        **rest,
    )


def shaped(shape, dtype):
    return jax.ShapeDtypeStruct(shape, dtype)


def iota(shape, axis):
    return lax.broadcasted_iota(jnp.int32, shape, axis)


def dot(a, b):
    return jnp.dot(a, b, preferred_element_type=F32)


def dot_nt(a, b):
    return lax.dot_general(a, b, (((1,), (1,)), ((), ())), preferred_element_type=F32)


def dot_tn(a, b):
    return lax.dot_general(a, b, (((0,), (0,)), ((), ())), preferred_element_type=F32)


def spread(packed, heads, base):
    row, column = iota((packed, heads * 128), 0), iota((packed, heads * 128), 1)
    lane = column % 128
    hit = (row == base + HEAD * (column // 128) + lane) & (lane < HEAD)
    return jnp.where(hit, 1.0, 0.0).astype(BF)


def pack(packed, heads, base):
    column, row = iota((heads * 128, packed), 0), iota((heads * 128, packed), 1)
    lane = column % 128
    hit = (row == base + HEAD * (column // 128) + lane) & (lane < HEAD)
    return jnp.where(hit, 1.0, 0.0).astype(BF)


def on_heads(table, heads, packed):
    row, column = iota((128, packed), 0), iota((128, packed), 1)
    place = jnp.where((row == column % HEAD) & (column < heads * HEAD), 1.0, 0.0).astype(BF)
    high = table.astype(BF)
    rest = table - high.astype(F32)
    middle = rest.astype(BF)
    low = (rest - middle.astype(F32)).astype(BF)
    return dot(high, place) + dot(middle, place) + dot(low, place)


def qkv_kernel(own, from_y, from_x, diag_a, diag_b, gain, cosine, sine, w_own, w_core, normed, qkv, halo):
    rows, lanes = own.shape[0], w_own.shape[1]
    lane = iota((rows, lanes), 1)
    first = lane % HEAD < HEAD // 2
    blocks = [own, from_y, from_x, None]
    for b in range(4):
        at = slice(b * rows, (b + 1) * rows)
        if b < 3:
            x = blocks[b][...].astype(F32)
        else:
            x = jnp.concatenate([diag_a[...], diag_b[...]], axis=0).astype(F32)
        inverse = lax.rsqrt(jnp.mean(x * x, axis=-1, keepdims=True) + EPS)
        low = (x * inverse * gain[...]).astype(BF)
        normed[at, :] = low
        cos_all = on_heads(cosine[at, :], 3, lanes) + jnp.where(lane >= 3 * HEAD, 1.0, 0.0)
        sin_all = on_heads(sine[at, :], 3, lanes)
        turned = []
        for w in (w_own, w_core):
            raw = dot(low, w[...])
            half = jnp.where(
                first, -pltpu.roll(raw, lanes - HEAD // 2, 1), pltpu.roll(raw, HEAD // 2, 1)
            )
            turned.append(raw * cos_all + half * sin_all)
        qkv[0, at, :] = turned[0].astype(BF)
        qkv[1, at, :] = turned[1].astype(BF)
        halo[at, :] = jnp.where(
            lane < lanes // 2, pltpu.roll(turned[1], lanes // 2, 1), turned[0]
        ).astype(BF)


def visible(seg_query, seg_key, a, rows):
    shape = (rows, 3 * rows)
    row, column = iota(shape, 0), iota(shape, 1)
    same = seg_query[0, a] == jnp.concatenate([seg_key[0, a + i] for i in range(3)], axis=1)
    allowed = (column > row) & (column <= row + 2 * rows) & same
    return jnp.concatenate([allowed, allowed], axis=0)


def heads_of(y, slot, qkv, halo, rows):
    lanes = qkv.shape[-1]

    def at(a):
        return pl.ds(pl.multiple_of((a ^ y) * rows, rows), rows)

    before = spread(lanes, 2, (1 - slot) * (lanes // 2))
    here = spread(lanes, 4, 0)
    local = [dot(qkv[0, at(a), :], here).astype(BF) for a in range(2)]
    key_value = [dot(halo[at(a), :], before).astype(BF) for a in range(2)]
    key_value += [part[:, 256:] for part in local]
    query = [jnp.concatenate([part[:, :128], part[:, 128:256]], axis=0) for part in local]
    return at, query, key_value


def padded_out(w_out):
    rows = w_out.shape[1]
    return dot(pack(rows, 2, 0), w_out[0]).astype(BF)


def attend_kernel(y_ref, qkv, halo, seg_query, seg_key, w_out, partial, context, logsum, total):
    slot = pl.program_id(1)
    rows = qkv.shape[1] // 2
    at, query, key_value = heads_of(y_ref[0], slot, qkv, halo, rows)
    w = padded_out(w_out)
    for a in range(2):
        kv = jnp.concatenate(key_value[a : a + 3], axis=0)
        scores = dot_nt(query[a], kv[:, :128]) * (1.0 / math.sqrt(HEAD))
        scores = jnp.where(visible(seg_query, seg_key, a, rows), scores, -1e30)
        peak = jnp.max(scores, axis=-1, keepdims=True)
        exponent = jnp.exp(scores - peak)
        row_total = jnp.sum(exponent, axis=-1, keepdims=True)
        probs = (exponent * (1.0 / row_total)).astype(BF)
        logsum[0, 0, a] = peak + jnp.log(row_total)
        seen = dot(probs, kv[:, 128:]).astype(BF)
        seen = jnp.concatenate([seen[:rows], seen[rows:]], axis=1)
        context[0, at(a), :] = seen
        product = dot(seen, w)

        @pl.when(slot == 0)
        def _():
            total[at(a), :] = product

        @pl.when(slot == 1)
        def _():
            partial[at(a), :] = (total[at(a), :] + product).astype(BF)


def attend(y, qkv, halo, seg_query, seg_key, w_out):
    slots, tokens, lanes = qkv.shape
    groups, reach = 2, tokens // 2
    rows, width = reach // 2, w_out.shape[-1]
    return call(
        attend_kernel,
        [
            shaped((tokens, width), BF),
            shaped((slots, tokens, 256), BF),
            shaped((groups, slots, 2, reach, 1), F32),
        ],
        flops=10 * 10**9,
        moved=14 * 10**6,
        grid_spec=pltpu.PrefetchScalarGridSpec(
            num_scalar_prefetch=1,
            grid=(groups, slots),
            in_specs=[
                pl.BlockSpec((1, reach, lanes), lambda g, s, y: (s, g, 0)),
                pl.BlockSpec((reach, lanes), lambda g, s, y: (g, 0)),
                pl.BlockSpec((1, 2, rows, 1), lambda g, s, y: (g, 0, 0, 0)),
                pl.BlockSpec((1, 4, 1, rows), lambda g, s, y: (g, 0, 0, 0)),
                pl.BlockSpec((1,) + w_out.shape[1:], lambda g, s, y: (s, 0, 0)),
            ],
            out_specs=[
                pl.BlockSpec((reach, width), lambda g, s, y: (g, 0)),
                pl.BlockSpec((1, reach, 256), lambda g, s, y: (s, g, 0)),
                pl.BlockSpec((1, 1, 2, reach, 1), lambda g, s, y: (g, s, 0, 0, 0)),
            ],
            scratch_shapes=[pltpu.VMEM((reach, width), F32)],
        ),
    )(y, qkv, halo, seg_query, seg_key, w_out)


def load_blocks(parts, whole, sems):
    copies, at = [], 0
    for i, part in enumerate(parts):
        copies.append(
            pltpu.make_async_copy(part, whole.at[pl.ds(at, part.shape[0])], sems.at[i])
        )
        at += part.shape[0]
    for copy in copies:
        copy.start()
    return copies


def mlp_kernel(*refs):
    n_parts, d_parts, weights = refs[:5], refs[5:10], refs[10]
    before, out_before = refs[11:13] if len(refs) == 24 else (None, None)
    hidden, grad_gu, grad_in, out, normed, upstream, gu, down, n_sems, d_sems, w_sems = refs[-11:]
    b = pl.program_id(0)
    wide, width = gu.shape[1], down.shape[1]
    n_z = weights.shape[0]
    ff_part = down.shape[0] // n_z
    step = width // n_z
    half = ff_part * (width - wide) // wide

    def weight_copies():
        copies = [
            pltpu.make_async_copy(
                weights.at[z, pl.ds(0, step)], gu.at[pl.ds(z * step, step)], w_sems.at[0, z]
            )
            for z in range(n_z)
        ]
        for z in range(n_z):
            copies.append(
                pltpu.make_async_copy(
                    weights.at[z, pl.ds(step, ff_part)],
                    down.at[pl.ds(z * ff_part, ff_part), pl.ds(0, wide)],
                    w_sems.at[1, z],
                )
            )
            for i in range(2):
                copies.append(
                    pltpu.make_async_copy(
                        weights.at[z, pl.ds(step + ff_part, half), pl.ds(i * wide // 2, wide // 2)],
                        down.at[pl.ds(z * ff_part + i * half, half), pl.ds(wide, width - wide)],
                        w_sems.at[2 + i, z],
                    )
                )
        return copies

    @pl.when(b == 0)
    def _():
        copies = load_blocks(n_parts, normed, n_sems)
        for copy in weight_copies():
            copy.start()
            copies.append(copy)
        copies += load_blocks(d_parts, upstream, d_sems)
        for copy in copies:
            copy.wait()

    rows = hidden.shape[0]
    ff = wide // 2
    at = pl.ds(pl.multiple_of(b * rows, rows), rows)
    n, dy = normed[at, :], upstream[at, :]
    gate = dot(n, gu[:, :ff])
    up = dot(n, gu[:, ff:])
    dh = dot_nt(dy, down[...])
    sigmoid = jax.nn.sigmoid(gate)
    silu = gate * sigmoid
    low = (silu * up).astype(BF)
    hidden[...] = low
    d_gate = (dh * up * sigmoid * (1.0 + gate * (1.0 - sigmoid))).astype(BF)
    d_up = (dh * silu).astype(BF)
    grad_gu[:, :ff] = d_gate
    grad_gu[:, ff:] = d_up
    total = dot_nt(d_gate, gu[:, :ff]) + dot_nt(d_up, gu[:, ff:])
    if before is not None:
        total = total + before[...].astype(F32)
    grad_in[...] = total.astype(grad_in.dtype)
    total = dot(low, down[...])
    if out_before is not None:
        total = total + out_before[...].astype(F32)
    out[...] = total.astype(out.dtype)


def feed_forward(normed, upstream, weights, before=()):
    rows, width = normed[0].shape
    n_z, _, wide = weights.shape
    tokens = 4 * rows
    anywhere = pl.BlockSpec(memory_space=pl.ANY)
    block = pl.BlockSpec((rows, width), lambda b: (b, 0))
    return call(
        mlp_kernel,
        [
            shaped((tokens, wide // 2), BF),
            shaped((tokens, wide), BF),
        ]
        + [shaped((tokens, width), BF if before else F32)] * 2,
        flops=6 * tokens * width * wide,
        moved=20 * 10**6,
        grid=(4,),
        in_specs=[anywhere] * 11 + [block] * len(before),
        out_specs=[
            pl.BlockSpec((rows, wide // 2), lambda b: (b, 0)),
            pl.BlockSpec((rows, wide), lambda b: (b, 0)),
            block,
            block,
        ],
        scratch_shapes=[
            pltpu.VMEM((tokens, width), BF),
            pltpu.VMEM((tokens, width), BF),
            pltpu.VMEM((width, wide), BF),
            pltpu.VMEM((wide // 2, width), BF),
            pltpu.SemaphoreType.DMA((5,)),
            pltpu.SemaphoreType.DMA((5,)),
            pltpu.SemaphoreType.DMA((4, n_z)),
        ],
    )(*normed, *upstream, weights, *before)


def turn_back(values, cosine, sine):
    lane = iota(values.shape, 1)
    across = values * sine
    moved = jnp.where(
        lane < HEAD // 2,
        pltpu.roll(across, 128 - HEAD // 2, 1),
        jnp.where(lane < HEAD, -pltpu.roll(across, HEAD // 2, 1), 0.0),
    )
    return values * cosine + moved


def attend_back_kernel(
    y_ref, qkv, halo, seg_query, seg_key, w_out, context, logsum, cosine, sine,
    d0, d1, d2, d3, d4, grad_query, grad_kv, grad_halo, grad_out, up, kv_total, out_total, sems
):
    group, slot = pl.program_id(0), pl.program_id(1)
    reach = qkv.shape[1]
    rows = reach // 2
    factor = 1.0 / math.sqrt(HEAD)

    @pl.when((group == 0) & (slot == 0))
    def _():
        for copy in load_blocks((d0, d1, d2, d3, d4), up, sems):
            copy.wait()

    at, query, key_value = heads_of(y_ref[0], slot, qkv, halo, rows)
    w = padded_out(w_out)
    kv_total[...] = jnp.zeros_like(kv_total)
    out_part = None
    for a in range(2):
        begin = pl.multiple_of(group * reach + (a ^ y_ref[0]) * rows, rows)
        dy = up[pl.ds(begin, rows), :]
        d_context = dot_nt(dy, w).astype(BF)
        part = dot_tn(context[0, at(a), :], dy)
        out_part = part if out_part is None else out_part + part
        d_seen = jnp.concatenate([d_context[:, :128], d_context[:, 128:]], axis=0)
        kv = jnp.concatenate(key_value[a : a + 3], axis=0)
        key, value = kv[:, :128], kv[:, 128:]
        scores = dot_nt(query[a], key) * factor
        probs = jnp.exp(
            jnp.where(visible(seg_query, seg_key, a, rows), scores - logsum[0, 0, a], -1e30)
        )
        d_probs = dot_nt(d_seen, value)
        delta = jnp.sum(probs * d_probs, axis=-1, keepdims=True)
        d_scores = (probs * (d_probs - delta)).astype(BF)
        d_query = dot(d_scores, key) * factor
        cos_a, sin_a = cosine[at(a), :], sine[at(a), :]
        turned = jnp.concatenate(
            [turn_back(d_query[:rows], cos_a, sin_a), turn_back(d_query[rows:], cos_a, sin_a)],
            axis=1,
        ).astype(BF)
        grad_query[0, at(a), :] = dot(turned, pack(qkv.shape[-1], 2, 0)).astype(BF)
        seen = slice(a * rows, (a + 3) * rows)
        kv_total[seen, :128] += dot_tn(d_scores, query[a]) * factor
        kv_total[seen, 128:] += dot_tn(probs.astype(BF), d_seen)
    back = pack(qkv.shape[-1], 2, (1 - slot) * (qkv.shape[-1] // 2))
    for a in range(2):
        grad_kv[0, at(a), :] = kv_total[(a + 2) * rows : (a + 3) * rows, :]
        placed = dot(kv_total[a * rows : (a + 1) * rows, :].astype(BF), back).astype(BF)

        @pl.when(slot == 0)
        def _():
            grad_halo[at(a), :] = placed

        @pl.when(slot == 1)
        def _():
            grad_halo[at(a), :] += placed

    @pl.when(group == 0)
    def _():
        out_total[slot] = out_part

    @pl.when(group == 1)
    def _():
        whole = (out_total[slot] + out_part).astype(BF)
        grad_out[slot] = dot(spread(w_out.shape[1], 2, 0), whole).astype(BF)


def attend_back(y, qkv, halo, seg_query, seg_key, w_out, context, logsum, cosine, sine, upstream):
    slots, tokens, lanes = qkv.shape
    groups, reach = 2, tokens // 2
    rows, width = reach // 2, w_out.shape[-1]
    return call(
        attend_back_kernel,
        [
            shaped((slots, tokens, lanes), BF),
            shaped((slots, tokens, 256), F32),
            shaped((tokens, lanes), BF),
            shaped(w_out.shape, BF),
        ],
        flops=24 * 10**9,
        moved=20 * 10**6,
        grid_spec=pltpu.PrefetchScalarGridSpec(
            num_scalar_prefetch=1,
            grid=(groups, slots),
            in_specs=[
                pl.BlockSpec((1, reach, lanes), lambda g, s, y: (s, g, 0)),
                pl.BlockSpec((reach, lanes), lambda g, s, y: (g, 0)),
                pl.BlockSpec((1, 2, rows, 1), lambda g, s, y: (g, 0, 0, 0)),
                pl.BlockSpec((1, 4, 1, rows), lambda g, s, y: (g, 0, 0, 0)),
                pl.BlockSpec((1,) + w_out.shape[1:], lambda g, s, y: (s, 0, 0)),
                pl.BlockSpec((1, reach, 256), lambda g, s, y: (s, g, 0)),
                pl.BlockSpec((1, 1, 2, reach, 1), lambda g, s, y: (g, s, 0, 0, 0)),
                pl.BlockSpec((reach, 128), lambda g, s, y: (g, 0)),
                pl.BlockSpec((reach, 128), lambda g, s, y: (g, 0)),
            ]
            + [pl.BlockSpec(memory_space=pl.ANY)] * 5,
            out_specs=[
                pl.BlockSpec((1, reach, lanes), lambda g, s, y: (s, g, 0)),
                pl.BlockSpec((1, reach, 256), lambda g, s, y: (s, g, 0)),
                pl.BlockSpec((reach, lanes), lambda g, s, y: (g, 0)),
                pl.BlockSpec(w_out.shape, lambda g, s, y: (0, 0, 0)),
            ],
            scratch_shapes=[
                pltpu.VMEM((tokens, width), BF),
                pltpu.VMEM((2 * reach, 256), F32),
                pltpu.VMEM((slots, 256, width), F32),
                pltpu.SemaphoreType.DMA((5,)),
            ],
        ),
    )(y, qkv, halo, seg_query, seg_key, w_out, context, logsum, cosine, sine, *upstream)


def qkv_back_kernel(grad_query, grad_kv, grad_halo, cosine, sine, w_own, w_core, grad_qkv, grad_in):
    lanes = grad_halo.shape[-1]
    total = None
    place = pack(lanes, 2, lanes // 2)
    for slot, w in enumerate((w_own, w_core)):
        kv = grad_kv[slot] + dot(grad_halo[...], spread(lanes, 2, (1 - slot) * (lanes // 2)))
        key = turn_back(kv[:, :128], cosine[...], sine[...])
        kv = jnp.concatenate([key, kv[:, 128:]], axis=1).astype(BF)
        both = grad_query[slot] + dot(kv, place).astype(BF)
        grad_qkv[slot] = both
        part = dot_nt(both, w[...])
        total = part if total is None else total + part
    grad_in[...] = total.astype(BF)


def qkv_back(grad_query, grad_kv, grad_halo, cosine, sine, w_own, w_core):
    slots, tokens, lanes = grad_query.shape
    width, rows = w_own.shape[0], tokens // 4
    return call(
        qkv_back_kernel,
        [shaped((slots, tokens, lanes), BF), shaped((tokens, width), BF)],
        flops=2 * slots * tokens * width * lanes,
        moved=12 * 10**6,
        grid=(4,),
        in_specs=[
            pl.BlockSpec((slots, rows, lanes), lambda b: (0, b, 0)),
            pl.BlockSpec((slots, rows, 256), lambda b: (0, b, 0)),
            pl.BlockSpec((rows, lanes), lambda b: (b, 0)),
            pl.BlockSpec((rows, 128), lambda b: (b, 0)),
            pl.BlockSpec((rows, 128), lambda b: (b, 0)),
            pl.BlockSpec(w_own.shape, lambda b: (0, 0)),
            pl.BlockSpec(w_core.shape, lambda b: (0, 0)),
        ],
        out_specs=[
            pl.BlockSpec((slots, rows, lanes), lambda b: (0, b, 0)),
            pl.BlockSpec((rows, width), lambda b: (b, 0)),
        ],
    )(grad_query, grad_kv, grad_halo, cosine, sine, w_own, w_core)


def lay_out_kernel(d_ref, *refs):
    b0, b1, b2, b3, r0, r1, r2, r3, w_gate, w_up, gain, out_gate, out_up, out_down, grad_gain = refs
    wide, width = b0.shape[2], out_down.shape[1]
    ff = wide // 2
    count = r0.shape[1] * wide // width
    half = count // 2

    @pl.when(pl.program_id(0) == 0)
    def _():
        for k, part in enumerate((r0, r1, r2, r3)):
            at = pl.multiple_of((d_ref[0] ^ k) * count, count)
            out_down[pl.ds(at, count), :wide] = part[0, :count, :].astype(F32)
            for i in range(2):
                to = pl.ds(pl.multiple_of(at + i * half, half), half)
                out_down[to, wide:] = part[0, count:, i * ff : (i + 1) * ff].astype(F32)

    for k, block in enumerate((b0, b1, b2, b3)):
        for y in range(2):
            for z in range(ff // 128):
                to = pl.multiple_of(((2 * z + y) * 4 + (d_ref[0] ^ k)) * 128, 128)
                out_gate[:, pl.ds(to, 128)] = block[y, :, z * 128 : (z + 1) * 128].astype(F32)
                out_up[:, pl.ds(to, 128)] = block[y, :, ff + z * 128 : ff + (z + 1) * 128].astype(F32)
    weighted = w_gate[...].astype(F32) * out_gate[...] + w_up[...].astype(F32) * out_up[...]
    grad_gain[...] = jnp.sum(weighted, axis=-1, keepdims=True) / gain[...]


def lay_out(d, blocks, w_gate, w_up, gain, width):
    shard, ff = w_gate.shape
    rows = 64
    blocks = [block.reshape(-1, shard, block.shape[1]) for block in blocks]
    part = pl.BlockSpec((2, rows, blocks[0].shape[2]), lambda i, d: (0, i, 0))
    whole = pl.BlockSpec((rows, ff), lambda i, d: (i, 0))
    column = pl.BlockSpec((rows, 1), lambda i, d: (i, 0))
    last = pl.BlockSpec((1, shard, blocks[0].shape[2]), lambda i, d: (2, 0, 0))
    down_shape = (4 * shard * blocks[0].shape[2] // width, width)
    return call(
        lay_out_kernel,
        [shaped((shard, ff), F32)] * 2 + [shaped(down_shape, F32), shaped((shard, 1), F32)],
        flops=6 * shard * ff,
        moved=16 * shard * ff,
        grid_spec=pltpu.PrefetchScalarGridSpec(
            num_scalar_prefetch=1,
            grid=(shard // rows,),
            in_specs=[part] * 4 + [last] * 4 + [whole, whole, column],
            out_specs=[whole, whole, pl.BlockSpec(down_shape, lambda i, d: (0, 0)), column],
        ),
    )(d, *blocks, *blocks, w_gate, w_up, gain)


def lay_out_heads_kernel(d_ref, *refs):
    blocks, (w_query, w_key, w_value, gain) = refs[:4], refs[4:8]
    out_query, out_key, out_value, out_out, grad_gain, ordered = refs[8:]
    shard, lanes = w_query.shape[0], blocks[0].shape[1]
    count = out_out.shape[0] // 4
    for k, block in enumerate(blocks):
        to = d_ref[0] ^ k
        ordered[to] = block[: 2 * shard, :]
        at = pl.ds(pl.multiple_of(to * count, count), count)
        for i in range(4):
            out_out[at, i * lanes : (i + 1) * lanes] = block[
                2 * shard + i * count : 2 * shard + (i + 1) * count, :
            ].astype(F32)
    row, column = iota((lanes, lanes), 0), iota((lanes, lanes), 1)

    def place(begin, count, to):
        hit = (column - to == row - begin) & (row >= begin) & (row < begin + count)
        return jnp.where(hit, 1.0, 0.0).astype(BF)

    def block_of(t):
        return ordered[t // 2, (t % 2) * shard : (t % 2 + 1) * shard, :]

    total = None
    for begin, count, out, w in (
        (0, 2 * HEAD, out_query, w_query),
        (2 * HEAD, HEAD, out_key, w_key),
        (3 * HEAD, HEAD, out_value, w_value),
    ):
        heads = lanes // count
        places = [place(begin, count, i * count) for i in range(heads)]
        for j in range(KV_HEADS // heads):
            piece = None
            for i in range(heads):
                part = dot(block_of(j * heads + i), places[i])
                piece = part if piece is None else piece + part
            at = slice(j * lanes, (j + 1) * lanes)
            out[:, at] = piece
            part = jnp.sum(w[:, at].astype(F32) * piece, axis=-1, keepdims=True)
            total = part if total is None else total + part
    grad_gain[...] = total / gain[...]


def lay_out_heads(d, blocks, w_query, w_key, w_value, gain, out_shape):
    shard = w_query.shape[0]
    vmem = pl.BlockSpec(memory_space=pltpu.VMEM)
    return call(
        lay_out_heads_kernel,
        [
            shaped(w_query.shape, F32),
            shaped(w_key.shape, F32),
            shaped(w_value.shape, F32),
            shaped(out_shape, F32),
            shaped((shard, 1), F32),
        ],
        flops=4 * 10**9,
        moved=8 * 10**6,
        in_specs=[pl.BlockSpec(memory_space=pltpu.SMEM)] + [vmem] * 8,
        out_specs=[vmem] * 5,
        scratch_shapes=[pltpu.VMEM((4, 2 * shard, blocks[0].shape[1]), BF)],
    )(d, *blocks, w_query, w_key, w_value, gain)


def layout_rows(lengths, index):
    ends = jnp.cumsum(lengths, axis=1)
    before = index[None, :, None] >= ends[:, None, :]
    segment = jnp.sum(before.astype(jnp.int32), axis=2)
    offset = jnp.sum(jnp.where(before, lengths[:, None, :], 0), axis=2)
    segment = jnp.where(segment < lengths.shape[1], segment, -1)
    segment = jnp.where(index[None, :] < 0, -3, segment)
    return (segment, index[None, :] - offset)


def on_device(
    tokens,
    lengths,
    cotangent,
    gain_attn,
    w_query,
    w_key,
    w_value,
    w_out,
    gain_mlp,
    w_gate,
    w_up,
    w_down,
):
    n_dp, n_seq = lax.axis_size("dp"), lax.axis_size("seq")
    d, me = lax.axis_index("dp"), lax.axis_index("seq")
    y, n_z = me % 2, n_seq // 2
    rows, width = tokens.shape
    reach = 2 * rows
    assert WINDOW <= reach and KV_HEADS == 2 * n_dp
    groups = HEADS // KV_HEADS
    q_w, k_w = groups * HEAD, HEAD
    shard = w_query.shape[0]
    ff_shard = w_down.shape[0]
    ff_part = ff_shard // n_dp

    def head_columns(j):
        t = 2 * d + j
        gains = jnp.zeros((16, q_w + 2 * k_w), BF)
        gains = gains.at[0, :shard].set(gain_attn).at[1, :shard].set(gain_mlp)
        columns = jnp.concatenate(
            [
                lax.dynamic_slice_in_dim(w_query, t * q_w, q_w, 1),
                lax.dynamic_slice_in_dim(w_key, t * k_w, k_w, 1),
                lax.dynamic_slice_in_dim(w_value, t * k_w, k_w, 1),
            ],
            axis=1,
        )
        return jnp.concatenate([columns, gains], axis=0)

    def ff_columns(j):
        parts = [
            lax.dynamic_slice_in_dim(w, ((2 * z + j) * n_dp + d) * ff_part, ff_part, 1)
            for w in (w_gate, w_up)
            for z in range(n_z)
        ]
        return jnp.concatenate(parts, axis=1)

    lens = jnp.concatenate([lengths, send(lengths, across_x)], axis=0)

    first_row = (me // 2) * reach
    steps = jnp.arange(reach, dtype=jnp.int32)
    order = jnp.arange(2, dtype=jnp.int32)[:, None] ^ y
    _, position = layout_rows(lens, first_row + (order * rows + steps[None, :rows]).reshape(-1))
    cosine, sine = rope_tables(position.reshape(-1))
    key_index = first_row - reach + jnp.arange(2 * reach, dtype=jnp.int32)
    segment, _ = layout_rows(lens, key_index)
    segment = jnp.where(segment == -1, -8 - key_index[None, :], segment)
    seg_key = segment.reshape(2, 4, 1, rows)
    seg_query = segment[:, reach:].reshape(2, 2, rows, 1)
    y_arg = jnp.reshape(y, (1,)).astype(jnp.int32)

    tokens_all = gather_plane(tokens, cosine, sine)
    lanes = q_w + 2 * k_w
    square = n_seq == 2 * n_dp
    part_qkv = pair_y(head_columns(y), send(head_columns(1 - y), across_y)).reshape(-1, lanes)
    if square:
        out_rows = shard // n_dp
        part_out = send(lax.dynamic_slice_in_dim(w_out, d * out_rows, out_rows, 0), turned)
    got_attn = lax.optimization_barrier((gather_z(part_qkv), *tokens_all))[0]
    part_mlp = jnp.concatenate(
        [
            pair_y(ff_columns(y), send(ff_columns(1 - y), across_y)).reshape(2 * shard, -1),
            fold(lax.dynamic_slice_in_dim(w_down, d * ff_part, ff_part, 0), 2 * n_z * ff_part),
        ],
        axis=0,
    )
    got_qkv = got_attn.reshape(n_z, 2, shard + 16, lanes)
    full_qkv = with_core(got_qkv[:, :, :shard].reshape(width, -1))
    if square:
        own_out = gather_z(after(part_out, got_attn)).reshape(shard, width)
    else:
        own_out = lax.all_gather(w_out, "seq", axis=0, tiled=True)
        own_out = lax.dynamic_slice_in_dim(own_out, (2 * d + y) * q_w, q_w, 0)
    full_out = jnp.stack(with_core(own_out))
    full_gain_attn = got_qkv[:, :, shard, :shard].reshape(1, -1).astype(F32)
    full_gain_mlp = got_qkv[:, :, shard + 1, :shard].reshape(1, -1).astype(F32)

    normed, qkv, halo = call(
        qkv_kernel,
        [
            shaped((4 * rows, width), BF),
            shaped((2, 4 * rows, lanes), BF),
            shaped((4 * rows, lanes), BF),
        ],
        flops=16 * rows * width * lanes,
        moved=12 * 10**6,
    )(*tokens_all, full_gain_attn, cosine, sine, *full_qkv)
    halo_in = send(after(halo, own_out), lambda d, s: (d, s + 2))
    got_mlp = line_gather_z(after(part_mlp, halo_in))
    cotangent_in = after(cotangent, *tokens_all)
    upstream_all = gather_plane(cotangent_in)
    halo_in = after(halo_in, *upstream_all)
    partial, context, logsum = attend(y_arg, qkv, halo_in, seg_query, seg_key, full_out)
    middle = tokens.astype(F32) + scatter_plane(partial)


    inverse_mlp = lax.rsqrt(jnp.mean(middle * middle, axis=-1, keepdims=True) + EPS)
    normed_mlp_own = (middle * inverse_mlp * full_gain_mlp).astype(BF)
    normed_mlp_all = gather_plane(normed_mlp_own)
    got_mlp = lax.optimization_barrier((got_mlp, *normed_mlp_all))[0]
    mlp_core = send(got_mlp, across_core)
    hidden_own, grad_gu_own, *before = feed_forward(normed_mlp_all, upstream_all, got_mlp)
    hidden_core, grad_gu_core, grad_in, down = feed_forward(
        normed_mlp_all, upstream_all, mlp_core, before
    )
    hidden_own, grad_gu_own = lax.optimization_barrier((hidden_own, grad_gu_own, grad_in))[:2]
    ff = n_z * ff_part
    upstream_low = jnp.concatenate(upstream_all, axis=0)
    normed_mlp = jnp.concatenate(normed_mlp_all, axis=0)

    def mlp_grads(hidden, grad_gu):
        for_down = dot_tn(hidden, upstream_low).astype(BF)
        for_down = [fold(for_down[z * ff_part : (z + 1) * ff_part], 2 * ff) for z in range(n_z)]
        for_gu = dot_tn(normed_mlp, grad_gu).astype(BF).reshape(n_z, 2 * shard, 2 * ff)
        return jnp.concatenate([for_gu, jnp.stack(for_down)], axis=1)

    grads_core = mlp_grads(hidden_core, grad_gu_core)
    grads_own = mlp_grads(hidden_own, grad_gu_own)
    grad_mlp = sum_core(grads_own, grads_core)
    grad_normed_mlp = scatter_plane(grad_in, grads_own, grads_core)
    upstream = cotangent.astype(F32)
    scaled = grad_normed_mlp * full_gain_mlp
    grad_middle = (
        upstream
        + inverse_mlp * scaled
        - middle * inverse_mlp**3 * jnp.mean(scaled * middle, axis=-1, keepdims=True)
    )
    grad_attended_all = gather_plane(grad_middle.astype(BF))

    total_mlp = line_scatter_z(grad_mlp).astype(BF)
    attended_in = lax.optimization_barrier((*grad_attended_all, grad_mlp))[:5]

    def swap_rows(total):
        mine = lax.dynamic_slice_in_dim(total, y * shard, shard, 0)
        other = lax.dynamic_slice_in_dim(total, (1 - y) * shard, shard, 0)
        return pair_y(mine, send(other, across_y)).reshape(2 * shard, -1)

    mlp_blocks = gather_dp(
        jnp.concatenate([swap_rows(total_mlp[: 2 * shard]), total_mlp[2 * shard :]], axis=0)
    )
    if ff_part % 128 == 0:
        d_arg = jnp.reshape(d, (1,)).astype(jnp.int32)
        gain_column = gain_mlp.astype(F32).reshape(-1, 1)
        out_gate, out_up, out_down, grad_gain_mlp = lay_out(
            d_arg, mlp_blocks, w_gate, w_up, gain_column, width
        )
    else:
        out_down = jnp.concatenate(
            [unfold(block[2 * shard :], width) for block in order_dp(mlp_blocks)], axis=0
        ).astype(F32)
        all_gu = jnp.stack([block[: 2 * shard] for block in order_dp(mlp_blocks)])
        all_gu = all_gu.reshape(n_dp, 2, shard, 2, n_z, ff_part)
        all_gu = all_gu.transpose(3, 2, 4, 1, 0, 5).reshape(2, shard, -1).astype(F32)
        out_gate, out_up = all_gu[0], all_gu[1]
        grad_gain_mlp = jnp.sum(
            w_gate.astype(F32) * out_gate + w_up.astype(F32) * out_up, axis=1
        ) / gain_mlp.astype(F32)

    grad_query, grad_kv, grad_halo, grad_out = attend_back(
        y_arg, qkv, halo_in, seg_query, seg_key, full_out, context, logsum,
        cosine, sine, attended_in,
    )
    grad_halo_in = send(after(grad_halo, total_mlp), lambda d, s: (d, s - 2))
    grad_qkv, grad_in = qkv_back(
        grad_query, grad_kv, grad_halo_in, cosine, sine, *full_qkv
    )
    def attn_grads(slot):
        for_qkv = dot_tn(normed, grad_qkv[slot]).astype(BF).reshape(n_z, 2 * shard, -1)
        if not square:
            return for_qkv
        for_out = [
            fold(grad_out[slot, z * out_rows : (z + 1) * out_rows], lanes) for z in range(n_z)
        ]
        return jnp.concatenate([for_qkv, jnp.stack(for_out)], axis=1)

    total_attn = scatter_z(sum_core(attn_grads(0), attn_grads(1))).astype(BF)
    mine_attn = swap_rows(total_attn[: 2 * shard])
    if square:
        mine_attn = jnp.concatenate([mine_attn, send(total_attn[2 * shard :], turned)], axis=0)
    attn_blocks = gather_dp(mine_attn)
    if square:
        out_query, out_key, out_value, out_out, grad_gain_attn = lay_out_heads(
            jnp.reshape(d, (1,)).astype(jnp.int32),
            attn_blocks,
            w_query,
            w_key,
            w_value,
            gain_attn.astype(F32).reshape(-1, 1),
            w_out.shape,
        )
    else:
        attn_blocks = order_dp(attn_blocks)
        grad_out = sum_core(grad_out[0], grad_out[1]).astype(F32)
        out_out = jnp.zeros((2 * n_dp * q_w, width), F32)
        out_out = lax.dynamic_update_slice_in_dim(out_out, grad_out, (2 * d + y) * q_w, 0)
        out_out = lax.psum_scatter(out_out, "seq", scatter_dimension=0, tiled=True)
        out_out = lax.psum(out_out.astype(BF), "dp").astype(F32)
        all_qkv = jnp.stack([block[: 2 * shard] for block in attn_blocks]).astype(F32)
        out_qkv = all_qkv.reshape(2 * n_dp, shard, lanes).transpose(1, 0, 2)
        out_query = out_qkv[..., :q_w].reshape(shard, -1)
        out_key = out_qkv[..., q_w : q_w + k_w].reshape(shard, -1)
        out_value = out_qkv[..., q_w + k_w :].reshape(shard, -1)
        grad_gain_attn = (
            jnp.sum(w_query.astype(F32) * out_query, axis=1)
            + jnp.sum(w_key.astype(F32) * out_key, axis=1)
            + jnp.sum(w_value.astype(F32) * out_value, axis=1)
        ) / gain_attn.astype(F32)

    own = scatter_plane(grad_in)
    wide = tokens.astype(F32)
    own_inverse = lax.rsqrt(jnp.mean(wide * wide, axis=-1, keepdims=True) + EPS)
    scaled = own * full_gain_attn
    grad_tokens = (
        grad_middle
        + own_inverse * scaled
        - wide * own_inverse**3 * jnp.mean(scaled * wide, axis=-1, keepdims=True)
    )
    output = (middle + scatter_plane(after(down, *grad_attended_all))).astype(BF)
    return (
        output,
        grad_tokens,
        grad_gain_attn.reshape(-1),
        out_query,
        out_key,
        out_value,
        out_out,
        grad_gain_mlp.reshape(-1),
        out_gate,
        out_up,
        out_down,
    )


def solution(mesh):
    return jax.shard_map(
        on_device,
        mesh=mesh,
        in_specs=(
            P(("dp", "seq"), None),
            P("dp", None),
            P(("dp", "seq"), None),
            P("seq"),
            P("seq", None),
            P("seq", None),
            P("seq", None),
            P("seq", None),
            P("seq"),
            P("seq", None),
            P("seq", None),
            P("seq", None),
        ),
        out_specs=(
            P(("dp", "seq"), None),
            P(("dp", "seq"), None),
            P("seq"),
            P("seq", None),
            P("seq", None),
            P("seq", None),
            P("seq", None),
            P("seq"),
            P("seq", None),
            P("seq", None),
            P("seq", None),
        ),
        check_vma=False,
    )
```

```python
import functools
import math

import jax
import jax.numpy as jnp
from jax import lax
from jax.experimental import pallas as pl
from jax.experimental.pallas import tpu as pltpu
from jax.sharding import PartitionSpec as P

HEADS = 16
KV_HEADS = 8
HEAD = 96
WINDOW = 512


EPS = 1e-05
THETA = 100000.0
BOTH = ("dp", "seq")
BF = jnp.bfloat16
F32 = jnp.float32


def send(block, target):
    n_dp, n_seq = lax.axis_size("dp"), lax.axis_size("seq")
    route = []
    for d in range(n_dp):
        for s in range(n_seq):
            to = target(d, s)
            if to is not None and 0 <= to[1] < n_seq:
                route.append((d * n_seq + s, to[0] * n_seq + to[1]))
    return lax.ppermute(block, BOTH, route)


def after(value, *others):
    return lax.optimization_barrier((value,) + others)[0]


def across_core(d, s):
    return (d ^ 1, s)


def across_x(d, s):
    return (d ^ 2, s)


def across_y(d, s):
    return (d, s ^ 1)


def gather_plane(block, *meanwhile, for_y=None, came=None):
    half = block.shape[0] // 2
    from_x, from_y = came or (
        send(block, across_x),
        send(block if for_y is None else for_y, across_y),
    )
    if meanwhile:
        from_x, from_y = lax.optimization_barrier((from_x, from_y, *meanwhile))[:2]
    first = send(from_x[:half], across_y)
    second = send(from_y[half:], across_x)
    return [block, from_y, from_x, first, second]


def scatter_plane(near, far, *meanwhile, at_first=()):
    own, own_y = near
    far, far_a, far_b = far
    half = far_a.shape[0]
    first = send(far_a, across_y)
    second = send(far_b, across_x)
    if at_first:
        first, second = lax.optimization_barrier((first, second, *at_first))[:2]

    def plus(a, b):
        return (a.astype(F32) + b.astype(F32)).astype(BF)

    far = jnp.concatenate([plus(far[:half], first), far[half:]], axis=0)
    own_y = jnp.concatenate([own_y[:half], plus(own_y[half:], second)], axis=0)
    from_x, from_y = send(far, across_x), send(own_y, across_y)
    if meanwhile:
        from_x, from_y = lax.optimization_barrier((from_x, from_y, *meanwhile))[:2]
    return own.astype(F32) + from_x.astype(F32) + from_y.astype(F32)


def with_core(block):
    return [block, send(block, across_core)]


def sum_core(mine, other):
    return (mine.astype(F32) + send(other.astype(BF), across_core).astype(F32)).astype(BF)


def across_z(k):
    return lambda d, s: (d, s ^ (2 * k))


def along_z(blocks):
    n_seq = lax.axis_size("seq")
    lines = [list(range(y, n_seq, 2)) for y in range(2)]
    return lax.all_to_all(blocks, "seq", 0, 0, axis_index_groups=lines)


def gather_z(block):
    return along_z(jnp.broadcast_to(block[None], (lax.axis_size("seq") // 2,) + block.shape))


def scatter_z(blocks):
    return jnp.sum(along_z(blocks).astype(F32), axis=0)


def pair_y(mine, other):
    y = lax.axis_index("seq") % 2
    return jnp.stack([jnp.where(y == 0, mine, other), jnp.where(y == 0, other, mine)])


def turned(d, s):
    return (s // 2, 2 * d + s % 2)


def fold(rows, wide):
    count, columns = rows.shape
    whole = columns // wide
    parts = [rows[:, i * wide : (i + 1) * wide] for i in range(whole)]
    rest = rows[:, whole * wide :]
    if rest.shape[1]:
        times = wide // rest.shape[1]
        step = count // times
        parts.append(
            jnp.concatenate([rest[i * step : (i + 1) * step] for i in range(times)], axis=1)
        )
    return jnp.concatenate(parts, axis=0)


def unfold(folded, columns):
    total, wide = folded.shape
    count = total * wide // columns
    whole = columns // wide
    parts = [folded[i * count : (i + 1) * count] for i in range(whole)]
    if columns % wide:
        rest, narrow = folded[whole * count :], columns % wide
        parts.append(
            jnp.concatenate(
                [rest[:, i * narrow : (i + 1) * narrow] for i in range(wide // narrow)], axis=0
            )
        )
    return jnp.concatenate(parts, axis=1)


def gather_dp(block):
    core = send(block, across_core)
    far = send(block, across_x)
    return [block, core, far, send(far, across_core)]


def order_dp(blocks):
    d = lax.axis_index("dp")
    pairs = [
        (jnp.where(d % 2 == 0, a, b), jnp.where(d % 2 == 0, b, a))
        for a, b in (blocks[:2], blocks[2:])
    ]
    low, high = pairs
    return [jnp.where(d < 2, a, b) for a, b in zip(low, high)] + [
        jnp.where(d < 2, b, a) for a, b in zip(low, high)
    ]


def rope_tables(position):
    lane = jnp.arange(128, dtype=jnp.float32) % (HEAD // 2)
    angles = position.astype(jnp.float32)[..., None] * THETA ** (-2.0 * lane / HEAD)
    return jnp.cos(angles), jnp.sin(angles)


SCALE = 0.3
VMEM_BYTES = 60 * 1024 * 1024


def call(kernel, out_shape, flops, moved, **rest):
    return pl.pallas_call(
        kernel,
        out_shape=out_shape,
        compiler_params=pltpu.CompilerParams(vmem_limit_bytes=VMEM_BYTES),
        cost_estimate=pl.CostEstimate(flops=int(flops * SCALE), bytes_accessed=int(moved * SCALE), transcendentals=0),
        **rest,
    )


def shaped(shape, dtype):
    return jax.ShapeDtypeStruct(shape, dtype)


def iota(shape, axis):
    return lax.broadcasted_iota(jnp.int32, shape, axis)


def dot(a, b):
    return jnp.dot(a, b, preferred_element_type=F32)


def dot_nt(a, b):
    return lax.dot_general(a, b, (((1,), (1,)), ((), ())), preferred_element_type=F32)


def dot_tn(a, b):
    return lax.dot_general(a, b, (((0,), (0,)), ((), ())), preferred_element_type=F32)


def spread(packed, heads, base):
    row, column = iota((packed, heads * 128), 0), iota((packed, heads * 128), 1)
    lane = column % 128
    hit = (row == base + HEAD * (column // 128) + lane) & (lane < HEAD)
    return jnp.where(hit, 1.0, 0.0).astype(BF)


def pack(packed, heads, base):
    column, row = iota((heads * 128, packed), 0), iota((heads * 128, packed), 1)
    lane = column % 128
    hit = (row == base + HEAD * (column // 128) + lane) & (lane < HEAD)
    return jnp.where(hit, 1.0, 0.0).astype(BF)


def on_heads(table, heads, packed):
    row, column = iota((128, packed), 0), iota((128, packed), 1)
    place = jnp.where((row == column % HEAD) & (column < heads * HEAD), 1.0, 0.0).astype(BF)
    high = table.astype(BF)
    rest = table - high.astype(F32)
    middle = rest.astype(BF)
    low = (rest - middle.astype(F32)).astype(BF)
    return dot(high, place) + dot(middle, place) + dot(low, place)


def qkv_kernel(*refs):
    parts, refs = refs[:-8], refs[-8:]
    gain, cosine, sine, w_own, w_core, normed, qkv, halo = refs
    tokens, lanes = halo.shape
    x = jnp.concatenate([part[...] for part in parts], axis=0).astype(F32)
    inverse = lax.rsqrt(jnp.mean(x * x, axis=-1, keepdims=True) + EPS)
    low = (x * inverse * gain[...]).astype(BF)
    normed[...] = low
    lane = iota((tokens, lanes), 1)
    first = lane % HEAD < HEAD // 2
    cos_all = on_heads(cosine[...], 3, lanes) + jnp.where(lane >= 3 * HEAD, 1.0, 0.0)
    sin_all = on_heads(sine[...], 3, lanes)
    turned = []
    size = normed.shape[1] // w_own.shape[0]
    for w in (w_own, w_core):
        raw = sum(dot(low[:, z * size : (z + 1) * size], w[z, :size, :]) for z in range(w.shape[0]))
        half = jnp.where(
            first, -pltpu.roll(raw, lanes - HEAD // 2, 1), pltpu.roll(raw, HEAD // 2, 1)
        )
        turned.append(raw * cos_all + half * sin_all)
    qkv[0] = turned[0].astype(BF)
    qkv[1] = turned[1].astype(BF)
    halo[...] = jnp.where(
        lane < lanes // 2, pltpu.roll(turned[1], lanes // 2, 1), turned[0]
    ).astype(BF)


def project(group, parts, gain, cosine, sine, w_own, w_core):
    tokens = sum(part.shape[0] for part in parts)
    width, lanes = gain.shape[1], w_own.shape[2]

    def whole(array):
        return pl.BlockSpec(array.shape, lambda i: (0,) * array.ndim)

    table = pl.BlockSpec((tokens, 128), lambda i: (group, 0))
    outs = [shaped((tokens, width), BF), shaped((2, tokens, lanes), BF), shaped((tokens, lanes), BF)]
    return call(
        qkv_kernel,
        outs,
        flops=4 * tokens * width * lanes,
        moved=6 * 10**6,
        grid=(1,),
        in_specs=[whole(part) for part in parts] + [whole(gain), table, table, whole(w_own), whole(w_core)],
        out_specs=[whole(out) for out in outs],
    )(*parts, gain, cosine, sine, w_own, w_core)


def visible(seg_query, seg_key, a, rows):
    shape = (rows, 3 * rows)
    row, column = iota(shape, 0), iota(shape, 1)
    same = seg_query[0, a] == jnp.concatenate([seg_key[0, a + i] for i in range(3)], axis=1)
    allowed = (column > row) & (column <= row + 2 * rows) & same
    return jnp.concatenate([allowed, allowed], axis=0)


def heads_of(y, slot, qkv, halo, rows):
    lanes = qkv.shape[-1]

    def at(a):
        return pl.ds(pl.multiple_of((a ^ y) * rows, rows), rows)

    before = spread(lanes, 2, (1 - slot) * (lanes // 2))
    here = spread(lanes, 4, 0)
    local = [dot(qkv[0, at(a), :], here).astype(BF) for a in range(2)]
    key_value = [dot(halo[at(a), :], before).astype(BF) for a in range(2)]
    key_value += [part[:, 256:] for part in local]
    query = [jnp.concatenate([part[:, :128], part[:, 128:256]], axis=0) for part in local]
    return at, query, key_value


def padded_out(w_out):
    rows = w_out.shape[1]
    return dot(pack(rows, 2, 0), w_out[0]).astype(BF)


def attend_kernel(y_ref, qkv, halo, seg_query, seg_key, w_out, *refs):
    *partial, context, logsum, total = refs
    slot = pl.program_id(0)
    rows = qkv.shape[1] // 2
    at, query, key_value = heads_of(y_ref[0], slot, qkv, halo, rows)
    w = padded_out(w_out)
    for a in range(2):
        kv = jnp.concatenate(key_value[a : a + 3], axis=0)
        scores = dot_nt(query[a], kv[:, :128]) * (1.0 / math.sqrt(HEAD))
        scores = jnp.where(visible(seg_query, seg_key, a, rows), scores, -1e30)
        peak = jnp.max(scores, axis=-1, keepdims=True)
        exponent = jnp.exp(scores - peak)
        row_total = jnp.sum(exponent, axis=-1, keepdims=True)
        probs = (exponent * (1.0 / row_total)).astype(BF)
        logsum[0, a] = peak + jnp.log(row_total)
        seen = dot(probs, kv[:, 128:]).astype(BF)
        seen = jnp.concatenate([seen[:rows], seen[rows:]], axis=1)
        context[0, at(a), :] = seen
        product = dot(seen, w)

        @pl.when(slot == 0)
        def _():
            total[at(a), :] = product

        @pl.when(slot == 1)
        def _():
            total[at(a), :] += product

    @pl.when(slot == 1)
    def _():
        begin = 0
        for out in partial:
            out[...] = total[begin : begin + out.shape[0], :].astype(BF)
            begin += out.shape[0]


def attend(y, group, qkv, halo, seg_query, seg_key, w_out):
    slots, reach, lanes = qkv.shape
    rows, width = reach // 2, w_out.shape[-1]
    sizes = (rows, rows // 2, rows // 2) if group else (rows, rows)
    return call(
        attend_kernel,
        [shaped((size, width), BF) for size in sizes]
        + [
            shaped((slots, reach, 256), BF),
            shaped((slots, 2, reach, 1), F32),
        ],
        flops=5 * 10**9,
        moved=7 * 10**6,
        grid_spec=pltpu.PrefetchScalarGridSpec(
            num_scalar_prefetch=1,
            grid=(slots,),
            in_specs=[
                pl.BlockSpec((1, reach, lanes), lambda s, y: (s, 0, 0)),
                pl.BlockSpec((reach, lanes), lambda s, y: (0, 0)),
                pl.BlockSpec((1, 2, rows, 1), lambda s, y: (group, 0, 0, 0)),
                pl.BlockSpec((1, 4, 1, rows), lambda s, y: (group, 0, 0, 0)),
                pl.BlockSpec((1,) + w_out.shape[1:], lambda s, y: (s, 0, 0)),
            ],
            out_specs=[pl.BlockSpec((size, width), lambda s, y: (0, 0)) for size in sizes]
            + [
                pl.BlockSpec((1, reach, 256), lambda s, y: (s, 0, 0)),
                pl.BlockSpec((1, 2, reach, 1), lambda s, y: (s, 0, 0, 0)),
            ],
            scratch_shapes=[pltpu.VMEM((reach, width), F32)],
        ),
    )(y, qkv, halo, seg_query, seg_key, w_out)


def load_blocks(parts, whole, sems):
    copies, at = [], 0
    for i, part in enumerate(parts):
        copies.append(
            pltpu.make_async_copy(part, whole.at[pl.ds(at, part.shape[0])], sems.at[i])
        )
        at += part.shape[0]
    for copy in copies:
        copy.start()
    return copies


def weight_copies(me, weights, gu, down, sems):
    n_z, wide = len(weights), weights[0].shape[1]
    width = down.shape[1]
    step, ff_part = width // n_z, down.shape[0] // n_z
    half = ff_part * (width - wide) // wide
    first, second = [], []
    for r, block in enumerate(weights):
        z = me ^ r
        row = pl.multiple_of(z * ff_part, ff_part)
        if gu is not None:
            first.append(
                pltpu.make_async_copy(
                    block.at[pl.ds(0, step)],
                    gu.at[pl.ds(pl.multiple_of(z * step, step), step)],
                    sems.at[0, r],
                )
            )
        second.append(
            pltpu.make_async_copy(
                block.at[pl.ds(step, ff_part)],
                down.at[pl.ds(row, ff_part), pl.ds(0, wide)],
                sems.at[1, r],
            )
        )
        for i in range(2):
            second.append(
                pltpu.make_async_copy(
                    block.at[pl.ds(step + ff_part, half), pl.ds(i * wide // 2, wide // 2)],
                    down.at[pl.ds(row + i * half, half), pl.ds(wide, width - wide)],
                    sems.at[2 + i, r],
                )
            )
    return first + second


def mlp_kernel(n_z, z_ref, *refs):
    n_parts, d_parts, refs = refs[:5], refs[5:10], refs[10:]
    w_own, w_core, refs = refs[:n_z], refs[n_z : 2 * n_z], refs[2 * n_z :]
    hidden, grad_gu, *grad_in, normed_out, upstream_out = refs[:9]
    normed, upstream, gu, down, total, n_sems, d_sems, w_sems, out_sems = refs[9:]
    slot = pl.program_id(0)
    ff = gu.shape[2] // 2
    core_copies = weight_copies(z_ref[0], w_core, gu.at[1], down.at[1], w_sems.at[1])
    kept = [
        pltpu.make_async_copy(normed, normed_out, out_sems.at[0]),
        pltpu.make_async_copy(upstream, upstream_out, out_sems.at[1]),
    ]

    @pl.when(slot == 0)
    def _():
        copies = load_blocks(n_parts, normed, n_sems)
        copies += weight_copies(z_ref[0], w_own, gu.at[0], down.at[0], w_sems.at[0])
        for copy in copies[5:]:
            copy.start()
        copies += load_blocks(d_parts, upstream, d_sems)
        for copy in core_copies:
            copy.start()
        for copy in copies:
            copy.wait()
        for copy in kept:
            copy.start()

    @pl.when(slot == 1)
    def _():
        for copy in core_copies:
            copy.wait()

    n, dy = normed[...], upstream[...]
    gate = dot(n, gu[slot, :, :ff])
    up = dot(n, gu[slot, :, ff:])
    dh = dot_nt(dy, down[slot])
    sigmoid = jax.nn.sigmoid(gate)
    silu = gate * sigmoid
    hidden[0] = (silu * up).astype(BF)
    d_gate = (dh * up * sigmoid * (1.0 + gate * (1.0 - sigmoid))).astype(BF)
    d_up = (dh * silu).astype(BF)
    grad_gu[0, :, :ff] = d_gate
    grad_gu[0, :, ff:] = d_up
    part = dot_nt(d_gate, gu[slot, :, :ff]) + dot_nt(d_up, gu[slot, :, ff:])

    @pl.when(slot == 0)
    def _():
        total[...] = part

    @pl.when(slot == 1)
    def _():
        whole = (total[...] + part).astype(BF)
        begin = 0
        for out in grad_in:
            out[...] = whole[begin : begin + out.shape[0]]
            begin += out.shape[0]
        for copy in kept:
            copy.wait()


def feed_forward(z, normed, upstream, w_own, w_core):
    rows, width = normed[0].shape
    n_z, wide = len(w_own), w_own[0].shape[1]
    tokens, ff = 4 * rows, wide // 2
    anywhere = pl.BlockSpec(memory_space=pl.ANY)
    block = pl.BlockSpec((rows, width), lambda s, z: (0, 0))
    half = pl.BlockSpec((rows // 2, width), lambda s, z: (0, 0))
    return call(
        functools.partial(mlp_kernel, n_z),
        [
            shaped((2, tokens, ff), BF),
            shaped((2, tokens, wide), BF),
            shaped((rows, width), BF),
            shaped((rows, width), BF),
            shaped((rows, width), BF),
            shaped((rows // 2, width), BF),
            shaped((rows // 2, width), BF),
            shaped((tokens, width), BF),
            shaped((tokens, width), BF),
        ],
        flops=10 * tokens * width * wide,
        moved=25 * 10**6,
        grid_spec=pltpu.PrefetchScalarGridSpec(
            num_scalar_prefetch=1,
            grid=(2,),
            in_specs=[anywhere] * (10 + 2 * n_z),
            out_specs=[
                pl.BlockSpec((1, tokens, ff), lambda s, z: (s, 0, 0)),
                pl.BlockSpec((1, tokens, wide), lambda s, z: (s, 0, 0)),
                block,
                block,
                block,
                half,
                half,
                anywhere,
                anywhere,
            ],
            scratch_shapes=[
                pltpu.VMEM((tokens, width), BF),
                pltpu.VMEM((tokens, width), BF),
                pltpu.VMEM((2, width, wide), BF),
                pltpu.VMEM((2, ff, width), BF),
                pltpu.VMEM((tokens, width), F32),
                pltpu.SemaphoreType.DMA((5,)),
                pltpu.SemaphoreType.DMA((5,)),
                pltpu.SemaphoreType.DMA((2, 4, n_z)),
                pltpu.SemaphoreType.DMA((2,)),
            ],
        ),
    )(z, *normed, *upstream, *w_own, *w_core)


def down_kernel(n_z, z_ref, hidden, *refs):
    w_own, w_core, refs = refs[:n_z], refs[n_z : 2 * n_z], refs[2 * n_z :]
    *outs, down, total, sems = refs
    slot = pl.program_id(0)
    core_copies = weight_copies(z_ref[0], w_core, None, down.at[1], sems.at[1])

    @pl.when(slot == 0)
    def _():
        copies = weight_copies(z_ref[0], w_own, None, down.at[0], sems.at[0])
        for copy in copies + core_copies:
            copy.start()
        for copy in copies:
            copy.wait()

    @pl.when(slot == 1)
    def _():
        for copy in core_copies:
            copy.wait()

    part = dot(hidden[0], down[slot])

    @pl.when(slot == 0)
    def _():
        total[...] = part

    @pl.when(slot == 1)
    def _():
        whole, begin = (total[...] + part).astype(BF), 0
        for out in outs:
            out[...] = whole[begin : begin + out.shape[0]]
            begin += out.shape[0]


def down_project(z, hidden, w_own, w_core, width):
    _, tokens, ff = hidden.shape
    n_z, rows = len(w_own), tokens // 4
    sizes = (rows, rows, rows, rows // 2, rows // 2)
    return call(
        functools.partial(down_kernel, n_z),
        [shaped((size, width), BF) for size in sizes],
        flops=4 * tokens * width * ff,
        moved=8 * 10**6,
        grid_spec=pltpu.PrefetchScalarGridSpec(
            num_scalar_prefetch=1,
            grid=(2,),
            in_specs=[pl.BlockSpec((1, tokens, ff), lambda s, z: (s, 0, 0))]
            + [pl.BlockSpec(memory_space=pl.ANY)] * (2 * n_z),
            out_specs=[pl.BlockSpec((size, width), lambda s, z: (0, 0)) for size in sizes],
            scratch_shapes=[
                pltpu.VMEM((2, ff, width), BF),
                pltpu.VMEM((tokens, width), F32),
                pltpu.SemaphoreType.DMA((2, 4, n_z)),
            ],
        ),
    )(z, hidden, *w_own, *w_core)


def grads_kernel(left, right, *rest):
    grad = dot_tn(left[...].reshape(left.shape[-2:]), right[...].reshape(right.shape[-2:]))
    if len(rest) == 2:
        grad = grad + rest[0][...].astype(F32)
    rest[-1][...] = grad.astype(BF)


def weight_grads(left, left_slot, right, right_slot, steps, *other):
    tokens, rows, columns = left.shape[-2], left.shape[-1], right.shape[-1]
    block = pl.BlockSpec((rows, columns // steps), lambda i: (0, i))

    def part(array, slot, blocks):
        if array.ndim == 2:
            return pl.BlockSpec((tokens, array.shape[1] // blocks), lambda i: (0, i if blocks > 1 else 0))
        return pl.BlockSpec(
            (1, tokens, array.shape[2] // blocks), lambda i: (slot, 0, i if blocks > 1 else 0)
        )

    return call(
        grads_kernel,
        shaped((rows, columns), BF),
        flops=2 * tokens * rows * columns,
        moved=10 * 10**6,
        grid=(steps,),
        in_specs=[part(left, left_slot, 1), part(right, right_slot, steps)] + [block] * len(other),
        out_specs=block,
    )(left, right, *other)


def cut_kernel(place_ref, w_gate, w_up, mine, other):
    ff = mine.shape[1] // 2
    for to, y in ((mine, place_ref[1]), (other, 1 - place_ref[1])):
        for i, w in enumerate((w_gate, w_up)):
            for z in range(ff // 128):
                at = pl.multiple_of(((2 * z + y) * 4 + place_ref[0]) * 128, 128)
                begin = i * ff + z * 128
                to[:, begin : begin + 128] = w[:, pl.ds(at, 128)]


def cut_columns(place, w_gate, w_up, columns):
    vmem = pl.BlockSpec(memory_space=pltpu.VMEM)
    return call(
        cut_kernel,
        [shaped((w_gate.shape[0], columns), BF)] * 2,
        flops=10**6,
        moved=8 * 10**6,
        in_specs=[pl.BlockSpec(memory_space=pltpu.SMEM)] + [vmem] * 2,
        out_specs=[vmem] * 2,
    )(place, w_gate, w_up)


def place_kernel(z_ref, own, core, out):
    rows = own.shape[1]
    for slot, pieces in enumerate((own, core)):
        for k in range(own.shape[0]):
            to = pl.multiple_of((z_ref[0] ^ k) * rows, rows)
            out[slot, pl.ds(to, rows), :] = pieces[k]


def place(z, own, core):
    n, rows, columns = own.shape
    vmem = pl.BlockSpec(memory_space=pltpu.VMEM)
    return call(
        place_kernel,
        shaped((2, n * rows, columns), BF),
        flops=10**6,
        moved=8 * n * rows * columns,
        in_specs=[pl.BlockSpec(memory_space=pltpu.SMEM)] + [vmem] * 2,
        out_specs=vmem,
    )(z, own, core)


def turn_back(values, cosine, sine):
    lane = iota(values.shape, 1)
    across = values * sine
    moved = jnp.where(
        lane < HEAD // 2,
        pltpu.roll(across, 128 - HEAD // 2, 1),
        jnp.where(lane < HEAD, -pltpu.roll(across, HEAD // 2, 1), 0.0),
    )
    return values * cosine + moved


def attend_back_kernel(n_parts, *refs):
    y_ref, qkv, halo, seg_query, seg_key, w_out, context, logsum, cosine, sine = refs[:10]
    parts, rest = refs[10 : 10 + n_parts], refs[10 + n_parts :]
    before = rest[0] if len(rest) == 9 else None
    grad_query, grad_kv, grad_halo, grad_out, up, kv_total, out_total, sems = rest[-8:]
    slot = pl.program_id(0)
    reach = qkv.shape[1]
    rows = reach // 2
    factor = 1.0 / math.sqrt(HEAD)

    @pl.when(slot == 0)
    def _():
        for copy in load_blocks(parts, up, sems):
            copy.wait()

    at, query, key_value = heads_of(y_ref[0], slot, qkv, halo, rows)
    w = padded_out(w_out)
    kv_total[...] = jnp.zeros_like(kv_total)
    out_part = None
    for a in range(2):
        dy = up[at(a), :]
        d_context = dot_nt(dy, w).astype(BF)
        part = dot_tn(context[0, at(a), :], dy)
        out_part = part if out_part is None else out_part + part
        d_seen = jnp.concatenate([d_context[:, :128], d_context[:, 128:]], axis=0)
        kv = jnp.concatenate(key_value[a : a + 3], axis=0)
        key, value = kv[:, :128], kv[:, 128:]
        scores = dot_nt(query[a], key) * factor
        probs = jnp.exp(
            jnp.where(visible(seg_query, seg_key, a, rows), scores - logsum[0, a], -1e30)
        )
        d_probs = dot_nt(d_seen, value)
        delta = jnp.sum(probs * d_probs, axis=-1, keepdims=True)
        d_scores = (probs * (d_probs - delta)).astype(BF)
        d_query = dot(d_scores, key) * factor
        cos_a, sin_a = cosine[at(a), :], sine[at(a), :]
        turned = jnp.concatenate(
            [turn_back(d_query[:rows], cos_a, sin_a), turn_back(d_query[rows:], cos_a, sin_a)],
            axis=1,
        ).astype(BF)
        grad_query[0, at(a), :] = dot(turned, pack(qkv.shape[-1], 2, 0)).astype(BF)
        seen = slice(a * rows, (a + 3) * rows)
        kv_total[seen, :128] += dot_tn(d_scores, query[a]) * factor
        kv_total[seen, 128:] += dot_tn(probs.astype(BF), d_seen)
    back = pack(qkv.shape[-1], 2, (1 - slot) * (qkv.shape[-1] // 2))
    for a in range(2):
        grad_kv[0, at(a), :] = kv_total[(a + 2) * rows : (a + 3) * rows, :]
        placed = dot(kv_total[a * rows : (a + 1) * rows, :].astype(BF), back).astype(BF)

        @pl.when(slot == 0)
        def _():
            grad_halo[at(a), :] = placed

        @pl.when(slot == 1)
        def _():
            grad_halo[at(a), :] += placed

    out_total[...] = out_part.astype(BF)
    part = dot(spread(w_out.shape[1], 2, 0), out_total[...])
    if before is not None:
        part = part + before[0].astype(F32)
    grad_out[0] = part.astype(BF)


def attend_back(y, group, qkv, halo, seg_query, seg_key, w_out, context, logsum, cosine, sine, upstream, before=()):
    slots, reach, lanes = qkv.shape
    rows, width = reach // 2, w_out.shape[-1]
    weight = pl.BlockSpec((1,) + w_out.shape[1:], lambda s, y: (s, 0, 0))
    return call(
        functools.partial(attend_back_kernel, len(upstream)),
        [
            shaped((slots, reach, lanes), BF),
            shaped((slots, reach, 256), F32),
            shaped((reach, lanes), BF),
            shaped(w_out.shape, BF),
        ],
        flops=12 * 10**9,
        moved=10 * 10**6,
        grid_spec=pltpu.PrefetchScalarGridSpec(
            num_scalar_prefetch=1,
            grid=(slots,),
            in_specs=[
                pl.BlockSpec((1, reach, lanes), lambda s, y: (s, 0, 0)),
                pl.BlockSpec((reach, lanes), lambda s, y: (0, 0)),
                pl.BlockSpec((1, 2, rows, 1), lambda s, y: (group, 0, 0, 0)),
                pl.BlockSpec((1, 4, 1, rows), lambda s, y: (group, 0, 0, 0)),
                weight,
                pl.BlockSpec((1, reach, 256), lambda s, y: (s, 0, 0)),
                pl.BlockSpec((1, 2, reach, 1), lambda s, y: (s, 0, 0, 0)),
                pl.BlockSpec((reach, 128), lambda s, y: (group, 0)),
                pl.BlockSpec((reach, 128), lambda s, y: (group, 0)),
            ]
            + [pl.BlockSpec(memory_space=pl.ANY)] * len(upstream)
            + [weight] * len(before),
            out_specs=[
                pl.BlockSpec((1, reach, lanes), lambda s, y: (s, 0, 0)),
                pl.BlockSpec((1, reach, 256), lambda s, y: (s, 0, 0)),
                pl.BlockSpec((reach, lanes), lambda s, y: (0, 0)),
                weight,
            ],
            scratch_shapes=[
                pltpu.VMEM((reach, width), BF),
                pltpu.VMEM((2 * reach, 256), F32),
                pltpu.VMEM((256, width), BF),
                pltpu.SemaphoreType.DMA((len(upstream),)),
            ],
        ),
    )(y, qkv, halo, seg_query, seg_key, w_out, context, logsum, cosine, sine, *upstream, *before)


def qkv_back_kernel(grad_query, grad_kv, grad_halo, cosine, sine, w_own, w_core, grad_qkv, *grad_in):
    lanes = grad_halo.shape[-1]
    total = None
    place = pack(lanes, 2, lanes // 2)
    size = grad_in[0].shape[1] // w_own.shape[0]
    for slot, w in enumerate((w_own, w_core)):
        kv = grad_kv[slot] + dot(grad_halo[...], spread(lanes, 2, (1 - slot) * (lanes // 2)))
        key = turn_back(kv[:, :128], cosine[...], sine[...])
        kv = jnp.concatenate([key, kv[:, 128:]], axis=1).astype(BF)
        both = grad_query[slot] + dot(kv, place).astype(BF)
        grad_qkv[slot] = both
        part = [dot_nt(both, w[z, :size, :]) for z in range(w.shape[0])]
        part = jnp.concatenate(part, axis=1)
        total = part if total is None else total + part
    whole, begin = total.astype(BF), 0
    for out in grad_in:
        out[...] = whole[begin : begin + out.shape[0]]
        begin += out.shape[0]


def qkv_back(group, grad_query, grad_kv, grad_halo, cosine, sine, w_own, w_core, width):
    slots, tokens, lanes = grad_query.shape
    rows = tokens // 2
    sizes = (rows, rows // 2, rows // 2) if group else (rows, rows)
    table = pl.BlockSpec((tokens, 128), lambda i: (group, 0))

    def whole(array):
        return pl.BlockSpec(array.shape, lambda i: (0,) * array.ndim)

    outs = [shaped((slots, tokens, lanes), BF)] + [shaped((size, width), BF) for size in sizes]
    return call(
        qkv_back_kernel,
        outs,
        flops=2 * slots * tokens * width * lanes,
        moved=6 * 10**6,
        grid=(1,),
        in_specs=[whole(grad_query), whole(grad_kv), whole(grad_halo), table, table]
        + [whole(w_own), whole(w_core)],
        out_specs=[whole(out) for out in outs],
    )(grad_query, grad_kv, grad_halo, cosine, sine, w_own, w_core)


def lay_out_kernel(d_ref, *refs):
    b0, b1, b2, b3, w_gate, w_up, gain, out_gate, out_up, grad_gain = refs
    ff = b0.shape[2] // 2
    for k, block in enumerate((b0, b1, b2, b3)):
        for y in range(2):
            for z in range(ff // 128):
                to = pl.multiple_of(((2 * z + y) * 4 + (d_ref[0] ^ k)) * 128, 128)
                out_gate[:, pl.ds(to, 128)] = block[y, :, z * 128 : (z + 1) * 128].astype(F32)
                out_up[:, pl.ds(to, 128)] = block[y, :, ff + z * 128 : ff + (z + 1) * 128].astype(F32)
    weighted = w_gate[...].astype(F32) * out_gate[...] + w_up[...].astype(F32) * out_up[...]
    grad_gain[...] = jnp.sum(weighted, axis=-1, keepdims=True) / gain[...]


def lay_out(d, blocks, w_gate, w_up, gain):
    shard, ff = w_gate.shape
    rows = 64
    blocks = [block.reshape(2, shard, block.shape[1]) for block in blocks]
    part = pl.BlockSpec((2, rows, blocks[0].shape[2]), lambda i, d: (0, i, 0))
    whole = pl.BlockSpec((rows, ff), lambda i, d: (i, 0))
    column = pl.BlockSpec((rows, 1), lambda i, d: (i, 0))
    return call(
        lay_out_kernel,
        [shaped((shard, ff), F32), shaped((shard, ff), F32), shaped((shard, 1), F32)],
        flops=6 * shard * ff,
        moved=16 * shard * ff,
        grid_spec=pltpu.PrefetchScalarGridSpec(
            num_scalar_prefetch=1,
            grid=(shard // rows,),
            in_specs=[part] * 4 + [whole, whole, column],
            out_specs=[whole, whole, column],
        ),
    )(d, *blocks, w_gate, w_up, gain)


def lay_out_rows_kernel(d_ref, b0, b1, b2, b3, out):
    rows = b0.shape[0]
    for k, block in enumerate((b0, b1, b2, b3)):
        at = pl.ds(pl.multiple_of((d_ref[0] ^ k) * rows, rows), rows)
        out[at, :] = block[...].astype(F32)


def lay_out_rows(d, blocks):
    rows, width = blocks[0].shape
    vmem = pl.BlockSpec(memory_space=pltpu.VMEM)
    return call(
        lay_out_rows_kernel,
        shaped((4 * rows, width), F32),
        flops=rows * width,
        moved=24 * rows * width,
        in_specs=[pl.BlockSpec(memory_space=pltpu.SMEM)] + [vmem] * 4,
        out_specs=vmem,
    )(d, *blocks)


def lay_out_heads_kernel(d_ref, *refs):
    blocks, (w_query, w_key, w_value, gain) = refs[:4], refs[4:8]
    out_query, out_key, out_value, out_out, grad_gain, ordered = refs[8:]
    shard, lanes = w_query.shape[0], blocks[0].shape[1]
    count = out_out.shape[0] // 4
    for k, block in enumerate(blocks):
        to = d_ref[0] ^ k
        ordered[to] = block[: 2 * shard, :]
        at = pl.ds(pl.multiple_of(to * count, count), count)
        for i in range(4):
            out_out[at, i * lanes : (i + 1) * lanes] = block[
                2 * shard + i * count : 2 * shard + (i + 1) * count, :
            ].astype(F32)
    row, column = iota((lanes, lanes), 0), iota((lanes, lanes), 1)

    def place(begin, count, to):
        hit = (column - to == row - begin) & (row >= begin) & (row < begin + count)
        return jnp.where(hit, 1.0, 0.0).astype(BF)

    def block_of(t):
        return ordered[t // 2, (t % 2) * shard : (t % 2 + 1) * shard, :]

    total = None
    for begin, count, out, w in (
        (0, 2 * HEAD, out_query, w_query),
        (2 * HEAD, HEAD, out_key, w_key),
        (3 * HEAD, HEAD, out_value, w_value),
    ):
        heads = lanes // count
        places = [place(begin, count, i * count) for i in range(heads)]
        for j in range(KV_HEADS // heads):
            piece = None
            for i in range(heads):
                part = dot(block_of(j * heads + i), places[i])
                piece = part if piece is None else piece + part
            at = slice(j * lanes, (j + 1) * lanes)
            out[:, at] = piece
            part = jnp.sum(w[:, at].astype(F32) * piece, axis=-1, keepdims=True)
            total = part if total is None else total + part
    grad_gain[...] = total / gain[...]


def lay_out_heads(d, blocks, w_query, w_key, w_value, gain, out_shape):
    shard = w_query.shape[0]
    vmem = pl.BlockSpec(memory_space=pltpu.VMEM)
    return call(
        lay_out_heads_kernel,
        [
            shaped(w_query.shape, F32),
            shaped(w_key.shape, F32),
            shaped(w_value.shape, F32),
            shaped(out_shape, F32),
            shaped((shard, 1), F32),
        ],
        flops=4 * 10**9,
        moved=8 * 10**6,
        in_specs=[pl.BlockSpec(memory_space=pltpu.SMEM)] + [vmem] * 8,
        out_specs=[vmem] * 5,
        scratch_shapes=[pltpu.VMEM((4, 2 * shard, blocks[0].shape[1]), BF)],
    )(d, *blocks, w_query, w_key, w_value, gain)


def layout_rows(lengths, index):
    ends = jnp.cumsum(lengths, axis=1)
    before = index[None, :, None] >= ends[:, None, :]
    segment = jnp.sum(before.astype(jnp.int32), axis=2)
    offset = jnp.sum(jnp.where(before, lengths[:, None, :], 0), axis=2)
    segment = jnp.where(segment < lengths.shape[1], segment, -1)
    segment = jnp.where(index[None, :] < 0, -3, segment)
    return (segment, index[None, :] - offset)


def on_device(
    tokens,
    lengths,
    cotangent,
    gain_attn,
    w_query,
    w_key,
    w_value,
    w_out,
    gain_mlp,
    w_gate,
    w_up,
    w_down,
):
    n_dp, n_seq = lax.axis_size("dp"), lax.axis_size("seq")
    d, me = lax.axis_index("dp"), lax.axis_index("seq")
    y, n_z = me % 2, n_seq // 2
    rows, width = tokens.shape
    reach = 2 * rows
    assert WINDOW <= reach and KV_HEADS == 2 * n_dp
    groups = HEADS // KV_HEADS
    q_w, k_w = groups * HEAD, HEAD
    shard = w_query.shape[0]
    ff_shard = w_down.shape[0]
    ff_part = ff_shard // n_dp

    def head_columns(j):
        t = 2 * d + j
        gains = jnp.zeros((16, q_w + 2 * k_w), BF)
        gains = gains.at[0, :shard].set(gain_attn).at[1, :shard].set(gain_mlp)
        columns = jnp.concatenate(
            [
                lax.dynamic_slice_in_dim(w_query, t * q_w, q_w, 1),
                lax.dynamic_slice_in_dim(w_key, t * k_w, k_w, 1),
                lax.dynamic_slice_in_dim(w_value, t * k_w, k_w, 1),
            ],
            axis=1,
        )
        return jnp.concatenate([columns, gains], axis=0)

    def ff_columns(j):
        parts = [
            lax.dynamic_slice_in_dim(w, ((2 * z + j) * n_dp + d) * ff_part, ff_part, 1)
            for w in (gate_in, up_in)
            for z in range(n_z)
        ]
        return jnp.concatenate(parts, axis=1)

    lanes = q_w + 2 * k_w
    square = n_seq == 2 * n_dp
    d_arg = jnp.reshape(d, (1,)).astype(jnp.int32)
    z_arg = jnp.reshape(me // 2, (1,)).astype(jnp.int32)

    lens_far = send(lengths, across_x)
    qkv_from_y = send(head_columns(1 - y), across_y)
    tokens_all = gather_plane(tokens, for_y=after(tokens, qkv_from_y))
    low, high = pair_y(head_columns(y), qkv_from_y)
    gain_rows = jnp.concatenate([low[shard:, :shard], high[shard:, :shard]], axis=1)
    gain_rows = jnp.pad(gain_rows, ((0, 0), (0, lanes - 2 * shard)))
    part_qkv = jnp.concatenate([low[:shard], high[:shard], gain_rows], axis=0)
    own_qkv = gather_z(part_qkv)
    lens = jnp.concatenate([lengths, after(lens_far, part_qkv)], axis=0)

    first_row = (me // 2) * reach
    steps = jnp.arange(reach, dtype=jnp.int32)
    order = jnp.arange(2, dtype=jnp.int32)[:, None] ^ y
    _, position = layout_rows(lens, first_row + (order * rows + steps[None, :rows]).reshape(-1))
    cosine, sine = rope_tables(position.reshape(-1))
    key_index = first_row - reach + jnp.arange(2 * reach, dtype=jnp.int32)
    segment, _ = layout_rows(lens, key_index)
    segment = jnp.where(segment == -1, -8 - key_index[None, :], segment)
    seg_key = segment.reshape(2, 4, 1, rows)
    seg_query = segment[:, reach:].reshape(2, 2, rows, 1)
    y_arg = jnp.reshape(y, (1,)).astype(jnp.int32)

    gate_in, up_in = lax.optimization_barrier((w_gate, w_up, qkv_from_y))[:2]
    if ff_part % 128 == 0:
        here = jnp.stack([d, y]).astype(jnp.int32)
        mine_ff, other_ff = cut_columns(here, gate_in, up_in, 2 * n_z * ff_part)
    else:
        mine_ff, other_ff = ff_columns(y), ff_columns(1 - y)
    other_ff = send(after(other_ff, tokens_all[1]), across_y)
    part_mlp = jnp.concatenate(
        [
            pair_y(mine_ff, other_ff).reshape(2 * shard, -1),
            fold(lax.dynamic_slice_in_dim(w_down, d * ff_part, ff_part, 0), 2 * n_z * ff_part),
        ],
        axis=0,
    )
    early = ()
    if square:
        out_rows = shard // n_dp
        part_out = lax.dynamic_slice_in_dim(w_out, d * out_rows, out_rows, 0)
        part_out = send(after(part_out, part_qkv), turned)
        early = (part_out,)
    own_qkv = lax.optimization_barrier((own_qkv, part_mlp, cosine, *early, *tokens_all))[0]
    core_qkv = send(own_qkv, across_core)
    if square:
        out_pieces = [send(after(part_out, own_qkv), across_z(k)) for k in (1, 2, 3)]
    else:
        own_out = lax.all_gather(w_out, "seq", axis=0, tiled=True)
        own_out = lax.dynamic_slice_in_dim(own_out, (2 * d + y) * q_w, q_w, 0)
    full_qkv = [own_qkv, core_qkv]
    if not square:
        full_qkv = [part[:, : 2 * shard].reshape(1, width, lanes) for part in full_qkv]
    gains = own_qkv[:, 2 * shard : 2 * shard + 2, : 2 * shard]
    full_gain_attn = gains[:, 0].reshape(1, -1).astype(F32)
    full_gain_mlp = gains[:, 1].reshape(1, -1).astype(F32)

    groups_of = ((0, 1), (2, 3, 4))

    def parts_of(pieces, group):
        return [pieces[i] for i in groups_of[group]]

    normed, qkv, halo, halo_in = [None] * 2, [None] * 2, [None] * 2, [None] * 2
    for group in (1, 0):
        normed[group], qkv[group], halo[group] = project(
            group, parts_of(tokens_all, group), full_gain_attn, cosine, sine, *full_qkv
        )
        halo_in[group] = send(halo[group], lambda d, s: (d, s + 2))
    if square:
        out_pieces = lax.optimization_barrier((*out_pieces, *halo))[:3]
        own_out = jnp.stack([part_out, *out_pieces])
        full_out = place(z_arg, own_out, send(own_out, across_core))
    else:
        full_out = jnp.stack(with_core(own_out))
    part_ready = lax.optimization_barrier((part_mlp, *halo_in))[0]
    if square:
        both = send(part_ready, across_z(2))
        mlp_near = send(part_ready, across_z(1))
    else:
        blocks = gather_z(part_ready)
        down_rows = jnp.concatenate([unfold(blocks[z, 2 * shard :], width) for z in range(n_z)], axis=0)
        own_mlp = [
            jnp.concatenate(
                [blocks[:, : 2 * shard].reshape(width, -1), fold(down_rows, 2 * n_z * ff_part)], axis=0
            )
        ]
    cotangent_in = after(cotangent, *tokens_all)
    came = (send(cotangent_in, across_x), send(cotangent_in, across_y))
    upstream_all = gather_plane(cotangent, *halo, came=came)
    halo_first = lax.optimization_barrier((halo_in[0], *upstream_all))[0]
    partial, context, logsum = [None] * 2, [None] * 2, [None] * 2
    for group in (1, 0):
        *partial[group], context[group], logsum[group] = attend(
            y_arg, group, qkv[group], halo_in[1] if group else halo_first, seg_query, seg_key, full_out
        )
    arrived = (both, mlp_near) if square else ()
    middle = tokens.astype(F32) + scatter_plane(*partial, *arrived)


    inverse_mlp = lax.rsqrt(jnp.mean(middle * middle, axis=-1, keepdims=True) + EPS)
    normed_mlp_own = (middle * inverse_mlp * full_gain_mlp).astype(BF)
    if square:
        mlp_far = both
        own_mlp = [part_mlp, mlp_near, mlp_far, send(mlp_far, across_z(1))]
    normed_mlp_all = gather_plane(normed_mlp_own)
    core_mlp = [send(block, across_core) for block in own_mlp]
    z_own = z_arg if square else jnp.zeros_like(z_arg)
    hidden, grad_gu, *grad_in, normed_mlp, upstream_low = feed_forward(
        z_own, normed_mlp_all, upstream_all, own_mlp, core_mlp
    )
    grad_near, grad_far = grad_in[:2], grad_in[2:]
    from_core_gu = send(weight_grads(normed_mlp, 0, grad_gu, 1, 2), across_core)
    down_core = weight_grads(hidden, 1, upstream_low, 0, 1)
    grad_w_gu = weight_grads(normed_mlp, 0, grad_gu, 0, 2, from_core_gu)
    grad_normed_mlp = scatter_plane(grad_near, grad_far, at_first=(down_core, grad_w_gu))
    got_gu = along_z(grad_w_gu.reshape(n_z, 2 * shard, -1))
    total_gu = jnp.sum(got_gu.astype(F32), axis=0).astype(BF)
    upstream = cotangent.astype(F32)
    scaled = grad_normed_mlp * full_gain_mlp
    grad_middle = (
        upstream
        + inverse_mlp * scaled
        - middle * inverse_mlp**3 * jnp.mean(scaled * middle, axis=-1, keepdims=True)
    )
    down = down_project(z_own, hidden, own_mlp, core_mlp, width)
    from_core = send(down_core, across_core)
    grad_w_down = weight_grads(hidden, 0, upstream_low, 0, 1, from_core)
    grad_attended_all = gather_plane(
        after(grad_middle.astype(BF), grad_w_gu), *down, grad_w_down
    )
    down = lax.optimization_barrier((*down, *grad_attended_all))[:5]

    def swap_rows(total):
        mine = lax.dynamic_slice_in_dim(total, y * shard, shard, 0)
        other = lax.dynamic_slice_in_dim(total, (1 - y) * shard, shard, 0)
        return pair_y(mine, send(other, across_y)).reshape(2 * shard, -1)

    mine_gu = swap_rows(total_gu)
    gu_blocks = gather_dp(mine_gu)
    if ff_part % 128 == 0:
        gain_column = gain_mlp.astype(F32).reshape(-1, 1)
        out_gate, out_up, grad_gain_mlp = lay_out(d_arg, gu_blocks, w_gate, w_up, gain_column)
    else:
        all_gu = jnp.stack(order_dp(gu_blocks)).reshape(n_dp, 2, shard, 2, n_z, ff_part)
        all_gu = all_gu.transpose(3, 2, 4, 1, 0, 5).reshape(2, shard, -1).astype(F32)
        out_gate, out_up = all_gu[0], all_gu[1]
        grad_gain_mlp = jnp.sum(
            w_gate.astype(F32) * out_gate + w_up.astype(F32) * out_up, axis=1
        ) / gain_mlp.astype(F32)

    grad_query, grad_kv, halo_back = [None] * 2, [None] * 2, [None] * 2
    grad_out = ()
    for group in (0, 1):
        dy = parts_of(grad_attended_all, group)
        grad_query[group], grad_kv[group], grad_halo, grad_out = attend_back(
            y_arg, group, qkv[group], halo_in[group], seg_query, seg_key, full_out,
            context[group], logsum[group], cosine, sine, dy, (grad_out,) if group else (),
        )
        halo_back[group] = send(after(grad_halo, got_gu), lambda d, s: (d, s - 2))
    grad_qkv, grad_in = [None] * 2, [None] * 2
    halo_back[1] = after(halo_back[1], mine_gu)
    for group in (0, 1):
        grad_qkv[group], *grad_in[group] = qkv_back(
            group, grad_query[group], grad_kv[group], halo_back[group], cosine, sine, *full_qkv, width
        )
    grad_w_down = lax.optimization_barrier((grad_w_down, halo_back[1]))[0]
    total_down = scatter_z(grad_w_down.reshape(n_z, ff_part, width)).astype(BF)
    out_down = lay_out_rows(d_arg, gather_dp(total_down))

    def attn_grads(slot):
        for_qkv = dot_tn(normed[0], grad_qkv[0][slot]) + dot_tn(normed[1], grad_qkv[1][slot])
        for_qkv = for_qkv.astype(BF).reshape(n_z, 2 * shard, -1)
        if not square:
            return for_qkv
        for_out = [
            fold(grad_out[slot, z * out_rows : (z + 1) * out_rows], lanes) for z in range(n_z)
        ]
        return jnp.concatenate([for_qkv, jnp.stack(for_out)], axis=1)

    grad_attn = sum_core(attn_grads(0), attn_grads(1))
    total_attn = along_z(grad_attn)
    total_attn, out_gate, out_up, out_down, grad_gain_mlp = lax.optimization_barrier(
        (total_attn, out_gate, out_up, out_down, grad_gain_mlp)
    )
    total_attn = jnp.sum(total_attn.astype(F32), axis=0).astype(BF)
    mine_attn = swap_rows(total_attn[: 2 * shard]).reshape(2 * shard, -1)
    if square:
        mine_attn = jnp.concatenate([mine_attn, send(total_attn[2 * shard :], turned)], axis=0)
    attn_blocks = gather_dp(mine_attn)
    if square:
        out_query, out_key, out_value, out_out, grad_gain_attn = lay_out_heads(
            d_arg, attn_blocks, w_query, w_key, w_value, gain_attn.astype(F32).reshape(-1, 1), w_out.shape
        )
    else:
        attn_blocks = order_dp(attn_blocks)
        grad_w_out = sum_core(grad_out[0], grad_out[1]).astype(F32)
        out_out = jnp.zeros((2 * n_dp * q_w, width), F32)
        out_out = lax.dynamic_update_slice_in_dim(out_out, grad_w_out, (2 * d + y) * q_w, 0)
        out_out = lax.psum_scatter(out_out, "seq", scatter_dimension=0, tiled=True)
        out_out = lax.psum(out_out.astype(BF), "dp").astype(F32)
        all_qkv = jnp.stack(attn_blocks).astype(F32)
        out_qkv = all_qkv.reshape(2 * n_dp, shard, lanes).transpose(1, 0, 2)
        out_query = out_qkv[..., :q_w].reshape(shard, -1)
        out_key = out_qkv[..., q_w : q_w + k_w].reshape(shard, -1)
        out_value = out_qkv[..., q_w + k_w :].reshape(shard, -1)
        grad_gain_attn = (
            jnp.sum(w_query.astype(F32) * out_query, axis=1)
            + jnp.sum(w_key.astype(F32) * out_key, axis=1)
            + jnp.sum(w_value.astype(F32) * out_value, axis=1)
        ) / gain_attn.astype(F32)

    own = scatter_plane(*grad_in)
    wide = tokens.astype(F32)
    own_inverse = lax.rsqrt(jnp.mean(wide * wide, axis=-1, keepdims=True) + EPS)
    scaled = own * full_gain_attn
    grad_tokens = (
        grad_middle
        + own_inverse * scaled
        - wide * own_inverse**3 * jnp.mean(scaled * wide, axis=-1, keepdims=True)
    )
    output = (middle + scatter_plane(down[:2], down[2:])).astype(BF)
    return (
        output,
        grad_tokens,
        grad_gain_attn.reshape(-1),
        out_query,
        out_key,
        out_value,
        out_out,
        grad_gain_mlp.reshape(-1),
        out_gate,
        out_up,
        out_down,
    )


def solution(mesh):
    return jax.shard_map(
        on_device,
        mesh=mesh,
        in_specs=(
            P(("dp", "seq"), None),
            P("dp", None),
            P(("dp", "seq"), None),
            P("seq"),
            P("seq", None),
            P("seq", None),
            P("seq", None),
            P("seq", None),
            P("seq"),
            P("seq", None),
            P("seq", None),
            P("seq", None),
        ),
        out_specs=(
            P(("dp", "seq"), None),
            P(("dp", "seq"), None),
            P("seq"),
            P("seq", None),
            P("seq", None),
            P("seq", None),
            P("seq", None),
            P("seq"),
            P("seq", None),
            P("seq", None),
            P("seq", None),
        ),
        check_vma=False,
    )
```

```python
import functools
import math

import jax
import jax.numpy as jnp
from jax import lax
from jax.experimental import pallas as pl
from jax.experimental.pallas import tpu as pltpu
from jax.sharding import PartitionSpec as P

HEADS = 16
KV_HEADS = 8
HEAD = 96
WINDOW = 512


EPS = 1e-05
THETA = 100000.0
BOTH = ("dp", "seq")
BF = jnp.bfloat16
F32 = jnp.float32


def send(block, target):
    n_dp, n_seq = lax.axis_size("dp"), lax.axis_size("seq")
    route = []
    for d in range(n_dp):
        for s in range(n_seq):
            to = target(d, s)
            if to is not None and 0 <= to[1] < n_seq:
                route.append((d * n_seq + s, to[0] * n_seq + to[1]))
    return lax.ppermute(block, BOTH, route)


def after(value, *others):
    return lax.optimization_barrier((value,) + others)[0]


def across_core(d, s):
    return (d ^ 1, s)


def across_x(d, s):
    return (d ^ 2, s)


def across_y(d, s):
    return (d, s ^ 1)


def gather_plane(block, *meanwhile, for_y=None, came=None):
    half = block.shape[0] // 2
    from_x, from_y = came or (
        send(block, across_x),
        send(block if for_y is None else for_y, across_y),
    )
    if meanwhile:
        from_x, from_y = lax.optimization_barrier((from_x, from_y, *meanwhile))[:2]
    first = send(from_x[:half], across_y)
    second = send(from_y[half:], across_x)
    return [block, from_y, from_x, first, second]


def plus(a, b):
    return (a.astype(F32) + b.astype(F32)).astype(BF)


def scatter_plane(near, far, *meanwhile, at_first=()):
    own, own_y = near
    far, far_a, far_b = far
    half = far_a.shape[0]
    first = send(far_a, across_y)
    second = send(far_b, across_x)
    if at_first:
        first, second = lax.optimization_barrier((first, second, *at_first))[:2]

    far = jnp.concatenate([plus(far[:half], first), far[half:]], axis=0)
    own_y = jnp.concatenate([own_y[:half], plus(own_y[half:], second)], axis=0)
    from_x, from_y = send(far, across_x), send(own_y, across_y)
    if meanwhile:
        from_x, from_y = lax.optimization_barrier((from_x, from_y, *meanwhile))[:2]
    return own.astype(F32) + from_x.astype(F32) + from_y.astype(F32)


def with_core(block):
    return [block, send(block, across_core)]


def sum_core(mine, other):
    return (mine.astype(F32) + send(other.astype(BF), across_core).astype(F32)).astype(BF)


def across_z(k):
    return lambda d, s: (d, s ^ (2 * k))


def along_z(blocks):
    n_seq = lax.axis_size("seq")
    lines = [list(range(y, n_seq, 2)) for y in range(2)]
    return lax.all_to_all(blocks, "seq", 0, 0, axis_index_groups=lines)


def gather_z(block):
    return along_z(jnp.broadcast_to(block[None], (lax.axis_size("seq") // 2,) + block.shape))


def scatter_z(blocks):
    return jnp.sum(along_z(blocks).astype(F32), axis=0)


def pair_y(mine, other):
    y = lax.axis_index("seq") % 2
    return jnp.stack([jnp.where(y == 0, mine, other), jnp.where(y == 0, other, mine)])


def turned(d, s):
    return (s // 2, 2 * d + s % 2)


def fold(rows, wide):
    count, columns = rows.shape
    whole = columns // wide
    parts = [rows[:, i * wide : (i + 1) * wide] for i in range(whole)]
    rest = rows[:, whole * wide :]
    if rest.shape[1]:
        times = wide // rest.shape[1]
        step = count // times
        parts.append(
            jnp.concatenate([rest[i * step : (i + 1) * step] for i in range(times)], axis=1)
        )
    return jnp.concatenate(parts, axis=0)


def unfold(folded, columns):
    total, wide = folded.shape
    count = total * wide // columns
    whole = columns // wide
    parts = [folded[i * count : (i + 1) * count] for i in range(whole)]
    if columns % wide:
        rest, narrow = folded[whole * count :], columns % wide
        parts.append(
            jnp.concatenate(
                [rest[:, i * narrow : (i + 1) * narrow] for i in range(wide // narrow)], axis=0
            )
        )
    return jnp.concatenate(parts, axis=1)


def gather_dp(block, *meanwhile):
    core = send(block, across_core)
    far = send(block, across_x)
    if meanwhile:
        far = lax.optimization_barrier((far, *meanwhile))[0]
    return [block, core, far, send(far, across_core)]


def order_dp(blocks):
    d = lax.axis_index("dp")
    pairs = [
        (jnp.where(d % 2 == 0, a, b), jnp.where(d % 2 == 0, b, a))
        for a, b in (blocks[:2], blocks[2:])
    ]
    low, high = pairs
    return [jnp.where(d < 2, a, b) for a, b in zip(low, high)] + [
        jnp.where(d < 2, b, a) for a, b in zip(low, high)
    ]


def rope_tables(position):
    lane = jnp.arange(128, dtype=jnp.float32) % (HEAD // 2)
    angles = position.astype(jnp.float32)[..., None] * THETA ** (-2.0 * lane / HEAD)
    return jnp.cos(angles), jnp.sin(angles)


SCALE = 0.3
VMEM_BYTES = 60 * 1024 * 1024


def call(kernel, out_shape, flops, moved, **rest):
    return pl.pallas_call(
        kernel,
        out_shape=out_shape,
        compiler_params=pltpu.CompilerParams(vmem_limit_bytes=VMEM_BYTES),
        cost_estimate=pl.CostEstimate(flops=int(flops * SCALE), bytes_accessed=int(moved * SCALE), transcendentals=0),
        **rest,
    )


def shaped(shape, dtype):
    return jax.ShapeDtypeStruct(shape, dtype)


def iota(shape, axis):
    return lax.broadcasted_iota(jnp.int32, shape, axis)


def dot(a, b):
    return jnp.dot(a, b, preferred_element_type=F32)


def dot_nt(a, b):
    return lax.dot_general(a, b, (((1,), (1,)), ((), ())), preferred_element_type=F32)


def dot_tn(a, b):
    return lax.dot_general(a, b, (((0,), (0,)), ((), ())), preferred_element_type=F32)


def spread(packed, heads, base):
    row, column = iota((packed, heads * 128), 0), iota((packed, heads * 128), 1)
    lane = column % 128
    hit = (row == base + HEAD * (column // 128) + lane) & (lane < HEAD)
    return jnp.where(hit, 1.0, 0.0).astype(BF)


def pack(packed, heads, base):
    column, row = iota((heads * 128, packed), 0), iota((heads * 128, packed), 1)
    lane = column % 128
    hit = (row == base + HEAD * (column // 128) + lane) & (lane < HEAD)
    return jnp.where(hit, 1.0, 0.0).astype(BF)


def on_heads(table, heads, packed):
    row, column = iota((128, packed), 0), iota((128, packed), 1)
    place = jnp.where((row == column % HEAD) & (column < heads * HEAD), 1.0, 0.0).astype(BF)
    high = table.astype(BF)
    rest = table - high.astype(F32)
    middle = rest.astype(BF)
    low = (rest - middle.astype(F32)).astype(BF)
    return dot(high, place) + dot(middle, place) + dot(low, place)


def qkv_kernel(*refs):
    parts, refs = refs[:-8], refs[-8:]
    gain, cosine, sine, w_own, w_core, normed, qkv, halo = refs
    tokens, lanes = halo.shape
    x = jnp.concatenate([part[...] for part in parts], axis=0).astype(F32)
    inverse = lax.rsqrt(jnp.mean(x * x, axis=-1, keepdims=True) + EPS)
    low = (x * inverse * gain[...]).astype(BF)
    normed[...] = low
    lane = iota((tokens, lanes), 1)
    first = lane % HEAD < HEAD // 2
    cos_all = on_heads(cosine[...], 3, lanes) + jnp.where(lane >= 3 * HEAD, 1.0, 0.0)
    sin_all = on_heads(sine[...], 3, lanes)
    turned = []
    size = normed.shape[1] // w_own.shape[0]
    for w in (w_own, w_core):
        raw = sum(dot(low[:, z * size : (z + 1) * size], w[z, :size, :]) for z in range(w.shape[0]))
        half = jnp.where(
            first, -pltpu.roll(raw, lanes - HEAD // 2, 1), pltpu.roll(raw, HEAD // 2, 1)
        )
        turned.append(raw * cos_all + half * sin_all)
    qkv[0] = turned[0].astype(BF)
    qkv[1] = turned[1].astype(BF)
    halo[...] = jnp.where(
        lane < lanes // 2, pltpu.roll(turned[1], lanes // 2, 1), turned[0]
    ).astype(BF)


def project(group, parts, gain, cosine, sine, w_own, w_core):
    tokens = sum(part.shape[0] for part in parts)
    width, lanes = gain.shape[1], w_own.shape[2]

    def whole(array):
        return pl.BlockSpec(array.shape, lambda i: (0,) * array.ndim)

    table = pl.BlockSpec((tokens, 128), lambda i: (group, 0))
    outs = [shaped((tokens, width), BF), shaped((2, tokens, lanes), BF), shaped((tokens, lanes), BF)]
    return call(
        qkv_kernel,
        outs,
        flops=4 * tokens * width * lanes,
        moved=6 * 10**6,
        grid=(1,),
        in_specs=[whole(part) for part in parts] + [whole(gain), table, table, whole(w_own), whole(w_core)],
        out_specs=[whole(out) for out in outs],
    )(*parts, gain, cosine, sine, w_own, w_core)


def visible(seg_query, seg_key, a, rows):
    shape = (rows, 3 * rows)
    row, column = iota(shape, 0), iota(shape, 1)
    same = seg_query[0, a] == jnp.concatenate([seg_key[0, a + i] for i in range(3)], axis=1)
    allowed = (column > row) & (column <= row + 2 * rows) & same
    return jnp.concatenate([allowed, allowed], axis=0)


def heads_of(y, slot, qkv, halo, rows):
    lanes = qkv.shape[-1]

    def at(a):
        return pl.ds(pl.multiple_of((a ^ y) * rows, rows), rows)

    before = spread(lanes, 2, (1 - slot) * (lanes // 2))
    here = spread(lanes, 4, 0)
    local = [dot(qkv[0, at(a), :], here).astype(BF) for a in range(2)]
    key_value = [dot(halo[at(a), :], before).astype(BF) for a in range(2)]
    key_value += [part[:, 256:] for part in local]
    query = [jnp.concatenate([part[:, :128], part[:, 128:256]], axis=0) for part in local]
    return at, query, key_value


def padded_out(w_out):
    rows = w_out.shape[1]
    return dot(pack(rows, 2, 0), w_out[0]).astype(BF)


def attend_kernel(y_ref, qkv, halo, seg_query, seg_key, w_out, *refs):
    *partial, context, logsum, total = refs
    slot = pl.program_id(0)
    rows = qkv.shape[1] // 2
    at, query, key_value = heads_of(y_ref[0], slot, qkv, halo, rows)
    w = padded_out(w_out)
    for a in range(2):
        kv = jnp.concatenate(key_value[a : a + 3], axis=0)
        scores = dot_nt(query[a], kv[:, :128]) * (1.0 / math.sqrt(HEAD))
        scores = jnp.where(visible(seg_query, seg_key, a, rows), scores, -1e30)
        peak = jnp.max(scores, axis=-1, keepdims=True)
        exponent = jnp.exp(scores - peak)
        row_total = jnp.sum(exponent, axis=-1, keepdims=True)
        probs = (exponent * (1.0 / row_total)).astype(BF)
        logsum[0, a] = peak + jnp.log(row_total)
        seen = dot(probs, kv[:, 128:]).astype(BF)
        seen = jnp.concatenate([seen[:rows], seen[rows:]], axis=1)
        context[0, at(a), :] = seen
        product = dot(seen, w)

        @pl.when(slot == 0)
        def _():
            total[at(a), :] = product

        @pl.when(slot == 1)
        def _():
            total[at(a), :] += product

    @pl.when(slot == 1)
    def _():
        begin = 0
        for out in partial:
            out[...] = total[begin : begin + out.shape[0], :].astype(BF)
            begin += out.shape[0]


def attend(y, group, qkv, halo, seg_query, seg_key, w_out):
    slots, reach, lanes = qkv.shape
    rows, width = reach // 2, w_out.shape[-1]
    sizes = (rows, rows // 2, rows // 2) if group else (rows, rows)
    return call(
        attend_kernel,
        [shaped((size, width), BF) for size in sizes]
        + [
            shaped((slots, reach, 256), BF),
            shaped((slots, 2, reach, 1), F32),
        ],
        flops=5 * 10**9,
        moved=7 * 10**6,
        grid_spec=pltpu.PrefetchScalarGridSpec(
            num_scalar_prefetch=1,
            grid=(slots,),
            in_specs=[
                pl.BlockSpec((1, reach, lanes), lambda s, y: (s, 0, 0)),
                pl.BlockSpec((reach, lanes), lambda s, y: (0, 0)),
                pl.BlockSpec((1, 2, rows, 1), lambda s, y: (group, 0, 0, 0)),
                pl.BlockSpec((1, 4, 1, rows), lambda s, y: (group, 0, 0, 0)),
                pl.BlockSpec((1,) + w_out.shape[1:], lambda s, y: (s, 0, 0)),
            ],
            out_specs=[pl.BlockSpec((size, width), lambda s, y: (0, 0)) for size in sizes]
            + [
                pl.BlockSpec((1, reach, 256), lambda s, y: (s, 0, 0)),
                pl.BlockSpec((1, 2, reach, 1), lambda s, y: (s, 0, 0, 0)),
            ],
            scratch_shapes=[pltpu.VMEM((reach, width), F32)],
        ),
    )(y, qkv, halo, seg_query, seg_key, w_out)


def load_blocks(parts, whole, sems):
    copies, at = [], 0
    for i, part in enumerate(parts):
        copies.append(
            pltpu.make_async_copy(part, whole.at[pl.ds(at, part.shape[0])], sems.at[i])
        )
        at += part.shape[0]
    for copy in copies:
        copy.start()
    return copies


def weight_copies(me, weights, gu, down, sems):
    n_z, wide = len(weights), weights[0].shape[1]
    width = down.shape[1]
    step, ff_part = width // n_z, down.shape[0] // n_z
    half = ff_part * (width - wide) // wide
    first, second = [], []
    for r, block in enumerate(weights):
        z = me ^ r
        row = pl.multiple_of(z * ff_part, ff_part)
        if gu is not None:
            first.append(
                pltpu.make_async_copy(
                    block.at[pl.ds(0, step)],
                    gu.at[pl.ds(pl.multiple_of(z * step, step), step)],
                    sems.at[0, r],
                )
            )
        second.append(
            pltpu.make_async_copy(
                block.at[pl.ds(step, ff_part)],
                down.at[pl.ds(row, ff_part), pl.ds(0, wide)],
                sems.at[1, r],
            )
        )
        for i in range(2):
            second.append(
                pltpu.make_async_copy(
                    block.at[pl.ds(step + ff_part, half), pl.ds(i * wide // 2, wide // 2)],
                    down.at[pl.ds(row + i * half, half), pl.ds(wide, width - wide)],
                    sems.at[2 + i, r],
                )
            )
    return first + second


def mlp_kernel(n_z, z_ref, *refs):
    n_parts, d_parts, refs = refs[:5], refs[5:10], refs[10:]
    w_own, w_core, refs = refs[:n_z], refs[n_z : 2 * n_z], refs[2 * n_z :]
    hidden, grad_gu, *grad_in, normed_out, upstream_out = refs[:9]
    normed, upstream, gu, down, total, n_sems, d_sems, w_sems, out_sems = refs[9:]
    slot = pl.program_id(0)
    ff = gu.shape[2] // 2
    core_copies = weight_copies(z_ref[0], w_core, gu.at[1], down.at[1], w_sems.at[1])
    kept = [
        pltpu.make_async_copy(normed, normed_out, out_sems.at[0]),
        pltpu.make_async_copy(upstream, upstream_out, out_sems.at[1]),
    ]

    @pl.when(slot == 0)
    def _():
        copies = load_blocks(n_parts, normed, n_sems)
        copies += weight_copies(z_ref[0], w_own, gu.at[0], down.at[0], w_sems.at[0])
        for copy in copies[5:]:
            copy.start()
        copies += load_blocks(d_parts, upstream, d_sems)
        for copy in core_copies:
            copy.start()
        for copy in copies:
            copy.wait()
        for copy in kept:
            copy.start()

    @pl.when(slot == 1)
    def _():
        for copy in core_copies:
            copy.wait()

    n, dy = normed[...], upstream[...]
    gate = dot(n, gu[slot, :, :ff])
    up = dot(n, gu[slot, :, ff:])
    dh = dot_nt(dy, down[slot])
    sigmoid = jax.nn.sigmoid(gate)
    silu = gate * sigmoid
    hidden[0] = (silu * up).astype(BF)
    d_gate = (dh * up * sigmoid * (1.0 + gate * (1.0 - sigmoid))).astype(BF)
    d_up = (dh * silu).astype(BF)
    grad_gu[0, :, :ff] = d_gate
    grad_gu[0, :, ff:] = d_up
    part = dot_nt(d_gate, gu[slot, :, :ff]) + dot_nt(d_up, gu[slot, :, ff:])

    @pl.when(slot == 0)
    def _():
        total[...] = part

    @pl.when(slot == 1)
    def _():
        whole = (total[...] + part).astype(BF)
        begin = 0
        for out in grad_in:
            out[...] = whole[begin : begin + out.shape[0]]
            begin += out.shape[0]
        for copy in kept:
            copy.wait()


def feed_forward(z, normed, upstream, w_own, w_core):
    rows, width = normed[0].shape
    n_z, wide = len(w_own), w_own[0].shape[1]
    tokens, ff = 4 * rows, wide // 2
    anywhere = pl.BlockSpec(memory_space=pl.ANY)
    block = pl.BlockSpec((rows, width), lambda s, z: (0, 0))
    half = pl.BlockSpec((rows // 2, width), lambda s, z: (0, 0))
    return call(
        functools.partial(mlp_kernel, n_z),
        [
            shaped((2, tokens, ff), BF),
            shaped((2, tokens, wide), BF),
            shaped((rows, width), BF),
            shaped((rows, width), BF),
            shaped((rows, width), BF),
            shaped((rows // 2, width), BF),
            shaped((rows // 2, width), BF),
            shaped((tokens, width), BF),
            shaped((tokens, width), BF),
        ],
        flops=10 * tokens * width * wide,
        moved=25 * 10**6,
        grid_spec=pltpu.PrefetchScalarGridSpec(
            num_scalar_prefetch=1,
            grid=(2,),
            in_specs=[anywhere] * (10 + 2 * n_z),
            out_specs=[
                pl.BlockSpec((1, tokens, ff), lambda s, z: (s, 0, 0)),
                pl.BlockSpec((1, tokens, wide), lambda s, z: (s, 0, 0)),
                block,
                block,
                block,
                half,
                half,
                anywhere,
                anywhere,
            ],
            scratch_shapes=[
                pltpu.VMEM((tokens, width), BF),
                pltpu.VMEM((tokens, width), BF),
                pltpu.VMEM((2, width, wide), BF),
                pltpu.VMEM((2, ff, width), BF),
                pltpu.VMEM((tokens, width), F32),
                pltpu.SemaphoreType.DMA((5,)),
                pltpu.SemaphoreType.DMA((5,)),
                pltpu.SemaphoreType.DMA((2, 4, n_z)),
                pltpu.SemaphoreType.DMA((2,)),
            ],
        ),
    )(z, *normed, *upstream, *w_own, *w_core)


def down_kernel(n_z, z_ref, hidden, *refs):
    w_own, w_core, refs = refs[:n_z], refs[n_z : 2 * n_z], refs[2 * n_z :]
    *outs, down, total, sems = refs
    slot = pl.program_id(0)
    core_copies = weight_copies(z_ref[0], w_core, None, down.at[1], sems.at[1])

    @pl.when(slot == 0)
    def _():
        copies = weight_copies(z_ref[0], w_own, None, down.at[0], sems.at[0])
        for copy in copies + core_copies:
            copy.start()
        for copy in copies:
            copy.wait()

    @pl.when(slot == 1)
    def _():
        for copy in core_copies:
            copy.wait()

    part = dot(hidden[0], down[slot])

    @pl.when(slot == 0)
    def _():
        total[...] = part

    @pl.when(slot == 1)
    def _():
        whole, begin = (total[...] + part).astype(BF), 0
        for out in outs:
            out[...] = whole[begin : begin + out.shape[0]]
            begin += out.shape[0]


def down_project(z, hidden, w_own, w_core, width):
    _, tokens, ff = hidden.shape
    n_z, rows = len(w_own), tokens // 4
    sizes = (rows, rows, rows, rows // 2, rows // 2)
    return call(
        functools.partial(down_kernel, n_z),
        [shaped((size, width), BF) for size in sizes],
        flops=4 * tokens * width * ff,
        moved=8 * 10**6,
        grid_spec=pltpu.PrefetchScalarGridSpec(
            num_scalar_prefetch=1,
            grid=(2,),
            in_specs=[pl.BlockSpec((1, tokens, ff), lambda s, z: (s, 0, 0))]
            + [pl.BlockSpec(memory_space=pl.ANY)] * (2 * n_z),
            out_specs=[pl.BlockSpec((size, width), lambda s, z: (0, 0)) for size in sizes],
            scratch_shapes=[
                pltpu.VMEM((2, ff, width), BF),
                pltpu.VMEM((tokens, width), F32),
                pltpu.SemaphoreType.DMA((2, 4, n_z)),
            ],
        ),
    )(z, hidden, *w_own, *w_core)


def grads_kernel(left, right, *rest):
    grad = dot_tn(left[...].reshape(left.shape[-2:]), right[...].reshape(right.shape[-2:]))
    if len(rest) == 2:
        grad = grad + rest[0][...].astype(F32)
    rest[-1][...] = grad.astype(BF)


def weight_grads(left, left_slot, right, right_slot, steps, *other):
    tokens, rows, columns = left.shape[-2], left.shape[-1], right.shape[-1]
    block = pl.BlockSpec((rows, columns // steps), lambda i: (0, i))

    def part(array, slot, blocks):
        if array.ndim == 2:
            return pl.BlockSpec((tokens, array.shape[1] // blocks), lambda i: (0, i if blocks > 1 else 0))
        return pl.BlockSpec(
            (1, tokens, array.shape[2] // blocks), lambda i: (slot, 0, i if blocks > 1 else 0)
        )

    return call(
        grads_kernel,
        shaped((rows, columns), BF),
        flops=2 * tokens * rows * columns,
        moved=10 * 10**6,
        grid=(steps,),
        in_specs=[part(left, left_slot, 1), part(right, right_slot, steps)] + [block] * len(other),
        out_specs=block,
    )(left, right, *other)


def cut_kernel(place_ref, w_gate, w_up, mine, other):
    ff = mine.shape[1] // 2
    for to, y in ((mine, place_ref[1]), (other, 1 - place_ref[1])):
        for i, w in enumerate((w_gate, w_up)):
            for z in range(ff // 128):
                at = pl.multiple_of(((2 * z + y) * 4 + place_ref[0]) * 128, 128)
                begin = i * ff + z * 128
                to[:, begin : begin + 128] = w[:, pl.ds(at, 128)]


def cut_columns(place, w_gate, w_up, columns):
    vmem = pl.BlockSpec(memory_space=pltpu.VMEM)
    return call(
        cut_kernel,
        [shaped((w_gate.shape[0], columns), BF)] * 2,
        flops=10**6,
        moved=8 * 10**6,
        in_specs=[pl.BlockSpec(memory_space=pltpu.SMEM)] + [vmem] * 2,
        out_specs=[vmem] * 2,
    )(place, w_gate, w_up)


def place_kernel(z_ref, own, core, out):
    rows = own.shape[1]
    for slot, pieces in enumerate((own, core)):
        for k in range(own.shape[0]):
            to = pl.multiple_of((z_ref[0] ^ k) * rows, rows)
            out[slot, pl.ds(to, rows), :] = pieces[k]


def place(z, own, core):
    n, rows, columns = own.shape
    vmem = pl.BlockSpec(memory_space=pltpu.VMEM)
    return call(
        place_kernel,
        shaped((2, n * rows, columns), BF),
        flops=10**6,
        moved=8 * n * rows * columns,
        in_specs=[pl.BlockSpec(memory_space=pltpu.SMEM)] + [vmem] * 2,
        out_specs=vmem,
    )(z, own, core)


def turn_back(values, cosine, sine):
    lane = iota(values.shape, 1)
    across = values * sine
    moved = jnp.where(
        lane < HEAD // 2,
        pltpu.roll(across, 128 - HEAD // 2, 1),
        jnp.where(lane < HEAD, -pltpu.roll(across, HEAD // 2, 1), 0.0),
    )
    return values * cosine + moved


def attend_back_kernel(n_parts, *refs):
    y_ref, qkv, halo, seg_query, seg_key, w_out, context, logsum, cosine, sine = refs[:10]
    parts, rest = refs[10 : 10 + n_parts], refs[10 + n_parts :]
    before = rest[0] if len(rest) == 9 else None
    grad_query, grad_kv, grad_halo, grad_out, up, kv_total, out_total, sems = rest[-8:]
    slot = pl.program_id(0)
    reach = qkv.shape[1]
    rows = reach // 2
    factor = 1.0 / math.sqrt(HEAD)

    @pl.when(slot == 0)
    def _():
        for copy in load_blocks(parts, up, sems):
            copy.wait()

    at, query, key_value = heads_of(y_ref[0], slot, qkv, halo, rows)
    w = padded_out(w_out)
    kv_total[...] = jnp.zeros_like(kv_total)
    out_part = None
    for a in range(2):
        dy = up[at(a), :]
        d_context = dot_nt(dy, w).astype(BF)
        part = dot_tn(context[0, at(a), :], dy)
        out_part = part if out_part is None else out_part + part
        d_seen = jnp.concatenate([d_context[:, :128], d_context[:, 128:]], axis=0)
        kv = jnp.concatenate(key_value[a : a + 3], axis=0)
        key, value = kv[:, :128], kv[:, 128:]
        scores = dot_nt(query[a], key) * factor
        probs = jnp.exp(
            jnp.where(visible(seg_query, seg_key, a, rows), scores - logsum[0, a], -1e30)
        )
        d_probs = dot_nt(d_seen, value)
        delta = jnp.sum(probs * d_probs, axis=-1, keepdims=True)
        d_scores = (probs * (d_probs - delta)).astype(BF)
        d_query = dot(d_scores, key) * factor
        cos_a, sin_a = cosine[at(a), :], sine[at(a), :]
        turned = jnp.concatenate(
            [turn_back(d_query[:rows], cos_a, sin_a), turn_back(d_query[rows:], cos_a, sin_a)],
            axis=1,
        ).astype(BF)
        grad_query[0, at(a), :] = dot(turned, pack(qkv.shape[-1], 2, 0)).astype(BF)
        seen = slice(a * rows, (a + 3) * rows)
        kv_total[seen, :128] += dot_tn(d_scores, query[a]) * factor
        kv_total[seen, 128:] += dot_tn(probs.astype(BF), d_seen)
    back = pack(qkv.shape[-1], 2, (1 - slot) * (qkv.shape[-1] // 2))
    for a in range(2):
        grad_kv[0, at(a), :] = kv_total[(a + 2) * rows : (a + 3) * rows, :]
        placed = dot(kv_total[a * rows : (a + 1) * rows, :].astype(BF), back).astype(BF)

        @pl.when(slot == 0)
        def _():
            grad_halo[at(a), :] = placed

        @pl.when(slot == 1)
        def _():
            grad_halo[at(a), :] += placed

    out_total[...] = out_part.astype(BF)
    part = dot(spread(w_out.shape[1], 2, 0), out_total[...])
    if before is not None:
        part = part + before[0].astype(F32)
    grad_out[0] = part.astype(BF)


def attend_back(y, group, qkv, halo, seg_query, seg_key, w_out, context, logsum, cosine, sine, upstream, before=()):
    slots, reach, lanes = qkv.shape
    rows, width = reach // 2, w_out.shape[-1]
    weight = pl.BlockSpec((1,) + w_out.shape[1:], lambda s, y: (s, 0, 0))
    return call(
        functools.partial(attend_back_kernel, len(upstream)),
        [
            shaped((slots, reach, lanes), BF),
            shaped((slots, reach, 256), F32),
            shaped((reach, lanes), BF),
            shaped(w_out.shape, BF),
        ],
        flops=12 * 10**9,
        moved=10 * 10**6,
        grid_spec=pltpu.PrefetchScalarGridSpec(
            num_scalar_prefetch=1,
            grid=(slots,),
            in_specs=[
                pl.BlockSpec((1, reach, lanes), lambda s, y: (s, 0, 0)),
                pl.BlockSpec((reach, lanes), lambda s, y: (0, 0)),
                pl.BlockSpec((1, 2, rows, 1), lambda s, y: (group, 0, 0, 0)),
                pl.BlockSpec((1, 4, 1, rows), lambda s, y: (group, 0, 0, 0)),
                weight,
                pl.BlockSpec((1, reach, 256), lambda s, y: (s, 0, 0)),
                pl.BlockSpec((1, 2, reach, 1), lambda s, y: (s, 0, 0, 0)),
                pl.BlockSpec((reach, 128), lambda s, y: (group, 0)),
                pl.BlockSpec((reach, 128), lambda s, y: (group, 0)),
            ]
            + [pl.BlockSpec(memory_space=pl.ANY)] * len(upstream)
            + [weight] * len(before),
            out_specs=[
                pl.BlockSpec((1, reach, lanes), lambda s, y: (s, 0, 0)),
                pl.BlockSpec((1, reach, 256), lambda s, y: (s, 0, 0)),
                pl.BlockSpec((reach, lanes), lambda s, y: (0, 0)),
                weight,
            ],
            scratch_shapes=[
                pltpu.VMEM((reach, width), BF),
                pltpu.VMEM((2 * reach, 256), F32),
                pltpu.VMEM((256, width), BF),
                pltpu.SemaphoreType.DMA((len(upstream),)),
            ],
        ),
    )(y, qkv, halo, seg_query, seg_key, w_out, context, logsum, cosine, sine, *upstream, *before)


def qkv_back_kernel(grad_query, grad_kv, grad_halo, cosine, sine, w_own, w_core, grad_qkv, *grad_in):
    lanes = grad_halo.shape[-1]
    total = None
    place = pack(lanes, 2, lanes // 2)
    size = grad_in[0].shape[1] // w_own.shape[0]
    for slot, w in enumerate((w_own, w_core)):
        kv = grad_kv[slot] + dot(grad_halo[...], spread(lanes, 2, (1 - slot) * (lanes // 2)))
        key = turn_back(kv[:, :128], cosine[...], sine[...])
        kv = jnp.concatenate([key, kv[:, 128:]], axis=1).astype(BF)
        both = grad_query[slot] + dot(kv, place).astype(BF)
        grad_qkv[slot] = both
        part = [dot_nt(both, w[z, :size, :]) for z in range(w.shape[0])]
        part = jnp.concatenate(part, axis=1)
        total = part if total is None else total + part
    whole, begin = total.astype(BF), 0
    for out in grad_in:
        out[...] = whole[begin : begin + out.shape[0]]
        begin += out.shape[0]


def qkv_back(group, grad_query, grad_kv, grad_halo, cosine, sine, w_own, w_core, width):
    slots, tokens, lanes = grad_query.shape
    rows = tokens // 2
    sizes = (rows, rows // 2, rows // 2) if group else (rows, rows)
    table = pl.BlockSpec((tokens, 128), lambda i: (group, 0))

    def whole(array):
        return pl.BlockSpec(array.shape, lambda i: (0,) * array.ndim)

    outs = [shaped((slots, tokens, lanes), BF)] + [shaped((size, width), BF) for size in sizes]
    return call(
        qkv_back_kernel,
        outs,
        flops=2 * slots * tokens * width * lanes,
        moved=6 * 10**6,
        grid=(1,),
        in_specs=[whole(grad_query), whole(grad_kv), whole(grad_halo), table, table]
        + [whole(w_own), whole(w_core)],
        out_specs=[whole(out) for out in outs],
    )(grad_query, grad_kv, grad_halo, cosine, sine, w_own, w_core)


def lay_out_kernel(d_ref, *refs):
    b0, b1, b2, b3, w_gate, w_up, gain, out_gate, out_up, grad_gain = refs
    ff = b0.shape[2] // 2
    for k, block in enumerate((b0, b1, b2, b3)):
        for y in range(2):
            for z in range(ff // 128):
                to = pl.multiple_of(((2 * z + y) * 4 + (d_ref[0] ^ k)) * 128, 128)
                out_gate[:, pl.ds(to, 128)] = block[y, :, z * 128 : (z + 1) * 128].astype(F32)
                out_up[:, pl.ds(to, 128)] = block[y, :, ff + z * 128 : ff + (z + 1) * 128].astype(F32)
    weighted = w_gate[...].astype(F32) * out_gate[...] + w_up[...].astype(F32) * out_up[...]
    grad_gain[...] = jnp.sum(weighted, axis=-1, keepdims=True) / gain[...]


def lay_out(d, blocks, w_gate, w_up, gain):
    shard, ff = w_gate.shape
    rows = 64
    blocks = [block.reshape(2, shard, block.shape[1]) for block in blocks]
    part = pl.BlockSpec((2, rows, blocks[0].shape[2]), lambda i, d: (0, i, 0))
    whole = pl.BlockSpec((rows, ff), lambda i, d: (i, 0))
    column = pl.BlockSpec((rows, 1), lambda i, d: (i, 0))
    return call(
        lay_out_kernel,
        [shaped((shard, ff), F32), shaped((shard, ff), F32), shaped((shard, 1), F32)],
        flops=6 * shard * ff,
        moved=16 * shard * ff,
        grid_spec=pltpu.PrefetchScalarGridSpec(
            num_scalar_prefetch=1,
            grid=(shard // rows,),
            in_specs=[part] * 4 + [whole, whole, column],
            out_specs=[whole, whole, column],
        ),
    )(d, *blocks, w_gate, w_up, gain)


def lay_out_rows_kernel(d_ref, b0, b1, b2, b3, out):
    rows = b0.shape[0]
    for k, block in enumerate((b0, b1, b2, b3)):
        at = pl.ds(pl.multiple_of((d_ref[0] ^ k) * rows, rows), rows)
        out[at, :] = block[...].astype(F32)


def lay_out_rows(d, blocks):
    rows, width = blocks[0].shape
    vmem = pl.BlockSpec(memory_space=pltpu.VMEM)
    return call(
        lay_out_rows_kernel,
        shaped((4 * rows, width), F32),
        flops=rows * width,
        moved=24 * rows * width,
        in_specs=[pl.BlockSpec(memory_space=pltpu.SMEM)] + [vmem] * 4,
        out_specs=vmem,
    )(d, *blocks)


def lay_out_heads_kernel(d_ref, *refs):
    blocks, (w_query, w_key, w_value, gain) = refs[:4], refs[4:8]
    out_query, out_key, out_value, out_out, grad_gain, ordered = refs[8:]
    shard, lanes = w_query.shape[0], blocks[0].shape[1]
    count = out_out.shape[0] // 4
    for k, block in enumerate(blocks):
        to = d_ref[0] ^ k
        ordered[to] = block[: 2 * shard, :]
        at = pl.ds(pl.multiple_of(to * count, count), count)
        for i in range(4):
            out_out[at, i * lanes : (i + 1) * lanes] = block[
                2 * shard + i * count : 2 * shard + (i + 1) * count, :
            ].astype(F32)
    row, column = iota((lanes, lanes), 0), iota((lanes, lanes), 1)

    def place(begin, count, to):
        hit = (column - to == row - begin) & (row >= begin) & (row < begin + count)
        return jnp.where(hit, 1.0, 0.0).astype(BF)

    def block_of(t):
        return ordered[t // 2, (t % 2) * shard : (t % 2 + 1) * shard, :]

    total = None
    for begin, count, out, w in (
        (0, 2 * HEAD, out_query, w_query),
        (2 * HEAD, HEAD, out_key, w_key),
        (3 * HEAD, HEAD, out_value, w_value),
    ):
        heads = lanes // count
        places = [place(begin, count, i * count) for i in range(heads)]
        for j in range(KV_HEADS // heads):
            piece = None
            for i in range(heads):
                part = dot(block_of(j * heads + i), places[i])
                piece = part if piece is None else piece + part
            at = slice(j * lanes, (j + 1) * lanes)
            out[:, at] = piece
            part = jnp.sum(w[:, at].astype(F32) * piece, axis=-1, keepdims=True)
            total = part if total is None else total + part
    grad_gain[...] = total / gain[...]


def lay_out_heads(d, blocks, w_query, w_key, w_value, gain, out_shape):
    shard = w_query.shape[0]
    vmem = pl.BlockSpec(memory_space=pltpu.VMEM)
    return call(
        lay_out_heads_kernel,
        [
            shaped(w_query.shape, F32),
            shaped(w_key.shape, F32),
            shaped(w_value.shape, F32),
            shaped(out_shape, F32),
            shaped((shard, 1), F32),
        ],
        flops=4 * 10**9,
        moved=8 * 10**6,
        in_specs=[pl.BlockSpec(memory_space=pltpu.SMEM)] + [vmem] * 8,
        out_specs=[vmem] * 5,
        scratch_shapes=[pltpu.VMEM((4, 2 * shard, blocks[0].shape[1]), BF)],
    )(d, *blocks, w_query, w_key, w_value, gain)


def layout_rows(lengths, index):
    ends = jnp.cumsum(lengths, axis=1)
    before = index[None, :, None] >= ends[:, None, :]
    segment = jnp.sum(before.astype(jnp.int32), axis=2)
    offset = jnp.sum(jnp.where(before, lengths[:, None, :], 0), axis=2)
    segment = jnp.where(segment < lengths.shape[1], segment, -1)
    segment = jnp.where(index[None, :] < 0, -3, segment)
    return (segment, index[None, :] - offset)


def on_device(
    tokens,
    lengths,
    cotangent,
    gain_attn,
    w_query,
    w_key,
    w_value,
    w_out,
    gain_mlp,
    w_gate,
    w_up,
    w_down,
):
    n_dp, n_seq = lax.axis_size("dp"), lax.axis_size("seq")
    d, me = lax.axis_index("dp"), lax.axis_index("seq")
    y, n_z = me % 2, n_seq // 2
    rows, width = tokens.shape
    reach = 2 * rows
    assert WINDOW <= reach and KV_HEADS == 2 * n_dp
    groups = HEADS // KV_HEADS
    q_w, k_w = groups * HEAD, HEAD
    shard = w_query.shape[0]
    ff_shard = w_down.shape[0]
    ff_part = ff_shard // n_dp

    def head_columns(j):
        t = 2 * d + j
        gains = jnp.zeros((16, q_w + 2 * k_w), BF)
        gains = gains.at[0, :shard].set(gain_attn).at[1, :shard].set(gain_mlp)
        columns = jnp.concatenate(
            [
                lax.dynamic_slice_in_dim(w_query, t * q_w, q_w, 1),
                lax.dynamic_slice_in_dim(w_key, t * k_w, k_w, 1),
                lax.dynamic_slice_in_dim(w_value, t * k_w, k_w, 1),
            ],
            axis=1,
        )
        return jnp.concatenate([columns, gains], axis=0)

    def ff_columns(j):
        parts = [
            lax.dynamic_slice_in_dim(w, ((2 * z + j) * n_dp + d) * ff_part, ff_part, 1)
            for w in (gate_in, up_in)
            for z in range(n_z)
        ]
        return jnp.concatenate(parts, axis=1)

    lanes = q_w + 2 * k_w
    square = n_seq == 2 * n_dp
    d_arg = jnp.reshape(d, (1,)).astype(jnp.int32)
    z_arg = jnp.reshape(me // 2, (1,)).astype(jnp.int32)

    lens_far = send(lengths, across_x)
    qkv_from_y = send(head_columns(1 - y), across_y)
    tokens_all = gather_plane(tokens, for_y=after(tokens, qkv_from_y))
    low, high = pair_y(head_columns(y), qkv_from_y)
    gain_rows = jnp.concatenate([low[shard:, :shard], high[shard:, :shard]], axis=1)
    gain_rows = jnp.pad(gain_rows, ((0, 0), (0, lanes - 2 * shard)))
    part_qkv = jnp.concatenate([low[:shard], high[:shard], gain_rows], axis=0)
    own_qkv = gather_z(part_qkv)
    lens = jnp.concatenate([lengths, after(lens_far, part_qkv)], axis=0)

    first_row = (me // 2) * reach
    steps = jnp.arange(reach, dtype=jnp.int32)
    order = jnp.arange(2, dtype=jnp.int32)[:, None] ^ y
    _, position = layout_rows(lens, first_row + (order * rows + steps[None, :rows]).reshape(-1))
    cosine, sine = rope_tables(position.reshape(-1))
    key_index = first_row - reach + jnp.arange(2 * reach, dtype=jnp.int32)
    segment, _ = layout_rows(lens, key_index)
    segment = jnp.where(segment == -1, -8 - key_index[None, :], segment)
    seg_key = segment.reshape(2, 4, 1, rows)
    seg_query = segment[:, reach:].reshape(2, 2, rows, 1)
    y_arg = jnp.reshape(y, (1,)).astype(jnp.int32)

    gate_in, up_in = lax.optimization_barrier((w_gate, w_up, qkv_from_y))[:2]
    if ff_part % 128 == 0:
        here = jnp.stack([d, y]).astype(jnp.int32)
        mine_ff, other_ff = cut_columns(here, gate_in, up_in, 2 * n_z * ff_part)
    else:
        mine_ff, other_ff = ff_columns(y), ff_columns(1 - y)
    other_ff = send(after(other_ff, tokens_all[1]), across_y)
    part_mlp = jnp.concatenate(
        [
            pair_y(mine_ff, other_ff).reshape(2 * shard, -1),
            fold(lax.dynamic_slice_in_dim(w_down, d * ff_part, ff_part, 0), 2 * n_z * ff_part),
        ],
        axis=0,
    )
    early = ()
    if square:
        out_rows = shard // n_dp
        part_out = lax.dynamic_slice_in_dim(w_out, d * out_rows, out_rows, 0)
        part_out = send(after(part_out, part_qkv), turned)
        early = (part_out,)
    own_qkv = lax.optimization_barrier((own_qkv, part_mlp, cosine, *early, *tokens_all))[0]
    core_qkv = send(own_qkv, across_core)
    if square:
        out_pieces = [send(after(part_out, own_qkv), across_z(k)) for k in (1, 2, 3)]
    else:
        own_out = lax.all_gather(w_out, "seq", axis=0, tiled=True)
        own_out = lax.dynamic_slice_in_dim(own_out, (2 * d + y) * q_w, q_w, 0)
    full_qkv = [own_qkv, core_qkv]
    if not square:
        full_qkv = [part[:, : 2 * shard].reshape(1, width, lanes) for part in full_qkv]
    gains = own_qkv[:, 2 * shard : 2 * shard + 2, : 2 * shard]
    full_gain_attn = gains[:, 0].reshape(1, -1).astype(F32)
    full_gain_mlp = gains[:, 1].reshape(1, -1).astype(F32)

    groups_of = ((0, 1), (2, 3, 4))

    def parts_of(pieces, group):
        return [pieces[i] for i in groups_of[group]]

    normed, qkv, halo, halo_in = [None] * 2, [None] * 2, [None] * 2, [None] * 2
    for group in (1, 0):
        normed[group], qkv[group], halo[group] = project(
            group, parts_of(tokens_all, group), full_gain_attn, cosine, sine, *full_qkv
        )
        halo_in[group] = send(halo[group], lambda d, s: (d, s + 2))
    if square:
        out_pieces = lax.optimization_barrier((*out_pieces, *halo))[:3]
        own_out = jnp.stack([part_out, *out_pieces])
        full_out = place(z_arg, own_out, send(own_out, across_core))
    else:
        full_out = jnp.stack(with_core(own_out))
    part_ready = lax.optimization_barrier((part_mlp, *halo_in))[0]
    if square:
        both = send(part_ready, across_z(2))
        mlp_near = send(part_ready, across_z(1))
    else:
        blocks = gather_z(part_ready)
        down_rows = jnp.concatenate([unfold(blocks[z, 2 * shard :], width) for z in range(n_z)], axis=0)
        own_mlp = [
            jnp.concatenate(
                [blocks[:, : 2 * shard].reshape(width, -1), fold(down_rows, 2 * n_z * ff_part)], axis=0
            )
        ]
    cotangent_in = after(cotangent, *tokens_all)
    came = (send(cotangent_in, across_x), send(cotangent_in, across_y))
    upstream_all = gather_plane(cotangent, *halo, came=came)
    halo_first = lax.optimization_barrier((halo_in[0], *upstream_all))[0]
    partial, context, logsum = [None] * 2, [None] * 2, [None] * 2
    for group in (1, 0):
        *partial[group], context[group], logsum[group] = attend(
            y_arg, group, qkv[group], halo_in[1] if group else halo_first, seg_query, seg_key, full_out
        )
    arrived = (both, mlp_near) if square else ()
    middle = tokens.astype(F32) + scatter_plane(*partial, *arrived)


    inverse_mlp = lax.rsqrt(jnp.mean(middle * middle, axis=-1, keepdims=True) + EPS)
    normed_mlp_own = (middle * inverse_mlp * full_gain_mlp).astype(BF)
    if square:
        mlp_far = both
        own_mlp = [part_mlp, mlp_near, mlp_far, send(mlp_far, across_z(1))]
    normed_mlp_all = gather_plane(normed_mlp_own)
    core_mlp = [send(block, across_core) for block in own_mlp]
    z_own = z_arg if square else jnp.zeros_like(z_arg)
    hidden, grad_gu, *grad_in, normed_mlp, upstream_low = feed_forward(
        z_own, normed_mlp_all, upstream_all, own_mlp, core_mlp
    )
    grad_near, grad_far = grad_in[:2], grad_in[2:]
    from_core_gu = send(weight_grads(normed_mlp, 0, grad_gu, 1, 2), across_core)
    down_core = weight_grads(hidden, 1, upstream_low, 0, 1)
    grad_w_gu = weight_grads(normed_mlp, 0, grad_gu, 0, 2, from_core_gu)
    grad_normed_mlp = scatter_plane(grad_near, grad_far, at_first=(down_core, grad_w_gu))
    got_gu = along_z(grad_w_gu.reshape(n_z, 2 * shard, -1))
    total_gu = jnp.sum(got_gu.astype(F32), axis=0).astype(BF)
    upstream = cotangent.astype(F32)
    scaled = grad_normed_mlp * full_gain_mlp
    grad_middle = (
        upstream
        + inverse_mlp * scaled
        - middle * inverse_mlp**3 * jnp.mean(scaled * middle, axis=-1, keepdims=True)
    )
    down = down_project(z_own, hidden, own_mlp, core_mlp, width)
    from_core = send(down_core, across_core)
    grad_w_down = weight_grads(hidden, 0, upstream_low, 0, 1, from_core)
    grad_attended_all = gather_plane(
        after(grad_middle.astype(BF), grad_w_gu), *down, grad_w_down
    )
    down = lax.optimization_barrier((*down, *grad_attended_all))[:5]
    (own, own_y), (far, far_a, far_b) = down[:2], down[2:]
    half = rows // 2
    first, second = send(far_a, across_y), send(far_b, across_x)

    def swap_rows(total):
        mine = lax.dynamic_slice_in_dim(total, y * shard, shard, 0)
        other = lax.dynamic_slice_in_dim(total, (1 - y) * shard, shard, 0)
        return pair_y(mine, send(other, across_y)).reshape(2 * shard, -1)

    mine_gu = swap_rows(total_gu)
    gu_blocks = gather_dp(mine_gu)
    if ff_part % 128 == 0:
        gain_column = gain_mlp.astype(F32).reshape(-1, 1)
        out_gate, out_up, grad_gain_mlp = lay_out(d_arg, gu_blocks, w_gate, w_up, gain_column)
    else:
        all_gu = jnp.stack(order_dp(gu_blocks)).reshape(n_dp, 2, shard, 2, n_z, ff_part)
        all_gu = all_gu.transpose(3, 2, 4, 1, 0, 5).reshape(2, shard, -1).astype(F32)
        out_gate, out_up = all_gu[0], all_gu[1]
        grad_gain_mlp = jnp.sum(
            w_gate.astype(F32) * out_gate + w_up.astype(F32) * out_up, axis=1
        ) / gain_mlp.astype(F32)

    grad_query, grad_kv, halo_back = [None] * 2, [None] * 2, [None] * 2
    grad_out = ()
    for group in (0, 1):
        dy = parts_of(grad_attended_all, group)
        grad_query[group], grad_kv[group], grad_halo, grad_out = attend_back(
            y_arg, group, qkv[group], halo_in[group], seg_query, seg_key, full_out,
            context[group], logsum[group], cosine, sine, dy, (grad_out,) if group else (),
        )
        grad_halo, first, second = lax.optimization_barrier((grad_halo, first, second, got_gu))[:3]
        halo_back[group] = send(grad_halo, lambda d, s: (d, s - 2))
    grad_qkv, grad_in = [None] * 2, [None] * 2
    far = jnp.concatenate([plus(far[:half], first), far[half:]], axis=0)
    own_y = jnp.concatenate([own_y[:half], plus(own_y[half:], second)], axis=0)
    down_x, down_y = send(far, across_x), send(own_y, across_y)
    halo_back[1] = after(halo_back[1], mine_gu)
    for group in (0, 1):
        grad_qkv[group], *grad_in[group] = qkv_back(
            group, grad_query[group], grad_kv[group], halo_back[group], cosine, sine, *full_qkv, width
        )
    grad_w_down = lax.optimization_barrier((grad_w_down, halo_back[1]))[0]
    total_down = scatter_z(grad_w_down.reshape(n_z, ff_part, width)).astype(BF)
    out_down = lay_out_rows(d_arg, gather_dp(total_down))

    def attn_grads(slot):
        for_qkv = dot_tn(normed[0], grad_qkv[0][slot]) + dot_tn(normed[1], grad_qkv[1][slot])
        for_qkv = for_qkv.astype(BF).reshape(n_z, 2 * shard, -1)
        if not square:
            return for_qkv
        for_out = [
            fold(grad_out[slot, z * out_rows : (z + 1) * out_rows], lanes) for z in range(n_z)
        ]
        return jnp.concatenate([for_qkv, jnp.stack(for_out)], axis=1)

    grad_attn = sum_core(attn_grads(0), attn_grads(1))
    output = (
        middle + own.astype(F32) + down_x.astype(F32) + down_y.astype(F32)
    ).astype(BF)
    total_attn = along_z(grad_attn)
    total_attn = jnp.sum(total_attn.astype(F32), axis=0).astype(BF)
    mine_attn = swap_rows(total_attn[: 2 * shard]).reshape(2 * shard, -1)
    if square:
        mine_attn = jnp.concatenate([mine_attn, send(total_attn[2 * shard :], turned)], axis=0)
    attn_blocks = gather_dp(mine_attn, out_gate, out_down)
    if square:
        out_query, out_key, out_value, out_out, grad_gain_attn = lay_out_heads(
            d_arg, attn_blocks, w_query, w_key, w_value, gain_attn.astype(F32).reshape(-1, 1), w_out.shape
        )
    else:
        attn_blocks = order_dp(attn_blocks)
        grad_w_out = sum_core(grad_out[0], grad_out[1]).astype(F32)
        out_out = jnp.zeros((2 * n_dp * q_w, width), F32)
        out_out = lax.dynamic_update_slice_in_dim(out_out, grad_w_out, (2 * d + y) * q_w, 0)
        out_out = lax.psum_scatter(out_out, "seq", scatter_dimension=0, tiled=True)
        out_out = lax.psum(out_out.astype(BF), "dp").astype(F32)
        all_qkv = jnp.stack(attn_blocks).astype(F32)
        out_qkv = all_qkv.reshape(2 * n_dp, shard, lanes).transpose(1, 0, 2)
        out_query = out_qkv[..., :q_w].reshape(shard, -1)
        out_key = out_qkv[..., q_w : q_w + k_w].reshape(shard, -1)
        out_value = out_qkv[..., q_w + k_w :].reshape(shard, -1)
        grad_gain_attn = (
            jnp.sum(w_query.astype(F32) * out_query, axis=1)
            + jnp.sum(w_key.astype(F32) * out_key, axis=1)
            + jnp.sum(w_value.astype(F32) * out_value, axis=1)
        ) / gain_attn.astype(F32)

    own = scatter_plane(*grad_in, at_first=(down_x, down_y))
    wide = tokens.astype(F32)
    own_inverse = lax.rsqrt(jnp.mean(wide * wide, axis=-1, keepdims=True) + EPS)
    scaled = own * full_gain_attn
    grad_tokens = (
        grad_middle
        + own_inverse * scaled
        - wide * own_inverse**3 * jnp.mean(scaled * wide, axis=-1, keepdims=True)
    )
    return (
        output,
        grad_tokens,
        grad_gain_attn.reshape(-1),
        out_query,
        out_key,
        out_value,
        out_out,
        grad_gain_mlp.reshape(-1),
        out_gate,
        out_up,
        out_down,
    )


def solution(mesh):
    return jax.shard_map(
        on_device,
        mesh=mesh,
        in_specs=(
            P(("dp", "seq"), None),
            P("dp", None),
            P(("dp", "seq"), None),
            P("seq"),
            P("seq", None),
            P("seq", None),
            P("seq", None),
            P("seq", None),
            P("seq"),
            P("seq", None),
            P("seq", None),
            P("seq", None),
        ),
        out_specs=(
            P(("dp", "seq"), None),
            P(("dp", "seq"), None),
            P("seq"),
            P("seq", None),
            P("seq", None),
            P("seq", None),
            P("seq", None),
            P("seq"),
            P("seq", None),
            P("seq", None),
            P("seq", None),
        ),
        check_vma=False,
    )
```

```python
import functools
import math

import jax
import jax.numpy as jnp
from jax import lax
from jax.experimental import pallas as pl
from jax.experimental.pallas import tpu as pltpu
from jax.sharding import PartitionSpec as P

HEADS = 16
KV_HEADS = 8
HEAD = 96
WINDOW = 512


EPS = 1e-05
THETA = 100000.0
BOTH = ("dp", "seq")
BF = jnp.bfloat16
F32 = jnp.float32


def send(block, target):
    n_dp, n_seq = lax.axis_size("dp"), lax.axis_size("seq")
    route = []
    for d in range(n_dp):
        for s in range(n_seq):
            to = target(d, s)
            if to is not None and 0 <= to[1] < n_seq:
                route.append((d * n_seq + s, to[0] * n_seq + to[1]))
    return lax.ppermute(block, BOTH, route)


def after(value, *others):
    return lax.optimization_barrier((value,) + others)[0]


def across_core(d, s):
    return (d ^ 1, s)


def across_x(d, s):
    return (d ^ 2, s)


def across_y(d, s):
    return (d, s ^ 1)


def gather_plane(block, *meanwhile, for_y=None, came=None):
    half = block.shape[0] // 2
    from_x, from_y = came or (
        send(block, across_x),
        send(block if for_y is None else for_y, across_y),
    )
    if meanwhile:
        from_x, from_y = lax.optimization_barrier((from_x, from_y, *meanwhile))[:2]
    first = send(from_x[:half], across_y)
    second = send(from_y[half:], across_x)
    return [block, from_y, from_x, first, second]


def plus(a, b):
    return (a.astype(F32) + b.astype(F32)).astype(BF)


def scatter_plane(near, far, *meanwhile, at_first=()):
    own, own_y = near
    far, far_a, far_b = far
    half = far_a.shape[0]
    first = send(far_a, across_y)
    second = send(far_b, across_x)
    if at_first:
        first, second = lax.optimization_barrier((first, second, *at_first))[:2]

    far = jnp.concatenate([plus(far[:half], first), far[half:]], axis=0)
    own_y = jnp.concatenate([own_y[:half], plus(own_y[half:], second)], axis=0)
    from_x, from_y = send(far, across_x), send(own_y, across_y)
    if meanwhile:
        from_x, from_y = lax.optimization_barrier((from_x, from_y, *meanwhile))[:2]
    return own.astype(F32) + from_x.astype(F32) + from_y.astype(F32)


def with_core(block):
    return [block, send(block, across_core)]


def sum_core(mine, other):
    return (mine.astype(F32) + send(other.astype(BF), across_core).astype(F32)).astype(BF)


def across_z(k):
    return lambda d, s: (d, s ^ (2 * k))


def along_z(blocks):
    n_seq = lax.axis_size("seq")
    lines = [list(range(y, n_seq, 2)) for y in range(2)]
    return lax.all_to_all(blocks, "seq", 0, 0, axis_index_groups=lines)


def gather_z(block):
    return along_z(jnp.broadcast_to(block[None], (lax.axis_size("seq") // 2,) + block.shape))


def scatter_z(blocks):
    return jnp.sum(along_z(blocks).astype(F32), axis=0)


def pair_y(mine, other):
    y = lax.axis_index("seq") % 2
    return jnp.stack([jnp.where(y == 0, mine, other), jnp.where(y == 0, other, mine)])


def turned(d, s):
    return (s // 2, 2 * d + s % 2)


def fold(rows, wide):
    count, columns = rows.shape
    whole = columns // wide
    parts = [rows[:, i * wide : (i + 1) * wide] for i in range(whole)]
    rest = rows[:, whole * wide :]
    if rest.shape[1]:
        times = wide // rest.shape[1]
        step = count // times
        parts.append(
            jnp.concatenate([rest[i * step : (i + 1) * step] for i in range(times)], axis=1)
        )
    return jnp.concatenate(parts, axis=0)


def unfold(folded, columns):
    total, wide = folded.shape
    count = total * wide // columns
    whole = columns // wide
    parts = [folded[i * count : (i + 1) * count] for i in range(whole)]
    if columns % wide:
        rest, narrow = folded[whole * count :], columns % wide
        parts.append(
            jnp.concatenate(
                [rest[:, i * narrow : (i + 1) * narrow] for i in range(wide // narrow)], axis=0
            )
        )
    return jnp.concatenate(parts, axis=1)


def gather_dp(block, *meanwhile):
    core = send(block, across_core)
    far = send(block, across_x)
    if meanwhile:
        far = lax.optimization_barrier((far, *meanwhile))[0]
    return [block, core, far, send(far, across_core)]


def order_dp(blocks):
    d = lax.axis_index("dp")
    pairs = [
        (jnp.where(d % 2 == 0, a, b), jnp.where(d % 2 == 0, b, a))
        for a, b in (blocks[:2], blocks[2:])
    ]
    low, high = pairs
    return [jnp.where(d < 2, a, b) for a, b in zip(low, high)] + [
        jnp.where(d < 2, b, a) for a, b in zip(low, high)
    ]


def rope_tables(position):
    lane = jnp.arange(128, dtype=jnp.float32) % (HEAD // 2)
    angles = position.astype(jnp.float32)[..., None] * THETA ** (-2.0 * lane / HEAD)
    return jnp.cos(angles), jnp.sin(angles)


SCALE = 0.3
VMEM_BYTES = 60 * 1024 * 1024


def call(kernel, out_shape, flops, moved, **rest):
    return pl.pallas_call(
        kernel,
        out_shape=out_shape,
        compiler_params=pltpu.CompilerParams(vmem_limit_bytes=VMEM_BYTES),
        cost_estimate=pl.CostEstimate(flops=int(flops * SCALE), bytes_accessed=int(moved * SCALE), transcendentals=0),
        **rest,
    )


def shaped(shape, dtype):
    return jax.ShapeDtypeStruct(shape, dtype)


def iota(shape, axis):
    return lax.broadcasted_iota(jnp.int32, shape, axis)


def dot(a, b):
    return jnp.dot(a, b, preferred_element_type=F32)


def dot_nt(a, b):
    return lax.dot_general(a, b, (((1,), (1,)), ((), ())), preferred_element_type=F32)


def dot_tn(a, b):
    return lax.dot_general(a, b, (((0,), (0,)), ((), ())), preferred_element_type=F32)


def spread(packed, heads, base):
    row, column = iota((packed, heads * 128), 0), iota((packed, heads * 128), 1)
    lane = column % 128
    hit = (row == base + HEAD * (column // 128) + lane) & (lane < HEAD)
    return jnp.where(hit, 1.0, 0.0).astype(BF)


def pack(packed, heads, base):
    column, row = iota((heads * 128, packed), 0), iota((heads * 128, packed), 1)
    lane = column % 128
    hit = (row == base + HEAD * (column // 128) + lane) & (lane < HEAD)
    return jnp.where(hit, 1.0, 0.0).astype(BF)


def on_heads(table, heads, packed):
    row, column = iota((128, packed), 0), iota((128, packed), 1)
    place = jnp.where((row == column % HEAD) & (column < heads * HEAD), 1.0, 0.0).astype(BF)
    high = table.astype(BF)
    rest = table - high.astype(F32)
    middle = rest.astype(BF)
    low = (rest - middle.astype(F32)).astype(BF)
    return dot(high, place) + dot(middle, place) + dot(low, place)


def qkv_kernel(*refs):
    parts, refs = refs[:-8], refs[-8:]
    gain, cosine, sine, w_own, w_core, normed, qkv, halo = refs
    tokens, lanes = halo.shape
    x = jnp.concatenate([part[...] for part in parts], axis=0).astype(F32)
    inverse = lax.rsqrt(jnp.mean(x * x, axis=-1, keepdims=True) + EPS)
    low = (x * inverse * gain[...]).astype(BF)
    normed[...] = low
    lane = iota((tokens, lanes), 1)
    first = lane % HEAD < HEAD // 2
    cos_all = on_heads(cosine[...], 3, lanes) + jnp.where(lane >= 3 * HEAD, 1.0, 0.0)
    sin_all = on_heads(sine[...], 3, lanes)
    turned = []
    size = normed.shape[1] // w_own.shape[0]
    for w in (w_own, w_core):
        raw = sum(dot(low[:, z * size : (z + 1) * size], w[z, :size, :]) for z in range(w.shape[0]))
        half = jnp.where(
            first, -pltpu.roll(raw, lanes - HEAD // 2, 1), pltpu.roll(raw, HEAD // 2, 1)
        )
        turned.append(raw * cos_all + half * sin_all)
    qkv[0] = turned[0].astype(BF)
    qkv[1] = turned[1].astype(BF)
    halo[...] = jnp.where(
        lane < lanes // 2, pltpu.roll(turned[1], lanes // 2, 1), turned[0]
    ).astype(BF)


def project(group, parts, gain, cosine, sine, w_own, w_core):
    tokens = sum(part.shape[0] for part in parts)
    width, lanes = gain.shape[1], w_own.shape[2]

    def whole(array):
        return pl.BlockSpec(array.shape, lambda i: (0,) * array.ndim)

    table = pl.BlockSpec((tokens, 128), lambda i: (group, 0))
    outs = [shaped((tokens, width), BF), shaped((2, tokens, lanes), BF), shaped((tokens, lanes), BF)]
    return call(
        qkv_kernel,
        outs,
        flops=4 * tokens * width * lanes,
        moved=6 * 10**6,
        grid=(1,),
        in_specs=[whole(part) for part in parts] + [whole(gain), table, table, whole(w_own), whole(w_core)],
        out_specs=[whole(out) for out in outs],
    )(*parts, gain, cosine, sine, w_own, w_core)


def visible(seg_query, seg_key, a, rows):
    shape = (rows, 3 * rows)
    row, column = iota(shape, 0), iota(shape, 1)
    same = seg_query[0, a] == jnp.concatenate([seg_key[0, a + i] for i in range(3)], axis=1)
    allowed = (column > row) & (column <= row + 2 * rows) & same
    return jnp.concatenate([allowed, allowed], axis=0)


def heads_of(y, slot, qkv, halo, rows):
    lanes = qkv.shape[-1]

    def at(a):
        return pl.ds(pl.multiple_of((a ^ y) * rows, rows), rows)

    before = spread(lanes, 2, (1 - slot) * (lanes // 2))
    here = spread(lanes, 4, 0)
    local = [dot(qkv[0, at(a), :], here).astype(BF) for a in range(2)]
    key_value = [dot(halo[at(a), :], before).astype(BF) for a in range(2)]
    key_value += [part[:, 256:] for part in local]
    query = [jnp.concatenate([part[:, :128], part[:, 128:256]], axis=0) for part in local]
    return at, query, key_value


def padded_out(w_out):
    rows = w_out.shape[1]
    return dot(pack(rows, 2, 0), w_out[0]).astype(BF)


def attend_kernel(y_ref, qkv, halo, seg_query, seg_key, w_out, *refs):
    *partial, context, logsum, total = refs
    slot = pl.program_id(0)
    rows = qkv.shape[1] // 2
    at, query, key_value = heads_of(y_ref[0], slot, qkv, halo, rows)
    w = padded_out(w_out)
    for a in range(2):
        kv = jnp.concatenate(key_value[a : a + 3], axis=0)
        scores = dot_nt(query[a], kv[:, :128]) * (1.0 / math.sqrt(HEAD))
        scores = jnp.where(visible(seg_query, seg_key, a, rows), scores, -1e30)
        peak = jnp.max(scores, axis=-1, keepdims=True)
        exponent = jnp.exp(scores - peak)
        row_total = jnp.sum(exponent, axis=-1, keepdims=True)
        probs = (exponent * (1.0 / row_total)).astype(BF)
        logsum[0, a] = peak + jnp.log(row_total)
        seen = dot(probs, kv[:, 128:]).astype(BF)
        seen = jnp.concatenate([seen[:rows], seen[rows:]], axis=1)
        context[0, at(a), :] = seen
        product = dot(seen, w)

        @pl.when(slot == 0)
        def _():
            total[at(a), :] = product

        @pl.when(slot == 1)
        def _():
            total[at(a), :] += product

    @pl.when(slot == 1)
    def _():
        begin = 0
        for out in partial:
            out[...] = total[begin : begin + out.shape[0], :].astype(BF)
            begin += out.shape[0]


def attend(y, group, qkv, halo, seg_query, seg_key, w_out):
    slots, reach, lanes = qkv.shape
    rows, width = reach // 2, w_out.shape[-1]
    sizes = (rows, rows // 2, rows // 2) if group else (rows, rows)
    return call(
        attend_kernel,
        [shaped((size, width), BF) for size in sizes]
        + [
            shaped((slots, reach, 256), BF),
            shaped((slots, 2, reach, 1), F32),
        ],
        flops=5 * 10**9,
        moved=7 * 10**6,
        grid_spec=pltpu.PrefetchScalarGridSpec(
            num_scalar_prefetch=1,
            grid=(slots,),
            in_specs=[
                pl.BlockSpec((1, reach, lanes), lambda s, y: (s, 0, 0)),
                pl.BlockSpec((reach, lanes), lambda s, y: (0, 0)),
                pl.BlockSpec((1, 2, rows, 1), lambda s, y: (group, 0, 0, 0)),
                pl.BlockSpec((1, 4, 1, rows), lambda s, y: (group, 0, 0, 0)),
                pl.BlockSpec((1,) + w_out.shape[1:], lambda s, y: (s, 0, 0)),
            ],
            out_specs=[pl.BlockSpec((size, width), lambda s, y: (0, 0)) for size in sizes]
            + [
                pl.BlockSpec((1, reach, 256), lambda s, y: (s, 0, 0)),
                pl.BlockSpec((1, 2, reach, 1), lambda s, y: (s, 0, 0, 0)),
            ],
            scratch_shapes=[pltpu.VMEM((reach, width), F32)],
        ),
    )(y, qkv, halo, seg_query, seg_key, w_out)


def load_blocks(parts, whole, sems):
    copies, at = [], 0
    for i, part in enumerate(parts):
        copies.append(
            pltpu.make_async_copy(part, whole.at[pl.ds(at, part.shape[0])], sems.at[i])
        )
        at += part.shape[0]
    for copy in copies:
        copy.start()
    return copies


def weight_copies(me, weights, gu, down, sems):
    n_z, wide = len(weights), weights[0].shape[1]
    width = down.shape[1]
    step, ff_part = width // n_z, down.shape[0] // n_z
    half = ff_part * (width - wide) // wide
    first, second = [], []
    for r, block in enumerate(weights):
        z = me ^ r
        row = pl.multiple_of(z * ff_part, ff_part)
        if gu is not None:
            first.append(
                pltpu.make_async_copy(
                    block.at[pl.ds(0, step)],
                    gu.at[pl.ds(pl.multiple_of(z * step, step), step)],
                    sems.at[0, r],
                )
            )
        second.append(
            pltpu.make_async_copy(
                block.at[pl.ds(step, ff_part)],
                down.at[pl.ds(row, ff_part), pl.ds(0, wide)],
                sems.at[1, r],
            )
        )
        for i in range(2):
            second.append(
                pltpu.make_async_copy(
                    block.at[pl.ds(step + ff_part, half), pl.ds(i * wide // 2, wide // 2)],
                    down.at[pl.ds(row + i * half, half), pl.ds(wide, width - wide)],
                    sems.at[2 + i, r],
                )
            )
    return first + second


def mlp_kernel(n_z, z_ref, *refs):
    n_parts, d_parts, refs = refs[:5], refs[5:10], refs[10:]
    w_own, w_core, refs = refs[:n_z], refs[n_z : 2 * n_z], refs[2 * n_z :]
    hidden, grad_gu, *grad_in, normed_out, upstream_out = refs[:9]
    normed, upstream, gu, down, total, n_sems, d_sems, w_sems, out_sems = refs[9:]
    slot = pl.program_id(0)
    ff = gu.shape[2] // 2
    core_copies = weight_copies(z_ref[0], w_core, gu.at[1], down.at[1], w_sems.at[1])
    kept = [
        pltpu.make_async_copy(normed, normed_out, out_sems.at[0]),
        pltpu.make_async_copy(upstream, upstream_out, out_sems.at[1]),
    ]

    @pl.when(slot == 0)
    def _():
        copies = load_blocks(n_parts, normed, n_sems)
        copies += weight_copies(z_ref[0], w_own, gu.at[0], down.at[0], w_sems.at[0])
        for copy in copies[5:]:
            copy.start()
        copies += load_blocks(d_parts, upstream, d_sems)
        for copy in core_copies:
            copy.start()
        for copy in copies:
            copy.wait()
        for copy in kept:
            copy.start()

    @pl.when(slot == 1)
    def _():
        for copy in core_copies:
            copy.wait()

    n, dy = normed[...], upstream[...]
    gate = dot(n, gu[slot, :, :ff])
    up = dot(n, gu[slot, :, ff:])
    dh = dot_nt(dy, down[slot])
    sigmoid = jax.nn.sigmoid(gate)
    silu = gate * sigmoid
    hidden[0] = (silu * up).astype(BF)
    d_gate = (dh * up * sigmoid * (1.0 + gate * (1.0 - sigmoid))).astype(BF)
    d_up = (dh * silu).astype(BF)
    grad_gu[0, :, :ff] = d_gate
    grad_gu[0, :, ff:] = d_up
    part = dot_nt(d_gate, gu[slot, :, :ff]) + dot_nt(d_up, gu[slot, :, ff:])

    @pl.when(slot == 0)
    def _():
        total[...] = part

    @pl.when(slot == 1)
    def _():
        whole = (total[...] + part).astype(BF)
        begin = 0
        for out in grad_in:
            out[...] = whole[begin : begin + out.shape[0]]
            begin += out.shape[0]
        for copy in kept:
            copy.wait()


def feed_forward(z, normed, upstream, w_own, w_core):
    rows, width = normed[0].shape
    n_z, wide = len(w_own), w_own[0].shape[1]
    tokens, ff = 4 * rows, wide // 2
    anywhere = pl.BlockSpec(memory_space=pl.ANY)
    block = pl.BlockSpec((rows, width), lambda s, z: (0, 0))
    half = pl.BlockSpec((rows // 2, width), lambda s, z: (0, 0))
    return call(
        functools.partial(mlp_kernel, n_z),
        [
            shaped((2, tokens, ff), BF),
            shaped((2, tokens, wide), BF),
            shaped((rows, width), BF),
            shaped((rows, width), BF),
            shaped((rows, width), BF),
            shaped((rows // 2, width), BF),
            shaped((rows // 2, width), BF),
            shaped((tokens, width), BF),
            shaped((tokens, width), BF),
        ],
        flops=10 * tokens * width * wide,
        moved=25 * 10**6,
        grid_spec=pltpu.PrefetchScalarGridSpec(
            num_scalar_prefetch=1,
            grid=(2,),
            in_specs=[anywhere] * (10 + 2 * n_z),
            out_specs=[
                pl.BlockSpec((1, tokens, ff), lambda s, z: (s, 0, 0)),
                pl.BlockSpec((1, tokens, wide), lambda s, z: (s, 0, 0)),
                block,
                block,
                block,
                half,
                half,
                anywhere,
                anywhere,
            ],
            scratch_shapes=[
                pltpu.VMEM((tokens, width), BF),
                pltpu.VMEM((tokens, width), BF),
                pltpu.VMEM((2, width, wide), BF),
                pltpu.VMEM((2, ff, width), BF),
                pltpu.VMEM((tokens, width), F32),
                pltpu.SemaphoreType.DMA((5,)),
                pltpu.SemaphoreType.DMA((5,)),
                pltpu.SemaphoreType.DMA((2, 4, n_z)),
                pltpu.SemaphoreType.DMA((2,)),
            ],
        ),
    )(z, *normed, *upstream, *w_own, *w_core)


def down_kernel(n_z, z_ref, hidden, *refs):
    w_own, w_core, refs = refs[:n_z], refs[n_z : 2 * n_z], refs[2 * n_z :]
    *outs, down, total, sems = refs
    slot = pl.program_id(0)
    core_copies = weight_copies(z_ref[0], w_core, None, down.at[1], sems.at[1])

    @pl.when(slot == 0)
    def _():
        copies = weight_copies(z_ref[0], w_own, None, down.at[0], sems.at[0])
        for copy in copies + core_copies:
            copy.start()
        for copy in copies:
            copy.wait()

    @pl.when(slot == 1)
    def _():
        for copy in core_copies:
            copy.wait()

    part = dot(hidden[0], down[slot])

    @pl.when(slot == 0)
    def _():
        total[...] = part

    @pl.when(slot == 1)
    def _():
        whole, begin = (total[...] + part).astype(BF), 0
        for out in outs:
            out[...] = whole[begin : begin + out.shape[0]]
            begin += out.shape[0]


def down_project(z, hidden, w_own, w_core, width):
    _, tokens, ff = hidden.shape
    n_z, rows = len(w_own), tokens // 4
    sizes = (rows, rows, rows, rows // 2, rows // 2)
    return call(
        functools.partial(down_kernel, n_z),
        [shaped((size, width), BF) for size in sizes],
        flops=4 * tokens * width * ff,
        moved=8 * 10**6,
        grid_spec=pltpu.PrefetchScalarGridSpec(
            num_scalar_prefetch=1,
            grid=(2,),
            in_specs=[pl.BlockSpec((1, tokens, ff), lambda s, z: (s, 0, 0))]
            + [pl.BlockSpec(memory_space=pl.ANY)] * (2 * n_z),
            out_specs=[pl.BlockSpec((size, width), lambda s, z: (0, 0)) for size in sizes],
            scratch_shapes=[
                pltpu.VMEM((2, ff, width), BF),
                pltpu.VMEM((tokens, width), F32),
                pltpu.SemaphoreType.DMA((2, 4, n_z)),
            ],
        ),
    )(z, hidden, *w_own, *w_core)


def grads_kernel(left, right, *rest):
    grad = dot_tn(left[...].reshape(left.shape[-2:]), right[...].reshape(right.shape[-2:]))
    if len(rest) == 2:
        grad = grad + rest[0][...].astype(F32)
    rest[-1][...] = grad.astype(BF)


def weight_grads(left, left_slot, right, right_slot, steps, *other):
    tokens, rows, columns = left.shape[-2], left.shape[-1], right.shape[-1]
    block = pl.BlockSpec((rows, columns // steps), lambda i: (0, i))

    def part(array, slot, blocks):
        if array.ndim == 2:
            return pl.BlockSpec((tokens, array.shape[1] // blocks), lambda i: (0, i if blocks > 1 else 0))
        return pl.BlockSpec(
            (1, tokens, array.shape[2] // blocks), lambda i: (slot, 0, i if blocks > 1 else 0)
        )

    return call(
        grads_kernel,
        shaped((rows, columns), BF),
        flops=2 * tokens * rows * columns,
        moved=10 * 10**6,
        grid=(steps,),
        in_specs=[part(left, left_slot, 1), part(right, right_slot, steps)] + [block] * len(other),
        out_specs=block,
    )(left, right, *other)


def cut_kernel(place_ref, w_gate, w_up, mine, other):
    ff = mine.shape[1] // 2
    for to, y in ((mine, place_ref[1]), (other, 1 - place_ref[1])):
        for i, w in enumerate((w_gate, w_up)):
            for z in range(ff // 128):
                at = pl.multiple_of(((2 * z + y) * 4 + place_ref[0]) * 128, 128)
                begin = i * ff + z * 128
                to[:, begin : begin + 128] = w[:, pl.ds(at, 128)]


def cut_columns(place, w_gate, w_up, columns):
    vmem = pl.BlockSpec(memory_space=pltpu.VMEM)
    return call(
        cut_kernel,
        [shaped((w_gate.shape[0], columns), BF)] * 2,
        flops=10**6,
        moved=8 * 10**6,
        in_specs=[pl.BlockSpec(memory_space=pltpu.SMEM)] + [vmem] * 2,
        out_specs=[vmem] * 2,
    )(place, w_gate, w_up)


def place_kernel(z_ref, own, core, out):
    rows = own.shape[1]
    for slot, pieces in enumerate((own, core)):
        for k in range(own.shape[0]):
            to = pl.multiple_of((z_ref[0] ^ k) * rows, rows)
            out[slot, pl.ds(to, rows), :] = pieces[k]


def place(z, own, core):
    n, rows, columns = own.shape
    vmem = pl.BlockSpec(memory_space=pltpu.VMEM)
    return call(
        place_kernel,
        shaped((2, n * rows, columns), BF),
        flops=10**6,
        moved=8 * n * rows * columns,
        in_specs=[pl.BlockSpec(memory_space=pltpu.SMEM)] + [vmem] * 2,
        out_specs=vmem,
    )(z, own, core)


def turn_back(values, cosine, sine):
    lane = iota(values.shape, 1)
    across = values * sine
    moved = jnp.where(
        lane < HEAD // 2,
        pltpu.roll(across, 128 - HEAD // 2, 1),
        jnp.where(lane < HEAD, -pltpu.roll(across, HEAD // 2, 1), 0.0),
    )
    return values * cosine + moved


def attend_back_kernel(n_parts, *refs):
    y_ref, qkv, halo, seg_query, seg_key, w_out, context, logsum, cosine, sine = refs[:10]
    parts, rest = refs[10 : 10 + n_parts], refs[10 + n_parts :]
    before = rest[0] if len(rest) == 9 else None
    grad_query, grad_kv, grad_halo, grad_out, up, kv_total, out_total, sems = rest[-8:]
    slot = pl.program_id(0)
    reach = qkv.shape[1]
    rows = reach // 2
    factor = 1.0 / math.sqrt(HEAD)

    @pl.when(slot == 0)
    def _():
        for copy in load_blocks(parts, up, sems):
            copy.wait()

    at, query, key_value = heads_of(y_ref[0], slot, qkv, halo, rows)
    w = padded_out(w_out)
    kv_total[...] = jnp.zeros_like(kv_total)
    out_part = None
    for a in range(2):
        dy = up[at(a), :]
        d_context = dot_nt(dy, w).astype(BF)
        part = dot_tn(context[0, at(a), :], dy)
        out_part = part if out_part is None else out_part + part
        d_seen = jnp.concatenate([d_context[:, :128], d_context[:, 128:]], axis=0)
        kv = jnp.concatenate(key_value[a : a + 3], axis=0)
        key, value = kv[:, :128], kv[:, 128:]
        scores = dot_nt(query[a], key) * factor
        probs = jnp.exp(
            jnp.where(visible(seg_query, seg_key, a, rows), scores - logsum[0, a], -1e30)
        )
        d_probs = dot_nt(d_seen, value)
        delta = jnp.sum(probs * d_probs, axis=-1, keepdims=True)
        d_scores = (probs * (d_probs - delta)).astype(BF)
        d_query = dot(d_scores, key) * factor
        cos_a, sin_a = cosine[at(a), :], sine[at(a), :]
        turned = jnp.concatenate(
            [turn_back(d_query[:rows], cos_a, sin_a), turn_back(d_query[rows:], cos_a, sin_a)],
            axis=1,
        ).astype(BF)
        grad_query[0, at(a), :] = dot(turned, pack(qkv.shape[-1], 2, 0)).astype(BF)
        seen = slice(a * rows, (a + 3) * rows)
        kv_total[seen, :128] += dot_tn(d_scores, query[a]) * factor
        kv_total[seen, 128:] += dot_tn(probs.astype(BF), d_seen)
    back = pack(qkv.shape[-1], 2, (1 - slot) * (qkv.shape[-1] // 2))
    for a in range(2):
        grad_kv[0, at(a), :] = kv_total[(a + 2) * rows : (a + 3) * rows, :]
        placed = dot(kv_total[a * rows : (a + 1) * rows, :].astype(BF), back).astype(BF)

        @pl.when(slot == 0)
        def _():
            grad_halo[at(a), :] = placed

        @pl.when(slot == 1)
        def _():
            grad_halo[at(a), :] += placed

    out_total[...] = out_part.astype(BF)
    part = dot(spread(w_out.shape[1], 2, 0), out_total[...])
    if before is not None:
        part = part + before[0].astype(F32)
    grad_out[0] = part.astype(BF)


def attend_back(y, group, qkv, halo, seg_query, seg_key, w_out, context, logsum, cosine, sine, upstream, before=()):
    slots, reach, lanes = qkv.shape
    rows, width = reach // 2, w_out.shape[-1]
    weight = pl.BlockSpec((1,) + w_out.shape[1:], lambda s, y: (s, 0, 0))
    return call(
        functools.partial(attend_back_kernel, len(upstream)),
        [
            shaped((slots, reach, lanes), BF),
            shaped((slots, reach, 256), F32),
            shaped((reach, lanes), BF),
            shaped(w_out.shape, BF),
        ],
        flops=12 * 10**9,
        moved=10 * 10**6,
        grid_spec=pltpu.PrefetchScalarGridSpec(
            num_scalar_prefetch=1,
            grid=(slots,),
            in_specs=[
                pl.BlockSpec((1, reach, lanes), lambda s, y: (s, 0, 0)),
                pl.BlockSpec((reach, lanes), lambda s, y: (0, 0)),
                pl.BlockSpec((1, 2, rows, 1), lambda s, y: (group, 0, 0, 0)),
                pl.BlockSpec((1, 4, 1, rows), lambda s, y: (group, 0, 0, 0)),
                weight,
                pl.BlockSpec((1, reach, 256), lambda s, y: (s, 0, 0)),
                pl.BlockSpec((1, 2, reach, 1), lambda s, y: (s, 0, 0, 0)),
                pl.BlockSpec((reach, 128), lambda s, y: (group, 0)),
                pl.BlockSpec((reach, 128), lambda s, y: (group, 0)),
            ]
            + [pl.BlockSpec(memory_space=pl.ANY)] * len(upstream)
            + [weight] * len(before),
            out_specs=[
                pl.BlockSpec((1, reach, lanes), lambda s, y: (s, 0, 0)),
                pl.BlockSpec((1, reach, 256), lambda s, y: (s, 0, 0)),
                pl.BlockSpec((reach, lanes), lambda s, y: (0, 0)),
                weight,
            ],
            scratch_shapes=[
                pltpu.VMEM((reach, width), BF),
                pltpu.VMEM((2 * reach, 256), F32),
                pltpu.VMEM((256, width), BF),
                pltpu.SemaphoreType.DMA((len(upstream),)),
            ],
        ),
    )(y, qkv, halo, seg_query, seg_key, w_out, context, logsum, cosine, sine, *upstream, *before)


def qkv_back_kernel(grad_query, grad_kv, grad_halo, cosine, sine, w_own, w_core, grad_qkv, *grad_in):
    lanes = grad_halo.shape[-1]
    total = None
    place = pack(lanes, 2, lanes // 2)
    size = grad_in[0].shape[1] // w_own.shape[0]
    for slot, w in enumerate((w_own, w_core)):
        kv = grad_kv[slot] + dot(grad_halo[...], spread(lanes, 2, (1 - slot) * (lanes // 2)))
        key = turn_back(kv[:, :128], cosine[...], sine[...])
        kv = jnp.concatenate([key, kv[:, 128:]], axis=1).astype(BF)
        both = grad_query[slot] + dot(kv, place).astype(BF)
        grad_qkv[slot] = both
        part = [dot_nt(both, w[z, :size, :]) for z in range(w.shape[0])]
        part = jnp.concatenate(part, axis=1)
        total = part if total is None else total + part
    whole, begin = total.astype(BF), 0
    for out in grad_in:
        out[...] = whole[begin : begin + out.shape[0]]
        begin += out.shape[0]


def qkv_back(group, grad_query, grad_kv, grad_halo, cosine, sine, w_own, w_core, width):
    slots, tokens, lanes = grad_query.shape
    rows = tokens // 2
    sizes = (rows, rows // 2, rows // 2) if group else (rows, rows)
    table = pl.BlockSpec((tokens, 128), lambda i: (group, 0))

    def whole(array):
        return pl.BlockSpec(array.shape, lambda i: (0,) * array.ndim)

    outs = [shaped((slots, tokens, lanes), BF)] + [shaped((size, width), BF) for size in sizes]
    return call(
        qkv_back_kernel,
        outs,
        flops=2 * slots * tokens * width * lanes,
        moved=6 * 10**6,
        grid=(1,),
        in_specs=[whole(grad_query), whole(grad_kv), whole(grad_halo), table, table]
        + [whole(w_own), whole(w_core)],
        out_specs=[whole(out) for out in outs],
    )(grad_query, grad_kv, grad_halo, cosine, sine, w_own, w_core)


def lay_out_kernel(d_ref, *refs):
    b0, b1, b2, b3, w_gate, w_up, gain, out_gate, out_up, grad_gain = refs
    ff = b0.shape[2] // 2
    for k, block in enumerate((b0, b1, b2, b3)):
        for y in range(2):
            for z in range(ff // 128):
                to = pl.multiple_of(((2 * z + y) * 4 + (d_ref[0] ^ k)) * 128, 128)
                out_gate[:, pl.ds(to, 128)] = block[y, :, z * 128 : (z + 1) * 128].astype(F32)
                out_up[:, pl.ds(to, 128)] = block[y, :, ff + z * 128 : ff + (z + 1) * 128].astype(F32)
    weighted = w_gate[...].astype(F32) * out_gate[...] + w_up[...].astype(F32) * out_up[...]
    grad_gain[...] = jnp.sum(weighted, axis=-1, keepdims=True) / gain[...]


def lay_out(d, blocks, w_gate, w_up, gain):
    shard, ff = w_gate.shape
    rows = 64
    blocks = [block.reshape(2, shard, block.shape[1]) for block in blocks]
    part = pl.BlockSpec((2, rows, blocks[0].shape[2]), lambda i, d: (0, i, 0))
    whole = pl.BlockSpec((rows, ff), lambda i, d: (i, 0))
    column = pl.BlockSpec((rows, 1), lambda i, d: (i, 0))
    return call(
        lay_out_kernel,
        [shaped((shard, ff), F32), shaped((shard, ff), F32), shaped((shard, 1), F32)],
        flops=6 * shard * ff,
        moved=16 * shard * ff,
        grid_spec=pltpu.PrefetchScalarGridSpec(
            num_scalar_prefetch=1,
            grid=(shard // rows,),
            in_specs=[part] * 4 + [whole, whole, column],
            out_specs=[whole, whole, column],
        ),
    )(d, *blocks, w_gate, w_up, gain)


def lay_out_rows_kernel(d_ref, b0, b1, b2, b3, out):
    rows = b0.shape[0]
    for k, block in enumerate((b0, b1, b2, b3)):
        at = pl.ds(pl.multiple_of((d_ref[0] ^ k) * rows, rows), rows)
        out[at, :] = block[...].astype(F32)


def lay_out_rows(d, blocks):
    rows, width = blocks[0].shape
    vmem = pl.BlockSpec(memory_space=pltpu.VMEM)
    return call(
        lay_out_rows_kernel,
        shaped((4 * rows, width), F32),
        flops=rows * width,
        moved=24 * rows * width,
        in_specs=[pl.BlockSpec(memory_space=pltpu.SMEM)] + [vmem] * 4,
        out_specs=vmem,
    )(d, *blocks)


def lay_out_heads_kernel(d_ref, *refs):
    blocks, (w_query, w_key, w_value, gain) = refs[:4], refs[4:8]
    out_query, out_key, out_value, out_out, grad_gain, ordered = refs[8:]
    shard, lanes = w_query.shape[0], blocks[0].shape[1]
    count = out_out.shape[0] // 4
    for k, block in enumerate(blocks):
        to = d_ref[0] ^ k
        ordered[to] = block[: 2 * shard, :]
        at = pl.ds(pl.multiple_of(to * count, count), count)
        for i in range(4):
            out_out[at, i * lanes : (i + 1) * lanes] = block[
                2 * shard + i * count : 2 * shard + (i + 1) * count, :
            ].astype(F32)
    row, column = iota((lanes, lanes), 0), iota((lanes, lanes), 1)

    def place(begin, count, to):
        hit = (column - to == row - begin) & (row >= begin) & (row < begin + count)
        return jnp.where(hit, 1.0, 0.0).astype(BF)

    def block_of(t):
        return ordered[t // 2, (t % 2) * shard : (t % 2 + 1) * shard, :]

    total = None
    for begin, count, out, w in (
        (0, 2 * HEAD, out_query, w_query),
        (2 * HEAD, HEAD, out_key, w_key),
        (3 * HEAD, HEAD, out_value, w_value),
    ):
        heads = lanes // count
        places = [place(begin, count, i * count) for i in range(heads)]
        for j in range(KV_HEADS // heads):
            piece = None
            for i in range(heads):
                part = dot(block_of(j * heads + i), places[i])
                piece = part if piece is None else piece + part
            at = slice(j * lanes, (j + 1) * lanes)
            out[:, at] = piece
            part = jnp.sum(w[:, at].astype(F32) * piece, axis=-1, keepdims=True)
            total = part if total is None else total + part
    grad_gain[...] = total / gain[...]


def lay_out_heads(d, blocks, w_query, w_key, w_value, gain, out_shape):
    shard = w_query.shape[0]
    vmem = pl.BlockSpec(memory_space=pltpu.VMEM)
    return call(
        lay_out_heads_kernel,
        [
            shaped(w_query.shape, F32),
            shaped(w_key.shape, F32),
            shaped(w_value.shape, F32),
            shaped(out_shape, F32),
            shaped((shard, 1), F32),
        ],
        flops=4 * 10**9,
        moved=8 * 10**6,
        in_specs=[pl.BlockSpec(memory_space=pltpu.SMEM)] + [vmem] * 8,
        out_specs=[vmem] * 5,
        scratch_shapes=[pltpu.VMEM((4, 2 * shard, blocks[0].shape[1]), BF)],
    )(d, *blocks, w_query, w_key, w_value, gain)


def layout_rows(lengths, index):
    ends = jnp.cumsum(lengths, axis=1)
    before = index[None, :, None] >= ends[:, None, :]
    segment = jnp.sum(before.astype(jnp.int32), axis=2)
    offset = jnp.sum(jnp.where(before, lengths[:, None, :], 0), axis=2)
    segment = jnp.where(segment < lengths.shape[1], segment, -1)
    segment = jnp.where(index[None, :] < 0, -3, segment)
    return (segment, index[None, :] - offset)


def on_device(
    tokens,
    lengths,
    cotangent,
    gain_attn,
    w_query,
    w_key,
    w_value,
    w_out,
    gain_mlp,
    w_gate,
    w_up,
    w_down,
):
    n_dp, n_seq = lax.axis_size("dp"), lax.axis_size("seq")
    d, me = lax.axis_index("dp"), lax.axis_index("seq")
    y, n_z = me % 2, n_seq // 2
    rows, width = tokens.shape
    reach = 2 * rows
    assert WINDOW <= reach and KV_HEADS == 2 * n_dp
    groups = HEADS // KV_HEADS
    q_w, k_w = groups * HEAD, HEAD
    shard = w_query.shape[0]
    ff_shard = w_down.shape[0]
    ff_part = ff_shard // n_dp

    def head_columns(j):
        t = 2 * d + j
        gains = jnp.zeros((16, q_w + 2 * k_w), BF)
        gains = gains.at[0, :shard].set(gain_attn).at[1, :shard].set(gain_mlp)
        columns = jnp.concatenate(
            [
                lax.dynamic_slice_in_dim(w_query, t * q_w, q_w, 1),
                lax.dynamic_slice_in_dim(w_key, t * k_w, k_w, 1),
                lax.dynamic_slice_in_dim(w_value, t * k_w, k_w, 1),
            ],
            axis=1,
        )
        return jnp.concatenate([columns, gains], axis=0)

    def ff_columns(j):
        parts = [
            lax.dynamic_slice_in_dim(w, ((2 * z + j) * n_dp + d) * ff_part, ff_part, 1)
            for w in (gate_in, up_in)
            for z in range(n_z)
        ]
        return jnp.concatenate(parts, axis=1)

    lanes = q_w + 2 * k_w
    square = n_seq == 2 * n_dp
    d_arg = jnp.reshape(d, (1,)).astype(jnp.int32)
    z_arg = jnp.reshape(me // 2, (1,)).astype(jnp.int32)

    lens_far = send(lengths, across_x)
    qkv_from_y = send(head_columns(1 - y), across_y)
    tokens_all = gather_plane(tokens, for_y=after(tokens, qkv_from_y))
    low, high = pair_y(head_columns(y), qkv_from_y)
    gain_rows = jnp.concatenate([low[shard:, :shard], high[shard:, :shard]], axis=1)
    gain_rows = jnp.pad(gain_rows, ((0, 0), (0, lanes - 2 * shard)))
    part_qkv = jnp.concatenate([low[:shard], high[:shard], gain_rows], axis=0)
    own_qkv = gather_z(part_qkv)
    lens = jnp.concatenate([lengths, after(lens_far, tokens_all[3])], axis=0)

    first_row = (me // 2) * reach
    steps = jnp.arange(reach, dtype=jnp.int32)
    order = jnp.arange(2, dtype=jnp.int32)[:, None] ^ y
    _, position = layout_rows(lens, first_row + (order * rows + steps[None, :rows]).reshape(-1))
    cosine, sine = rope_tables(position.reshape(-1))
    key_index = first_row - reach + jnp.arange(2 * reach, dtype=jnp.int32)
    segment, _ = layout_rows(lens, key_index)
    segment = jnp.where(segment == -1, -8 - key_index[None, :], segment)
    seg_key = segment.reshape(2, 4, 1, rows)
    seg_query = segment[:, reach:].reshape(2, 2, rows, 1)
    y_arg = jnp.reshape(y, (1,)).astype(jnp.int32)

    gate_in, up_in = lax.optimization_barrier((w_gate, w_up, qkv_from_y))[:2]
    if ff_part % 128 == 0:
        here = jnp.stack([d, y]).astype(jnp.int32)
        mine_ff, other_ff = cut_columns(here, gate_in, up_in, 2 * n_z * ff_part)
    else:
        mine_ff, other_ff = ff_columns(y), ff_columns(1 - y)
    other_ff = send(after(other_ff, tokens_all[1]), across_y)
    part_mlp = jnp.concatenate(
        [
            pair_y(mine_ff, other_ff).reshape(2 * shard, -1),
            fold(lax.dynamic_slice_in_dim(w_down, d * ff_part, ff_part, 0), 2 * n_z * ff_part),
        ],
        axis=0,
    )
    early = ()
    if square:
        out_rows = shard // n_dp
        part_out = lax.dynamic_slice_in_dim(w_out, d * out_rows, out_rows, 0)
        part_out = send(after(part_out, part_qkv), turned)
        early = (part_out,)
    own_qkv = lax.optimization_barrier((own_qkv, part_mlp, cosine, *early, *tokens_all))[0]
    core_qkv = send(own_qkv, across_core)
    if square:
        out_pieces = [send(after(part_out, own_qkv), across_z(k)) for k in (1, 2, 3)]
    else:
        own_out = lax.all_gather(w_out, "seq", axis=0, tiled=True)
        own_out = lax.dynamic_slice_in_dim(own_out, (2 * d + y) * q_w, q_w, 0)
    full_qkv = [own_qkv, core_qkv]
    if not square:
        full_qkv = [part[:, : 2 * shard].reshape(1, width, lanes) for part in full_qkv]
    gains = own_qkv[:, 2 * shard : 2 * shard + 2, : 2 * shard]
    full_gain_attn = gains[:, 0].reshape(1, -1).astype(F32)
    full_gain_mlp = gains[:, 1].reshape(1, -1).astype(F32)

    groups_of = ((0, 1), (2, 3, 4))

    def parts_of(pieces, group):
        return [pieces[i] for i in groups_of[group]]

    normed, qkv, halo, halo_in = [None] * 2, [None] * 2, [None] * 2, [None] * 2
    for group in (1, 0):
        normed[group], qkv[group], halo[group] = project(
            group, parts_of(tokens_all, group), full_gain_attn, cosine, sine, *full_qkv
        )
        halo_in[group] = send(halo[group], lambda d, s: (d, s + 2))
    if square:
        out_pieces = lax.optimization_barrier((*out_pieces, *halo))[:3]
        own_out = jnp.stack([part_out, *out_pieces])
        full_out = place(z_arg, own_out, send(own_out, across_core))
    else:
        full_out = jnp.stack(with_core(own_out))
    part_ready = lax.optimization_barrier((part_mlp, *halo_in))[0]
    if square:
        both = send(part_ready, across_z(2))
        mlp_near = send(part_ready, across_z(1))
    else:
        blocks = gather_z(part_ready)
        down_rows = jnp.concatenate([unfold(blocks[z, 2 * shard :], width) for z in range(n_z)], axis=0)
        own_mlp = [
            jnp.concatenate(
                [blocks[:, : 2 * shard].reshape(width, -1), fold(down_rows, 2 * n_z * ff_part)], axis=0
            )
        ]
    cotangent_in = after(cotangent, *tokens_all)
    came = (send(cotangent_in, across_x), send(cotangent_in, across_y))
    upstream_all = gather_plane(cotangent, *halo, came=came)
    halo_first = lax.optimization_barrier((halo_in[0], *upstream_all))[0]
    partial, context, logsum = [None] * 2, [None] * 2, [None] * 2
    for group in (1, 0):
        *partial[group], context[group], logsum[group] = attend(
            y_arg, group, qkv[group], halo_in[1] if group else halo_first, seg_query, seg_key, full_out
        )
    arrived = (both, mlp_near) if square else ()
    middle = tokens.astype(F32) + scatter_plane(*partial, *arrived)


    inverse_mlp = lax.rsqrt(jnp.mean(middle * middle, axis=-1, keepdims=True) + EPS)
    normed_mlp_own = (middle * inverse_mlp * full_gain_mlp).astype(BF)
    if square:
        mlp_far = both
        own_mlp = [part_mlp, mlp_near, mlp_far, send(mlp_far, across_z(1))]
    normed_mlp_all = gather_plane(normed_mlp_own)
    core_mlp = [send(block, across_core) for block in own_mlp]
    z_own = z_arg if square else jnp.zeros_like(z_arg)
    hidden, grad_gu, *grad_in, normed_mlp, upstream_low = feed_forward(
        z_own, normed_mlp_all, upstream_all, own_mlp, core_mlp
    )
    grad_near, grad_far = grad_in[:2], grad_in[2:]
    from_core_gu = send(weight_grads(normed_mlp, 0, grad_gu, 1, 2), across_core)
    down_core = weight_grads(hidden, 1, upstream_low, 0, 1)
    grad_w_gu = weight_grads(normed_mlp, 0, grad_gu, 0, 2, from_core_gu)
    grad_normed_mlp = scatter_plane(grad_near, grad_far, at_first=(down_core, grad_w_gu))
    got_gu = along_z(grad_w_gu.reshape(n_z, 2 * shard, -1))
    total_gu = jnp.sum(got_gu.astype(F32), axis=0).astype(BF)
    upstream = cotangent.astype(F32)
    scaled = grad_normed_mlp * full_gain_mlp
    grad_middle = (
        upstream
        + inverse_mlp * scaled
        - middle * inverse_mlp**3 * jnp.mean(scaled * middle, axis=-1, keepdims=True)
    )
    down = down_project(z_own, hidden, own_mlp, core_mlp, width)
    from_core = send(down_core, across_core)
    grad_w_down = weight_grads(hidden, 0, upstream_low, 0, 1, from_core)
    grad_attended_all = gather_plane(
        after(grad_middle.astype(BF), grad_w_gu), *down, grad_w_down
    )
    down = lax.optimization_barrier((*down, *grad_attended_all))[:5]
    (own, own_y), (far, far_a, far_b) = down[:2], down[2:]
    half = rows // 2
    first, second = send(far_a, across_y), send(far_b, across_x)

    def swap_rows(total):
        mine = lax.dynamic_slice_in_dim(total, y * shard, shard, 0)
        other = lax.dynamic_slice_in_dim(total, (1 - y) * shard, shard, 0)
        return pair_y(mine, send(other, across_y)).reshape(2 * shard, -1)

    mine_gu = swap_rows(total_gu)
    gu_blocks = gather_dp(mine_gu)
    if ff_part % 128 == 0:
        gain_column = gain_mlp.astype(F32).reshape(-1, 1)
        out_gate, out_up, grad_gain_mlp = lay_out(d_arg, gu_blocks, w_gate, w_up, gain_column)
    else:
        all_gu = jnp.stack(order_dp(gu_blocks)).reshape(n_dp, 2, shard, 2, n_z, ff_part)
        all_gu = all_gu.transpose(3, 2, 4, 1, 0, 5).reshape(2, shard, -1).astype(F32)
        out_gate, out_up = all_gu[0], all_gu[1]
        grad_gain_mlp = jnp.sum(
            w_gate.astype(F32) * out_gate + w_up.astype(F32) * out_up, axis=1
        ) / gain_mlp.astype(F32)

    grad_query, grad_kv, halo_back = [None] * 2, [None] * 2, [None] * 2
    grad_out = ()
    for group in (0, 1):
        dy = parts_of(grad_attended_all, group)
        grad_query[group], grad_kv[group], grad_halo, grad_out = attend_back(
            y_arg, group, qkv[group], halo_in[group], seg_query, seg_key, full_out,
            context[group], logsum[group], cosine, sine, dy, (grad_out,) if group else (),
        )
        grad_halo, first, second = lax.optimization_barrier((grad_halo, first, second, got_gu))[:3]
        halo_back[group] = send(grad_halo, lambda d, s: (d, s - 2))
    grad_qkv, grad_in = [None] * 2, [None] * 2
    far = jnp.concatenate([plus(far[:half], first), far[half:]], axis=0)
    own_y = jnp.concatenate([own_y[:half], plus(own_y[half:], second)], axis=0)
    down_x, down_y = send(far, across_x), send(own_y, across_y)
    halo_back[1] = after(halo_back[1], mine_gu)
    for group in (0, 1):
        grad_qkv[group], *grad_in[group] = qkv_back(
            group, grad_query[group], grad_kv[group], halo_back[group], cosine, sine, *full_qkv, width
        )
    grad_w_down = lax.optimization_barrier((grad_w_down, halo_back[1]))[0]
    total_down = scatter_z(grad_w_down.reshape(n_z, ff_part, width)).astype(BF)
    out_down = lay_out_rows(d_arg, gather_dp(total_down))

    def attn_grads(slot):
        for_qkv = dot_tn(normed[0], grad_qkv[0][slot]) + dot_tn(normed[1], grad_qkv[1][slot])
        for_qkv = for_qkv.astype(BF).reshape(n_z, 2 * shard, -1)
        if not square:
            return for_qkv
        for_out = [
            fold(grad_out[slot, z * out_rows : (z + 1) * out_rows], lanes) for z in range(n_z)
        ]
        return jnp.concatenate([for_qkv, jnp.stack(for_out)], axis=1)

    grad_attn = sum_core(attn_grads(0), attn_grads(1))
    output = (
        middle + own.astype(F32) + down_x.astype(F32) + down_y.astype(F32)
    ).astype(BF)
    total_attn = along_z(grad_attn)
    total_attn = jnp.sum(total_attn.astype(F32), axis=0).astype(BF)
    mine_attn = swap_rows(total_attn[: 2 * shard]).reshape(2 * shard, -1)
    if square:
        mine_attn = jnp.concatenate([mine_attn, send(total_attn[2 * shard :], turned)], axis=0)
    attn_blocks = gather_dp(mine_attn, out_gate, out_down)
    if square:
        out_query, out_key, out_value, out_out, grad_gain_attn = lay_out_heads(
            d_arg, attn_blocks, w_query, w_key, w_value, gain_attn.astype(F32).reshape(-1, 1), w_out.shape
        )
    else:
        attn_blocks = order_dp(attn_blocks)
        grad_w_out = sum_core(grad_out[0], grad_out[1]).astype(F32)
        out_out = jnp.zeros((2 * n_dp * q_w, width), F32)
        out_out = lax.dynamic_update_slice_in_dim(out_out, grad_w_out, (2 * d + y) * q_w, 0)
        out_out = lax.psum_scatter(out_out, "seq", scatter_dimension=0, tiled=True)
        out_out = lax.psum(out_out.astype(BF), "dp").astype(F32)
        all_qkv = jnp.stack(attn_blocks).astype(F32)
        out_qkv = all_qkv.reshape(2 * n_dp, shard, lanes).transpose(1, 0, 2)
        out_query = out_qkv[..., :q_w].reshape(shard, -1)
        out_key = out_qkv[..., q_w : q_w + k_w].reshape(shard, -1)
        out_value = out_qkv[..., q_w + k_w :].reshape(shard, -1)
        grad_gain_attn = (
            jnp.sum(w_query.astype(F32) * out_query, axis=1)
            + jnp.sum(w_key.astype(F32) * out_key, axis=1)
            + jnp.sum(w_value.astype(F32) * out_value, axis=1)
        ) / gain_attn.astype(F32)

    own = scatter_plane(*grad_in, at_first=(down_x, down_y))
    wide = tokens.astype(F32)
    own_inverse = lax.rsqrt(jnp.mean(wide * wide, axis=-1, keepdims=True) + EPS)
    scaled = own * full_gain_attn
    grad_tokens = (
        grad_middle
        + own_inverse * scaled
        - wide * own_inverse**3 * jnp.mean(scaled * wide, axis=-1, keepdims=True)
    )
    return (
        output,
        grad_tokens,
        grad_gain_attn.reshape(-1),
        out_query,
        out_key,
        out_value,
        out_out,
        grad_gain_mlp.reshape(-1),
        out_gate,
        out_up,
        out_down,
    )


def solution(mesh):
    return jax.shard_map(
        on_device,
        mesh=mesh,
        in_specs=(
            P(("dp", "seq"), None),
            P("dp", None),
            P(("dp", "seq"), None),
            P("seq"),
            P("seq", None),
            P("seq", None),
            P("seq", None),
            P("seq", None),
            P("seq"),
            P("seq", None),
            P("seq", None),
            P("seq", None),
        ),
        out_specs=(
            P(("dp", "seq"), None),
            P(("dp", "seq"), None),
            P("seq"),
            P("seq", None),
            P("seq", None),
            P("seq", None),
            P("seq", None),
            P("seq"),
            P("seq", None),
            P("seq", None),
            P("seq", None),
        ),
        check_vma=False,
    )
```

```python
import functools
import math

import jax
import jax.numpy as jnp
from jax import lax
from jax.experimental import pallas as pl
from jax.experimental.pallas import tpu as pltpu
from jax.sharding import PartitionSpec as P

HEADS = 16
KV_HEADS = 8
HEAD = 96
WINDOW = 512


EPS = 1e-05
THETA = 100000.0
BOTH = ("dp", "seq")
BF = jnp.bfloat16
F32 = jnp.float32


def send(block, target):
    n_dp, n_seq = lax.axis_size("dp"), lax.axis_size("seq")
    route = []
    for d in range(n_dp):
        for s in range(n_seq):
            to = target(d, s)
            if to is not None and 0 <= to[1] < n_seq:
                route.append((d * n_seq + s, to[0] * n_seq + to[1]))
    return lax.ppermute(block, BOTH, route)


def after(value, *others):
    return lax.optimization_barrier((value,) + others)[0]


def across_core(d, s):
    return (d ^ 1, s)


def across_x(d, s):
    return (d ^ 2, s)


def across_y(d, s):
    return (d, s ^ 1)


def gather_plane(block, *meanwhile, for_y=None, came=None):
    half = block.shape[0] // 2
    from_x, from_y = came or (
        send(block, across_x),
        send(block if for_y is None else for_y, across_y),
    )
    if meanwhile:
        from_x, from_y = lax.optimization_barrier((from_x, from_y, *meanwhile))[:2]
    first = send(from_x[:half], across_y)
    second = send(from_y[half:], across_x)
    return [block, from_y, from_x, first, second]


def plus(a, b):
    return (a.astype(F32) + b.astype(F32)).astype(BF)


def scatter_plane(near, far, *meanwhile, at_first=()):
    own, own_y = near
    far, far_a, far_b = far
    half = far_a.shape[0]
    first = send(far_a, across_y)
    second = send(far_b, across_x)
    if at_first:
        first, second = lax.optimization_barrier((first, second, *at_first))[:2]

    far = jnp.concatenate([plus(far[:half], first), far[half:]], axis=0)
    own_y = jnp.concatenate([own_y[:half], plus(own_y[half:], second)], axis=0)
    from_x, from_y = send(far, across_x), send(own_y, across_y)
    if meanwhile:
        from_x, from_y = lax.optimization_barrier((from_x, from_y, *meanwhile))[:2]
    return own.astype(F32) + from_x.astype(F32) + from_y.astype(F32)


def with_core(block):
    return [block, send(block, across_core)]


def sum_core(mine, other):
    return (mine.astype(F32) + send(other.astype(BF), across_core).astype(F32)).astype(BF)


def across_z(k):
    return lambda d, s: (d, s ^ (2 * k))


def along_z(blocks):
    n_seq = lax.axis_size("seq")
    lines = [list(range(y, n_seq, 2)) for y in range(2)]
    return lax.all_to_all(blocks, "seq", 0, 0, axis_index_groups=lines)


def gather_z(block):
    return along_z(jnp.broadcast_to(block[None], (lax.axis_size("seq") // 2,) + block.shape))


def scatter_z(blocks):
    return jnp.sum(along_z(blocks).astype(F32), axis=0)


def pair_y(mine, other):
    y = lax.axis_index("seq") % 2
    return jnp.stack([jnp.where(y == 0, mine, other), jnp.where(y == 0, other, mine)])


def turned(d, s):
    return (s // 2, 2 * d + s % 2)


def fold(rows, wide):
    count, columns = rows.shape
    whole = columns // wide
    parts = [rows[:, i * wide : (i + 1) * wide] for i in range(whole)]
    rest = rows[:, whole * wide :]
    if rest.shape[1]:
        times = wide // rest.shape[1]
        step = count // times
        parts.append(
            jnp.concatenate([rest[i * step : (i + 1) * step] for i in range(times)], axis=1)
        )
    return jnp.concatenate(parts, axis=0)


def unfold(folded, columns):
    total, wide = folded.shape
    count = total * wide // columns
    whole = columns // wide
    parts = [folded[i * count : (i + 1) * count] for i in range(whole)]
    if columns % wide:
        rest, narrow = folded[whole * count :], columns % wide
        parts.append(
            jnp.concatenate(
                [rest[:, i * narrow : (i + 1) * narrow] for i in range(wide // narrow)], axis=0
            )
        )
    return jnp.concatenate(parts, axis=1)


def gather_dp(block, *meanwhile):
    core = send(block, across_core)
    far = send(block, across_x)
    if meanwhile:
        far = lax.optimization_barrier((far, *meanwhile))[0]
    return [block, core, far, send(far, across_core)]


def order_dp(blocks):
    d = lax.axis_index("dp")
    pairs = [
        (jnp.where(d % 2 == 0, a, b), jnp.where(d % 2 == 0, b, a))
        for a, b in (blocks[:2], blocks[2:])
    ]
    low, high = pairs
    return [jnp.where(d < 2, a, b) for a, b in zip(low, high)] + [
        jnp.where(d < 2, b, a) for a, b in zip(low, high)
    ]


def rope_tables(position):
    lane = jnp.arange(128, dtype=jnp.float32) % (HEAD // 2)
    angles = position.astype(jnp.float32)[..., None] * THETA ** (-2.0 * lane / HEAD)
    return jnp.cos(angles), jnp.sin(angles)


SCALE = 0.3
VMEM_BYTES = 60 * 1024 * 1024


def call(kernel, out_shape, flops, moved, **rest):
    return pl.pallas_call(
        kernel,
        out_shape=out_shape,
        compiler_params=pltpu.CompilerParams(vmem_limit_bytes=VMEM_BYTES),
        cost_estimate=pl.CostEstimate(flops=int(flops * SCALE), bytes_accessed=int(moved * SCALE), transcendentals=0),
        **rest,
    )


def shaped(shape, dtype):
    return jax.ShapeDtypeStruct(shape, dtype)


def iota(shape, axis):
    return lax.broadcasted_iota(jnp.int32, shape, axis)


def dot(a, b):
    return jnp.dot(a, b, preferred_element_type=F32)


def dot_nt(a, b):
    return lax.dot_general(a, b, (((1,), (1,)), ((), ())), preferred_element_type=F32)


def dot_tn(a, b):
    return lax.dot_general(a, b, (((0,), (0,)), ((), ())), preferred_element_type=F32)


def spread(packed, heads, base):
    row, column = iota((packed, heads * 128), 0), iota((packed, heads * 128), 1)
    lane = column % 128
    hit = (row == base + HEAD * (column // 128) + lane) & (lane < HEAD)
    return jnp.where(hit, 1.0, 0.0).astype(BF)


def pack(packed, heads, base):
    column, row = iota((heads * 128, packed), 0), iota((heads * 128, packed), 1)
    lane = column % 128
    hit = (row == base + HEAD * (column // 128) + lane) & (lane < HEAD)
    return jnp.where(hit, 1.0, 0.0).astype(BF)


def on_heads(table, heads, packed):
    row, column = iota((128, packed), 0), iota((128, packed), 1)
    place = jnp.where((row == column % HEAD) & (column < heads * HEAD), 1.0, 0.0).astype(BF)
    high = table.astype(BF)
    rest = table - high.astype(F32)
    middle = rest.astype(BF)
    low = (rest - middle.astype(F32)).astype(BF)
    return dot(high, place) + dot(middle, place) + dot(low, place)


def qkv_kernel(*refs):
    parts, refs = refs[:-8], refs[-8:]
    gain, cosine, sine, w_own, w_core, normed, qkv, halo = refs
    tokens, lanes = halo.shape
    x = jnp.concatenate([part[...] for part in parts], axis=0).astype(F32)
    inverse = lax.rsqrt(jnp.mean(x * x, axis=-1, keepdims=True) + EPS)
    low = (x * inverse * gain[...]).astype(BF)
    normed[...] = low
    lane = iota((tokens, lanes), 1)
    first = lane % HEAD < HEAD // 2
    cos_all = on_heads(cosine[...], 3, lanes) + jnp.where(lane >= 3 * HEAD, 1.0, 0.0)
    sin_all = on_heads(sine[...], 3, lanes)
    turned = []
    size = normed.shape[1] // w_own.shape[0]
    for w in (w_own, w_core):
        raw = sum(dot(low[:, z * size : (z + 1) * size], w[z, :size, :]) for z in range(w.shape[0]))
        half = jnp.where(
            first, -pltpu.roll(raw, lanes - HEAD // 2, 1), pltpu.roll(raw, HEAD // 2, 1)
        )
        turned.append(raw * cos_all + half * sin_all)
    qkv[0] = turned[0].astype(BF)
    qkv[1] = turned[1].astype(BF)
    halo[...] = jnp.where(
        lane < lanes // 2, pltpu.roll(turned[1], lanes // 2, 1), turned[0]
    ).astype(BF)


def project(group, parts, gain, cosine, sine, w_own, w_core):
    tokens = sum(part.shape[0] for part in parts)
    width, lanes = gain.shape[1], w_own.shape[2]

    def whole(array):
        return pl.BlockSpec(array.shape, lambda i: (0,) * array.ndim)

    table = pl.BlockSpec((tokens, 128), lambda i: (group, 0))
    outs = [shaped((tokens, width), BF), shaped((2, tokens, lanes), BF), shaped((tokens, lanes), BF)]
    return call(
        qkv_kernel,
        outs,
        flops=4 * tokens * width * lanes,
        moved=6 * 10**6,
        grid=(1,),
        in_specs=[whole(part) for part in parts] + [whole(gain), table, table, whole(w_own), whole(w_core)],
        out_specs=[whole(out) for out in outs],
    )(*parts, gain, cosine, sine, w_own, w_core)


def visible(seg_query, seg_key, a, rows):
    shape = (rows, 3 * rows)
    row, column = iota(shape, 0), iota(shape, 1)
    same = seg_query[0, a] == jnp.concatenate([seg_key[0, a + i] for i in range(3)], axis=1)
    allowed = (column > row) & (column <= row + 2 * rows) & same
    return jnp.concatenate([allowed, allowed], axis=0)


def heads_of(y, slot, qkv, halo, rows):
    lanes = qkv.shape[-1]

    def at(a):
        return pl.ds(pl.multiple_of((a ^ y) * rows, rows), rows)

    before = spread(lanes, 2, (1 - slot) * (lanes // 2))
    here = spread(lanes, 4, 0)
    local = [dot(qkv[0, at(a), :], here).astype(BF) for a in range(2)]
    key_value = [dot(halo[at(a), :], before).astype(BF) for a in range(2)]
    key_value += [part[:, 256:] for part in local]
    query = [jnp.concatenate([part[:, :128], part[:, 128:256]], axis=0) for part in local]
    return at, query, key_value


def padded_out(w_out):
    rows = w_out.shape[1]
    return dot(pack(rows, 2, 0), w_out[0]).astype(BF)


def attend_kernel(y_ref, qkv, halo, seg_query, seg_key, w_out, *refs):
    *partial, context, logsum, total = refs
    slot = pl.program_id(0)
    rows = qkv.shape[1] // 2
    at, query, key_value = heads_of(y_ref[0], slot, qkv, halo, rows)
    w = padded_out(w_out)
    for a in range(2):
        kv = jnp.concatenate(key_value[a : a + 3], axis=0)
        scores = dot_nt(query[a], kv[:, :128]) * (1.0 / math.sqrt(HEAD))
        scores = jnp.where(visible(seg_query, seg_key, a, rows), scores, -1e30)
        peak = jnp.max(scores, axis=-1, keepdims=True)
        exponent = jnp.exp(scores - peak)
        row_total = jnp.sum(exponent, axis=-1, keepdims=True)
        probs = (exponent * (1.0 / row_total)).astype(BF)
        logsum[0, a] = peak + jnp.log(row_total)
        seen = dot(probs, kv[:, 128:]).astype(BF)
        seen = jnp.concatenate([seen[:rows], seen[rows:]], axis=1)
        context[0, at(a), :] = seen
        product = dot(seen, w)

        @pl.when(slot == 0)
        def _():
            total[at(a), :] = product

        @pl.when(slot == 1)
        def _():
            total[at(a), :] += product

    @pl.when(slot == 1)
    def _():
        begin = 0
        for out in partial:
            out[...] = total[begin : begin + out.shape[0], :].astype(BF)
            begin += out.shape[0]


def attend(y, group, qkv, halo, seg_query, seg_key, w_out):
    slots, reach, lanes = qkv.shape
    rows, width = reach // 2, w_out.shape[-1]
    sizes = (rows, rows // 2, rows // 2) if group else (rows, rows)
    return call(
        attend_kernel,
        [shaped((size, width), BF) for size in sizes]
        + [
            shaped((slots, reach, 256), BF),
            shaped((slots, 2, reach, 1), F32),
        ],
        flops=5 * 10**9,
        moved=7 * 10**6,
        grid_spec=pltpu.PrefetchScalarGridSpec(
            num_scalar_prefetch=1,
            grid=(slots,),
            in_specs=[
                pl.BlockSpec((1, reach, lanes), lambda s, y: (s, 0, 0)),
                pl.BlockSpec((reach, lanes), lambda s, y: (0, 0)),
                pl.BlockSpec((1, 2, rows, 1), lambda s, y: (group, 0, 0, 0)),
                pl.BlockSpec((1, 4, 1, rows), lambda s, y: (group, 0, 0, 0)),
                pl.BlockSpec((1,) + w_out.shape[1:], lambda s, y: (s, 0, 0)),
            ],
            out_specs=[pl.BlockSpec((size, width), lambda s, y: (0, 0)) for size in sizes]
            + [
                pl.BlockSpec((1, reach, 256), lambda s, y: (s, 0, 0)),
                pl.BlockSpec((1, 2, reach, 1), lambda s, y: (s, 0, 0, 0)),
            ],
            scratch_shapes=[pltpu.VMEM((reach, width), F32)],
        ),
    )(y, qkv, halo, seg_query, seg_key, w_out)


def load_blocks(parts, whole, sems):
    copies, at = [], 0
    for i, part in enumerate(parts):
        copies.append(
            pltpu.make_async_copy(part, whole.at[pl.ds(at, part.shape[0])], sems.at[i])
        )
        at += part.shape[0]
    for copy in copies:
        copy.start()
    return copies


def weight_copies(me, weights, gu, down, sems):
    n_z, wide = len(weights), weights[0].shape[1]
    width = down.shape[1]
    step, ff_part = width // n_z, down.shape[0] // n_z
    half = ff_part * (width - wide) // wide
    first, second = [], []
    for r, block in enumerate(weights):
        z = me ^ r
        row = pl.multiple_of(z * ff_part, ff_part)
        if gu is not None:
            first.append(
                pltpu.make_async_copy(
                    block.at[pl.ds(0, step)],
                    gu.at[pl.ds(pl.multiple_of(z * step, step), step)],
                    sems.at[0, r],
                )
            )
        second.append(
            pltpu.make_async_copy(
                block.at[pl.ds(step, ff_part)],
                down.at[pl.ds(row, ff_part), pl.ds(0, wide)],
                sems.at[1, r],
            )
        )
        for i in range(2):
            second.append(
                pltpu.make_async_copy(
                    block.at[pl.ds(step + ff_part, half), pl.ds(i * wide // 2, wide // 2)],
                    down.at[pl.ds(row + i * half, half), pl.ds(wide, width - wide)],
                    sems.at[2 + i, r],
                )
            )
    return first + second


def mlp_kernel(n_z, z_ref, *refs):
    n_parts, d_parts, refs = refs[:5], refs[5:10], refs[10:]
    w_own, w_core, refs = refs[:n_z], refs[n_z : 2 * n_z], refs[2 * n_z :]
    hidden, grad_gu, *grad_in, normed_out, upstream_out = refs[:9]
    normed, upstream, gu, down, total, n_sems, d_sems, w_sems, out_sems = refs[9:]
    slot = pl.program_id(0)
    ff = gu.shape[2] // 2
    core_copies = weight_copies(z_ref[0], w_core, gu.at[1], down.at[1], w_sems.at[1])
    kept = [
        pltpu.make_async_copy(normed, normed_out, out_sems.at[0]),
        pltpu.make_async_copy(upstream, upstream_out, out_sems.at[1]),
    ]

    @pl.when(slot == 0)
    def _():
        copies = load_blocks(n_parts, normed, n_sems)
        copies += weight_copies(z_ref[0], w_own, gu.at[0], down.at[0], w_sems.at[0])
        for copy in copies[5:]:
            copy.start()
        copies += load_blocks(d_parts, upstream, d_sems)
        for copy in core_copies:
            copy.start()
        for copy in copies:
            copy.wait()
        for copy in kept:
            copy.start()

    @pl.when(slot == 1)
    def _():
        for copy in core_copies:
            copy.wait()

    n, dy = normed[...], upstream[...]
    gate = dot(n, gu[slot, :, :ff])
    up = dot(n, gu[slot, :, ff:])
    dh = dot_nt(dy, down[slot])
    sigmoid = jax.nn.sigmoid(gate)
    silu = gate * sigmoid
    hidden[0] = (silu * up).astype(BF)
    d_gate = (dh * up * sigmoid * (1.0 + gate * (1.0 - sigmoid))).astype(BF)
    d_up = (dh * silu).astype(BF)
    grad_gu[0, :, :ff] = d_gate
    grad_gu[0, :, ff:] = d_up
    part = dot_nt(d_gate, gu[slot, :, :ff]) + dot_nt(d_up, gu[slot, :, ff:])

    @pl.when(slot == 0)
    def _():
        total[...] = part

    @pl.when(slot == 1)
    def _():
        whole = (total[...] + part).astype(BF)
        begin = 0
        for out in grad_in:
            out[...] = whole[begin : begin + out.shape[0]]
            begin += out.shape[0]
        for copy in kept:
            copy.wait()


def feed_forward(z, normed, upstream, w_own, w_core):
    rows, width = normed[0].shape
    n_z, wide = len(w_own), w_own[0].shape[1]
    tokens, ff = 4 * rows, wide // 2
    anywhere = pl.BlockSpec(memory_space=pl.ANY)
    block = pl.BlockSpec((rows, width), lambda s, z: (0, 0))
    half = pl.BlockSpec((rows // 2, width), lambda s, z: (0, 0))
    return call(
        functools.partial(mlp_kernel, n_z),
        [
            shaped((2, tokens, ff), BF),
            shaped((2, tokens, wide), BF),
            shaped((rows, width), BF),
            shaped((rows, width), BF),
            shaped((rows, width), BF),
            shaped((rows // 2, width), BF),
            shaped((rows // 2, width), BF),
            shaped((tokens, width), BF),
            shaped((tokens, width), BF),
        ],
        flops=10 * tokens * width * wide,
        moved=25 * 10**6,
        grid_spec=pltpu.PrefetchScalarGridSpec(
            num_scalar_prefetch=1,
            grid=(2,),
            in_specs=[anywhere] * (10 + 2 * n_z),
            out_specs=[
                pl.BlockSpec((1, tokens, ff), lambda s, z: (s, 0, 0)),
                pl.BlockSpec((1, tokens, wide), lambda s, z: (s, 0, 0)),
                block,
                block,
                block,
                half,
                half,
                anywhere,
                anywhere,
            ],
            scratch_shapes=[
                pltpu.VMEM((tokens, width), BF),
                pltpu.VMEM((tokens, width), BF),
                pltpu.VMEM((2, width, wide), BF),
                pltpu.VMEM((2, ff, width), BF),
                pltpu.VMEM((tokens, width), F32),
                pltpu.SemaphoreType.DMA((5,)),
                pltpu.SemaphoreType.DMA((5,)),
                pltpu.SemaphoreType.DMA((2, 4, n_z)),
                pltpu.SemaphoreType.DMA((2,)),
            ],
        ),
    )(z, *normed, *upstream, *w_own, *w_core)


def down_kernel(n_z, z_ref, hidden, *refs):
    w_own, w_core, refs = refs[:n_z], refs[n_z : 2 * n_z], refs[2 * n_z :]
    *outs, down, total, sems = refs
    slot = pl.program_id(0)
    core_copies = weight_copies(z_ref[0], w_core, None, down.at[1], sems.at[1])

    @pl.when(slot == 0)
    def _():
        copies = weight_copies(z_ref[0], w_own, None, down.at[0], sems.at[0])
        for copy in copies + core_copies:
            copy.start()
        for copy in copies:
            copy.wait()

    @pl.when(slot == 1)
    def _():
        for copy in core_copies:
            copy.wait()

    part = dot(hidden[0], down[slot])

    @pl.when(slot == 0)
    def _():
        total[...] = part

    @pl.when(slot == 1)
    def _():
        whole, begin = (total[...] + part).astype(BF), 0
        for out in outs:
            out[...] = whole[begin : begin + out.shape[0]]
            begin += out.shape[0]


def down_project(z, hidden, w_own, w_core, width):
    _, tokens, ff = hidden.shape
    n_z, rows = len(w_own), tokens // 4
    sizes = (rows, rows, rows, rows // 2, rows // 2)
    return call(
        functools.partial(down_kernel, n_z),
        [shaped((size, width), BF) for size in sizes],
        flops=4 * tokens * width * ff,
        moved=8 * 10**6,
        grid_spec=pltpu.PrefetchScalarGridSpec(
            num_scalar_prefetch=1,
            grid=(2,),
            in_specs=[pl.BlockSpec((1, tokens, ff), lambda s, z: (s, 0, 0))]
            + [pl.BlockSpec(memory_space=pl.ANY)] * (2 * n_z),
            out_specs=[pl.BlockSpec((size, width), lambda s, z: (0, 0)) for size in sizes],
            scratch_shapes=[
                pltpu.VMEM((2, ff, width), BF),
                pltpu.VMEM((tokens, width), F32),
                pltpu.SemaphoreType.DMA((2, 4, n_z)),
            ],
        ),
    )(z, hidden, *w_own, *w_core)


def grads_kernel(left, right, *rest):
    grad = dot_tn(left[...].reshape(left.shape[-2:]), right[...].reshape(right.shape[-2:]))
    if len(rest) == 2:
        grad = grad + rest[0][...].astype(F32)
    rest[-1][...] = grad.astype(BF)


def weight_grads(left, left_slot, right, right_slot, steps, *other):
    tokens, rows, columns = left.shape[-2], left.shape[-1], right.shape[-1]
    block = pl.BlockSpec((rows, columns // steps), lambda i: (0, i))

    def part(array, slot, blocks):
        if array.ndim == 2:
            return pl.BlockSpec((tokens, array.shape[1] // blocks), lambda i: (0, i if blocks > 1 else 0))
        return pl.BlockSpec(
            (1, tokens, array.shape[2] // blocks), lambda i: (slot, 0, i if blocks > 1 else 0)
        )

    return call(
        grads_kernel,
        shaped((rows, columns), BF),
        flops=2 * tokens * rows * columns,
        moved=10 * 10**6,
        grid=(steps,),
        in_specs=[part(left, left_slot, 1), part(right, right_slot, steps)] + [block] * len(other),
        out_specs=block,
    )(left, right, *other)


def cut_kernel(place_ref, w_gate, w_up, mine, other):
    ff = mine.shape[1] // 2
    for to, y in ((mine, place_ref[1]), (other, 1 - place_ref[1])):
        for i, w in enumerate((w_gate, w_up)):
            for z in range(ff // 128):
                at = pl.multiple_of(((2 * z + y) * 4 + place_ref[0]) * 128, 128)
                begin = i * ff + z * 128
                to[:, begin : begin + 128] = w[:, pl.ds(at, 128)]


def cut_columns(place, w_gate, w_up, columns):
    vmem = pl.BlockSpec(memory_space=pltpu.VMEM)
    return call(
        cut_kernel,
        [shaped((w_gate.shape[0], columns), BF)] * 2,
        flops=10**6,
        moved=8 * 10**6,
        in_specs=[pl.BlockSpec(memory_space=pltpu.SMEM)] + [vmem] * 2,
        out_specs=[vmem] * 2,
    )(place, w_gate, w_up)


def place_kernel(z_ref, own, core, out):
    rows = own.shape[1]
    for slot, pieces in enumerate((own, core)):
        for k in range(own.shape[0]):
            to = pl.multiple_of((z_ref[0] ^ k) * rows, rows)
            out[slot, pl.ds(to, rows), :] = pieces[k]


def place(z, own, core):
    n, rows, columns = own.shape
    vmem = pl.BlockSpec(memory_space=pltpu.VMEM)
    return call(
        place_kernel,
        shaped((2, n * rows, columns), BF),
        flops=10**6,
        moved=8 * n * rows * columns,
        in_specs=[pl.BlockSpec(memory_space=pltpu.SMEM)] + [vmem] * 2,
        out_specs=vmem,
    )(z, own, core)


def turn_back(values, cosine, sine):
    lane = iota(values.shape, 1)
    across = values * sine
    moved = jnp.where(
        lane < HEAD // 2,
        pltpu.roll(across, 128 - HEAD // 2, 1),
        jnp.where(lane < HEAD, -pltpu.roll(across, HEAD // 2, 1), 0.0),
    )
    return values * cosine + moved


def attend_back_kernel(n_parts, *refs):
    y_ref, qkv, halo, seg_query, seg_key, w_out, context, logsum, cosine, sine = refs[:10]
    parts, rest = refs[10 : 10 + n_parts], refs[10 + n_parts :]
    before = rest[0] if len(rest) == 9 else None
    grad_query, grad_kv, grad_halo, grad_out, up, kv_total, out_total, sems = rest[-8:]
    slot = pl.program_id(0)
    reach = qkv.shape[1]
    rows = reach // 2
    factor = 1.0 / math.sqrt(HEAD)

    @pl.when(slot == 0)
    def _():
        for copy in load_blocks(parts, up, sems):
            copy.wait()

    at, query, key_value = heads_of(y_ref[0], slot, qkv, halo, rows)
    w = padded_out(w_out)
    kv_total[...] = jnp.zeros_like(kv_total)
    out_part = None
    for a in range(2):
        dy = up[at(a), :]
        d_context = dot_nt(dy, w).astype(BF)
        part = dot_tn(context[0, at(a), :], dy)
        out_part = part if out_part is None else out_part + part
        d_seen = jnp.concatenate([d_context[:, :128], d_context[:, 128:]], axis=0)
        kv = jnp.concatenate(key_value[a : a + 3], axis=0)
        key, value = kv[:, :128], kv[:, 128:]
        scores = dot_nt(query[a], key) * factor
        probs = jnp.exp(
            jnp.where(visible(seg_query, seg_key, a, rows), scores - logsum[0, a], -1e30)
        )
        d_probs = dot_nt(d_seen, value)
        delta = jnp.sum(probs * d_probs, axis=-1, keepdims=True)
        d_scores = (probs * (d_probs - delta)).astype(BF)
        d_query = dot(d_scores, key) * factor
        cos_a, sin_a = cosine[at(a), :], sine[at(a), :]
        turned = jnp.concatenate(
            [turn_back(d_query[:rows], cos_a, sin_a), turn_back(d_query[rows:], cos_a, sin_a)],
            axis=1,
        ).astype(BF)
        grad_query[0, at(a), :] = dot(turned, pack(qkv.shape[-1], 2, 0)).astype(BF)
        seen = slice(a * rows, (a + 3) * rows)
        kv_total[seen, :128] += dot_tn(d_scores, query[a]) * factor
        kv_total[seen, 128:] += dot_tn(probs.astype(BF), d_seen)
    back = pack(qkv.shape[-1], 2, (1 - slot) * (qkv.shape[-1] // 2))
    for a in range(2):
        grad_kv[0, at(a), :] = kv_total[(a + 2) * rows : (a + 3) * rows, :]
        placed = dot(kv_total[a * rows : (a + 1) * rows, :].astype(BF), back).astype(BF)

        @pl.when(slot == 0)
        def _():
            grad_halo[at(a), :] = placed

        @pl.when(slot == 1)
        def _():
            grad_halo[at(a), :] += placed

    out_total[...] = out_part.astype(BF)
    part = dot(spread(w_out.shape[1], 2, 0), out_total[...])
    if before is not None:
        part = part + before[0].astype(F32)
    grad_out[0] = part.astype(BF)


def attend_back(y, group, qkv, halo, seg_query, seg_key, w_out, context, logsum, cosine, sine, upstream, before=()):
    slots, reach, lanes = qkv.shape
    rows, width = reach // 2, w_out.shape[-1]
    weight = pl.BlockSpec((1,) + w_out.shape[1:], lambda s, y: (s, 0, 0))
    return call(
        functools.partial(attend_back_kernel, len(upstream)),
        [
            shaped((slots, reach, lanes), BF),
            shaped((slots, reach, 256), F32),
            shaped((reach, lanes), BF),
            shaped(w_out.shape, BF),
        ],
        flops=12 * 10**9,
        moved=10 * 10**6,
        grid_spec=pltpu.PrefetchScalarGridSpec(
            num_scalar_prefetch=1,
            grid=(slots,),
            in_specs=[
                pl.BlockSpec((1, reach, lanes), lambda s, y: (s, 0, 0)),
                pl.BlockSpec((reach, lanes), lambda s, y: (0, 0)),
                pl.BlockSpec((1, 2, rows, 1), lambda s, y: (group, 0, 0, 0)),
                pl.BlockSpec((1, 4, 1, rows), lambda s, y: (group, 0, 0, 0)),
                weight,
                pl.BlockSpec((1, reach, 256), lambda s, y: (s, 0, 0)),
                pl.BlockSpec((1, 2, reach, 1), lambda s, y: (s, 0, 0, 0)),
                pl.BlockSpec((reach, 128), lambda s, y: (group, 0)),
                pl.BlockSpec((reach, 128), lambda s, y: (group, 0)),
            ]
            + [pl.BlockSpec(memory_space=pl.ANY)] * len(upstream)
            + [weight] * len(before),
            out_specs=[
                pl.BlockSpec((1, reach, lanes), lambda s, y: (s, 0, 0)),
                pl.BlockSpec((1, reach, 256), lambda s, y: (s, 0, 0)),
                pl.BlockSpec((reach, lanes), lambda s, y: (0, 0)),
                weight,
            ],
            scratch_shapes=[
                pltpu.VMEM((reach, width), BF),
                pltpu.VMEM((2 * reach, 256), F32),
                pltpu.VMEM((256, width), BF),
                pltpu.SemaphoreType.DMA((len(upstream),)),
            ],
        ),
    )(y, qkv, halo, seg_query, seg_key, w_out, context, logsum, cosine, sine, *upstream, *before)


def qkv_back_kernel(grad_query, grad_kv, grad_halo, cosine, sine, w_own, w_core, grad_qkv, *grad_in):
    lanes = grad_halo.shape[-1]
    total = None
    place = pack(lanes, 2, lanes // 2)
    size = grad_in[0].shape[1] // w_own.shape[0]
    for slot, w in enumerate((w_own, w_core)):
        kv = grad_kv[slot] + dot(grad_halo[...], spread(lanes, 2, (1 - slot) * (lanes // 2)))
        key = turn_back(kv[:, :128], cosine[...], sine[...])
        kv = jnp.concatenate([key, kv[:, 128:]], axis=1).astype(BF)
        both = grad_query[slot] + dot(kv, place).astype(BF)
        grad_qkv[slot] = both
        part = [dot_nt(both, w[z, :size, :]) for z in range(w.shape[0])]
        part = jnp.concatenate(part, axis=1)
        total = part if total is None else total + part
    whole, begin = total.astype(BF), 0
    for out in grad_in:
        out[...] = whole[begin : begin + out.shape[0]]
        begin += out.shape[0]


def qkv_back(group, grad_query, grad_kv, grad_halo, cosine, sine, w_own, w_core, width):
    slots, tokens, lanes = grad_query.shape
    rows = tokens // 2
    sizes = (rows, rows // 2, rows // 2) if group else (rows, rows)
    table = pl.BlockSpec((tokens, 128), lambda i: (group, 0))

    def whole(array):
        return pl.BlockSpec(array.shape, lambda i: (0,) * array.ndim)

    outs = [shaped((slots, tokens, lanes), BF)] + [shaped((size, width), BF) for size in sizes]
    return call(
        qkv_back_kernel,
        outs,
        flops=2 * slots * tokens * width * lanes,
        moved=6 * 10**6,
        grid=(1,),
        in_specs=[whole(grad_query), whole(grad_kv), whole(grad_halo), table, table]
        + [whole(w_own), whole(w_core)],
        out_specs=[whole(out) for out in outs],
    )(grad_query, grad_kv, grad_halo, cosine, sine, w_own, w_core)


def lay_out_kernel(d_ref, *refs):
    b0, b1, b2, b3, w_gate, w_up, gain, out_gate, out_up, grad_gain = refs
    ff = b0.shape[2] // 2
    for k, block in enumerate((b0, b1, b2, b3)):
        for y in range(2):
            for z in range(ff // 128):
                to = pl.multiple_of(((2 * z + y) * 4 + (d_ref[0] ^ k)) * 128, 128)
                out_gate[:, pl.ds(to, 128)] = block[y, :, z * 128 : (z + 1) * 128].astype(F32)
                out_up[:, pl.ds(to, 128)] = block[y, :, ff + z * 128 : ff + (z + 1) * 128].astype(F32)
    weighted = w_gate[...].astype(F32) * out_gate[...] + w_up[...].astype(F32) * out_up[...]
    grad_gain[...] = jnp.sum(weighted, axis=-1, keepdims=True) / gain[...]


def lay_out(d, blocks, w_gate, w_up, gain):
    shard, ff = w_gate.shape
    rows = 64
    blocks = [block.reshape(2, shard, block.shape[1]) for block in blocks]
    part = pl.BlockSpec((2, rows, blocks[0].shape[2]), lambda i, d: (0, i, 0))
    whole = pl.BlockSpec((rows, ff), lambda i, d: (i, 0))
    column = pl.BlockSpec((rows, 1), lambda i, d: (i, 0))
    return call(
        lay_out_kernel,
        [shaped((shard, ff), F32), shaped((shard, ff), F32), shaped((shard, 1), F32)],
        flops=6 * shard * ff,
        moved=16 * shard * ff,
        grid_spec=pltpu.PrefetchScalarGridSpec(
            num_scalar_prefetch=1,
            grid=(shard // rows,),
            in_specs=[part] * 4 + [whole, whole, column],
            out_specs=[whole, whole, column],
        ),
    )(d, *blocks, w_gate, w_up, gain)


def lay_out_rows_kernel(d_ref, b0, b1, b2, b3, out):
    rows = b0.shape[0]
    for k, block in enumerate((b0, b1, b2, b3)):
        at = pl.ds(pl.multiple_of((d_ref[0] ^ k) * rows, rows), rows)
        out[at, :] = block[...].astype(F32)


def lay_out_rows(d, blocks):
    rows, width = blocks[0].shape
    vmem = pl.BlockSpec(memory_space=pltpu.VMEM)
    return call(
        lay_out_rows_kernel,
        shaped((4 * rows, width), F32),
        flops=rows * width,
        moved=24 * rows * width,
        in_specs=[pl.BlockSpec(memory_space=pltpu.SMEM)] + [vmem] * 4,
        out_specs=vmem,
    )(d, *blocks)


def lay_out_heads_kernel(d_ref, *refs):
    blocks, (w_query, w_key, w_value, gain) = refs[:4], refs[4:8]
    out_query, out_key, out_value, out_out, grad_gain, ordered = refs[8:]
    shard, lanes = w_query.shape[0], blocks[0].shape[1]
    count = out_out.shape[0] // 4
    for k, block in enumerate(blocks):
        to = d_ref[0] ^ k
        ordered[to] = block[: 2 * shard, :]
        at = pl.ds(pl.multiple_of(to * count, count), count)
        for i in range(4):
            out_out[at, i * lanes : (i + 1) * lanes] = block[
                2 * shard + i * count : 2 * shard + (i + 1) * count, :
            ].astype(F32)
    row, column = iota((lanes, lanes), 0), iota((lanes, lanes), 1)

    def place(begin, count, to):
        hit = (column - to == row - begin) & (row >= begin) & (row < begin + count)
        return jnp.where(hit, 1.0, 0.0).astype(BF)

    def block_of(t):
        return ordered[t // 2, (t % 2) * shard : (t % 2 + 1) * shard, :]

    total = None
    for begin, count, out, w in (
        (0, 2 * HEAD, out_query, w_query),
        (2 * HEAD, HEAD, out_key, w_key),
        (3 * HEAD, HEAD, out_value, w_value),
    ):
        heads = lanes // count
        places = [place(begin, count, i * count) for i in range(heads)]
        for j in range(KV_HEADS // heads):
            piece = None
            for i in range(heads):
                part = dot(block_of(j * heads + i), places[i])
                piece = part if piece is None else piece + part
            at = slice(j * lanes, (j + 1) * lanes)
            out[:, at] = piece
            part = jnp.sum(w[:, at].astype(F32) * piece, axis=-1, keepdims=True)
            total = part if total is None else total + part
    grad_gain[...] = total / gain[...]


def lay_out_heads(d, blocks, w_query, w_key, w_value, gain, out_shape):
    shard = w_query.shape[0]
    vmem = pl.BlockSpec(memory_space=pltpu.VMEM)
    return call(
        lay_out_heads_kernel,
        [
            shaped(w_query.shape, F32),
            shaped(w_key.shape, F32),
            shaped(w_value.shape, F32),
            shaped(out_shape, F32),
            shaped((shard, 1), F32),
        ],
        flops=4 * 10**9,
        moved=8 * 10**6,
        in_specs=[pl.BlockSpec(memory_space=pltpu.SMEM)] + [vmem] * 8,
        out_specs=[vmem] * 5,
        scratch_shapes=[pltpu.VMEM((4, 2 * shard, blocks[0].shape[1]), BF)],
    )(d, *blocks, w_query, w_key, w_value, gain)


def layout_rows(lengths, index):
    ends = jnp.cumsum(lengths, axis=1)
    before = index[None, :, None] >= ends[:, None, :]
    segment = jnp.sum(before.astype(jnp.int32), axis=2)
    offset = jnp.sum(jnp.where(before, lengths[:, None, :], 0), axis=2)
    segment = jnp.where(segment < lengths.shape[1], segment, -1)
    segment = jnp.where(index[None, :] < 0, -3, segment)
    return (segment, index[None, :] - offset)


def on_device(
    tokens,
    lengths,
    cotangent,
    gain_attn,
    w_query,
    w_key,
    w_value,
    w_out,
    gain_mlp,
    w_gate,
    w_up,
    w_down,
):
    n_dp, n_seq = lax.axis_size("dp"), lax.axis_size("seq")
    d, me = lax.axis_index("dp"), lax.axis_index("seq")
    y, n_z = me % 2, n_seq // 2
    rows, width = tokens.shape
    reach = 2 * rows
    assert WINDOW <= reach and KV_HEADS == 2 * n_dp
    groups = HEADS // KV_HEADS
    q_w, k_w = groups * HEAD, HEAD
    shard = w_query.shape[0]
    ff_shard = w_down.shape[0]
    ff_part = ff_shard // n_dp

    def head_columns(j):
        t = 2 * d + j
        gains = jnp.zeros((16, q_w + 2 * k_w), BF)
        gains = gains.at[0, :shard].set(gain_attn).at[1, :shard].set(gain_mlp)
        columns = jnp.concatenate(
            [
                lax.dynamic_slice_in_dim(w_query, t * q_w, q_w, 1),
                lax.dynamic_slice_in_dim(w_key, t * k_w, k_w, 1),
                lax.dynamic_slice_in_dim(w_value, t * k_w, k_w, 1),
            ],
            axis=1,
        )
        return jnp.concatenate([columns, gains], axis=0)

    def ff_columns(j):
        parts = [
            lax.dynamic_slice_in_dim(w, ((2 * z + j) * n_dp + d) * ff_part, ff_part, 1)
            for w in (gate_in, up_in)
            for z in range(n_z)
        ]
        return jnp.concatenate(parts, axis=1)

    lanes = q_w + 2 * k_w
    square = n_seq == 2 * n_dp
    d_arg = jnp.reshape(d, (1,)).astype(jnp.int32)
    z_arg = jnp.reshape(me // 2, (1,)).astype(jnp.int32)

    lens_far = send(lengths, across_x)
    qkv_from_y = send(head_columns(1 - y), across_y)
    tokens_all = gather_plane(tokens, for_y=after(tokens, qkv_from_y))
    low, high = pair_y(head_columns(y), qkv_from_y)
    gain_rows = jnp.concatenate([low[shard:, :shard], high[shard:, :shard]], axis=1)
    gain_rows = jnp.pad(gain_rows, ((0, 0), (0, lanes - 2 * shard)))
    part_qkv = jnp.concatenate([low[:shard], high[:shard], gain_rows], axis=0)
    own_qkv = gather_z(part_qkv)
    lens = jnp.concatenate([lengths, after(lens_far, tokens_all[3])], axis=0)

    first_row = (me // 2) * reach
    steps = jnp.arange(reach, dtype=jnp.int32)
    order = jnp.arange(2, dtype=jnp.int32)[:, None] ^ y
    _, position = layout_rows(lens, first_row + (order * rows + steps[None, :rows]).reshape(-1))
    cosine, sine = rope_tables(position.reshape(-1))
    key_index = first_row - reach + jnp.arange(2 * reach, dtype=jnp.int32)
    segment, _ = layout_rows(lens, key_index)
    segment = jnp.where(segment == -1, -8 - key_index[None, :], segment)
    seg_key = segment.reshape(2, 4, 1, rows)
    seg_query = segment[:, reach:].reshape(2, 2, rows, 1)
    y_arg = jnp.reshape(y, (1,)).astype(jnp.int32)

    gate_in, up_in = lax.optimization_barrier((w_gate, w_up, qkv_from_y))[:2]
    if ff_part % 128 == 0:
        here = jnp.stack([d, y]).astype(jnp.int32)
        mine_ff, other_ff = cut_columns(here, gate_in, up_in, 2 * n_z * ff_part)
    else:
        mine_ff, other_ff = ff_columns(y), ff_columns(1 - y)
    other_ff = send(after(other_ff, tokens_all[1]), across_y)
    part_mlp = jnp.concatenate(
        [
            pair_y(mine_ff, other_ff).reshape(2 * shard, -1),
            fold(lax.dynamic_slice_in_dim(w_down, d * ff_part, ff_part, 0), 2 * n_z * ff_part),
        ],
        axis=0,
    )
    early = ()
    if square:
        out_rows = shard // n_dp
        part_out = lax.dynamic_slice_in_dim(w_out, d * out_rows, out_rows, 0)
        part_out = send(after(part_out, part_qkv), turned)
        early = (part_out,)
    own_qkv = lax.optimization_barrier((own_qkv, part_mlp, cosine, *early, *tokens_all))[0]
    core_qkv = send(own_qkv, across_core)
    if square:
        out_pieces = [send(after(part_out, own_qkv), across_z(k)) for k in (1, 2, 3)]
    else:
        own_out = lax.all_gather(w_out, "seq", axis=0, tiled=True)
        own_out = lax.dynamic_slice_in_dim(own_out, (2 * d + y) * q_w, q_w, 0)
    full_qkv = [own_qkv, core_qkv]
    if not square:
        full_qkv = [part[:, : 2 * shard].reshape(1, width, lanes) for part in full_qkv]
    gains = own_qkv[:, 2 * shard : 2 * shard + 2, : 2 * shard]
    full_gain_attn = gains[:, 0].reshape(1, -1).astype(F32)
    full_gain_mlp = gains[:, 1].reshape(1, -1).astype(F32)

    groups_of = ((0, 1), (2, 3, 4))

    def parts_of(pieces, group):
        return [pieces[i] for i in groups_of[group]]

    normed, qkv, halo, halo_in = [None] * 2, [None] * 2, [None] * 2, [None] * 2
    for group in (1, 0):
        normed[group], qkv[group], halo[group] = project(
            group, parts_of(tokens_all, group), full_gain_attn, cosine, sine, *full_qkv
        )
        halo_in[group] = send(halo[group], lambda d, s: (d, s + 2))
    if square:
        out_pieces = lax.optimization_barrier((*out_pieces, *halo))[:3]
        own_out = jnp.stack([part_out, *out_pieces])
        full_out = place(z_arg, own_out, send(own_out, across_core))
    else:
        full_out = jnp.stack(with_core(own_out))
    part_ready = lax.optimization_barrier((part_mlp, *halo_in))[0]
    if square:
        both = send(part_ready, across_z(2))
        mlp_near = send(part_ready, across_z(1))
    else:
        blocks = gather_z(part_ready)
        down_rows = jnp.concatenate([unfold(blocks[z, 2 * shard :], width) for z in range(n_z)], axis=0)
        own_mlp = [
            jnp.concatenate(
                [blocks[:, : 2 * shard].reshape(width, -1), fold(down_rows, 2 * n_z * ff_part)], axis=0
            )
        ]
    cotangent_in = after(cotangent, normed[1])
    came = (send(cotangent_in, across_x), send(cotangent_in, across_y))
    upstream_all = gather_plane(cotangent, *halo, came=came)
    halo_first = lax.optimization_barrier((halo_in[0], *upstream_all))[0]
    partial, context, logsum = [None] * 2, [None] * 2, [None] * 2
    for group in (1, 0):
        *partial[group], context[group], logsum[group] = attend(
            y_arg, group, qkv[group], halo_in[1] if group else halo_first, seg_query, seg_key, full_out
        )
    arrived = (both, mlp_near) if square else ()
    middle = tokens.astype(F32) + scatter_plane(*partial, *arrived)


    inverse_mlp = lax.rsqrt(jnp.mean(middle * middle, axis=-1, keepdims=True) + EPS)
    normed_mlp_own = (middle * inverse_mlp * full_gain_mlp).astype(BF)
    if square:
        mlp_far = both
        own_mlp = [part_mlp, mlp_near, mlp_far, send(mlp_far, across_z(1))]
    normed_mlp_all = gather_plane(normed_mlp_own)
    core_mlp = [send(block, across_core) for block in own_mlp]
    z_own = z_arg if square else jnp.zeros_like(z_arg)
    hidden, grad_gu, *grad_in, normed_mlp, upstream_low = feed_forward(
        z_own, normed_mlp_all, upstream_all, own_mlp, core_mlp
    )
    grad_near, grad_far = grad_in[:2], grad_in[2:]
    from_core_gu = send(weight_grads(normed_mlp, 0, grad_gu, 1, 2), across_core)
    down_core = weight_grads(hidden, 1, upstream_low, 0, 1)
    grad_w_gu = weight_grads(normed_mlp, 0, grad_gu, 0, 2, from_core_gu)
    grad_normed_mlp = scatter_plane(grad_near, grad_far, at_first=(down_core, grad_w_gu))
    got_gu = along_z(grad_w_gu.reshape(n_z, 2 * shard, -1))
    total_gu = jnp.sum(got_gu.astype(F32), axis=0).astype(BF)
    upstream = cotangent.astype(F32)
    scaled = grad_normed_mlp * full_gain_mlp
    grad_middle = (
        upstream
        + inverse_mlp * scaled
        - middle * inverse_mlp**3 * jnp.mean(scaled * middle, axis=-1, keepdims=True)
    )
    down = down_project(z_own, hidden, own_mlp, core_mlp, width)
    from_core = send(down_core, across_core)
    grad_w_down = weight_grads(hidden, 0, upstream_low, 0, 1, from_core)
    grad_attended_all = gather_plane(
        after(grad_middle.astype(BF), grad_w_gu), *down, grad_w_down
    )
    down = lax.optimization_barrier((*down, *grad_attended_all))[:5]
    (own, own_y), (far, far_a, far_b) = down[:2], down[2:]
    half = rows // 2
    first, second = send(far_a, across_y), send(far_b, across_x)

    def swap_rows(total):
        mine = lax.dynamic_slice_in_dim(total, y * shard, shard, 0)
        other = lax.dynamic_slice_in_dim(total, (1 - y) * shard, shard, 0)
        return pair_y(mine, send(other, across_y)).reshape(2 * shard, -1)

    mine_gu = swap_rows(total_gu)
    gu_blocks = gather_dp(mine_gu)
    if ff_part % 128 == 0:
        gain_column = gain_mlp.astype(F32).reshape(-1, 1)
        out_gate, out_up, grad_gain_mlp = lay_out(d_arg, gu_blocks, w_gate, w_up, gain_column)
    else:
        all_gu = jnp.stack(order_dp(gu_blocks)).reshape(n_dp, 2, shard, 2, n_z, ff_part)
        all_gu = all_gu.transpose(3, 2, 4, 1, 0, 5).reshape(2, shard, -1).astype(F32)
        out_gate, out_up = all_gu[0], all_gu[1]
        grad_gain_mlp = jnp.sum(
            w_gate.astype(F32) * out_gate + w_up.astype(F32) * out_up, axis=1
        ) / gain_mlp.astype(F32)

    grad_query, grad_kv, halo_back = [None] * 2, [None] * 2, [None] * 2
    grad_out = ()
    for group in (0, 1):
        dy = parts_of(grad_attended_all, group)
        grad_query[group], grad_kv[group], grad_halo, grad_out = attend_back(
            y_arg, group, qkv[group], halo_in[group], seg_query, seg_key, full_out,
            context[group], logsum[group], cosine, sine, dy, (grad_out,) if group else (),
        )
        grad_halo, first, second = lax.optimization_barrier((grad_halo, first, second, got_gu))[:3]
        halo_back[group] = send(grad_halo, lambda d, s: (d, s - 2))
    grad_qkv, grad_in = [None] * 2, [None] * 2
    far = jnp.concatenate([plus(far[:half], first), far[half:]], axis=0)
    own_y = jnp.concatenate([own_y[:half], plus(own_y[half:], second)], axis=0)
    down_x, down_y = send(far, across_x), send(own_y, across_y)
    halo_back[1] = after(halo_back[1], mine_gu)
    for group in (0, 1):
        grad_qkv[group], *grad_in[group] = qkv_back(
            group, grad_query[group], grad_kv[group], halo_back[group], cosine, sine, *full_qkv, width
        )
    grad_w_down = lax.optimization_barrier((grad_w_down, halo_back[1]))[0]
    total_down = scatter_z(grad_w_down.reshape(n_z, ff_part, width)).astype(BF)
    out_down = lay_out_rows(d_arg, gather_dp(total_down))

    def attn_grads(slot):
        for_qkv = dot_tn(normed[0], grad_qkv[0][slot]) + dot_tn(normed[1], grad_qkv[1][slot])
        for_qkv = for_qkv.astype(BF).reshape(n_z, 2 * shard, -1)
        if not square:
            return for_qkv
        for_out = [
            fold(grad_out[slot, z * out_rows : (z + 1) * out_rows], lanes) for z in range(n_z)
        ]
        return jnp.concatenate([for_qkv, jnp.stack(for_out)], axis=1)

    grad_attn = sum_core(attn_grads(0), attn_grads(1))
    output = (
        middle + own.astype(F32) + down_x.astype(F32) + down_y.astype(F32)
    ).astype(BF)
    total_attn = along_z(grad_attn)
    total_attn = jnp.sum(total_attn.astype(F32), axis=0).astype(BF)
    mine_attn = swap_rows(total_attn[: 2 * shard]).reshape(2 * shard, -1)
    if square:
        mine_attn = jnp.concatenate([mine_attn, send(total_attn[2 * shard :], turned)], axis=0)
    attn_blocks = gather_dp(mine_attn, out_gate, out_down)
    if square:
        out_query, out_key, out_value, out_out, grad_gain_attn = lay_out_heads(
            d_arg, attn_blocks, w_query, w_key, w_value, gain_attn.astype(F32).reshape(-1, 1), w_out.shape
        )
    else:
        attn_blocks = order_dp(attn_blocks)
        grad_w_out = sum_core(grad_out[0], grad_out[1]).astype(F32)
        out_out = jnp.zeros((2 * n_dp * q_w, width), F32)
        out_out = lax.dynamic_update_slice_in_dim(out_out, grad_w_out, (2 * d + y) * q_w, 0)
        out_out = lax.psum_scatter(out_out, "seq", scatter_dimension=0, tiled=True)
        out_out = lax.psum(out_out.astype(BF), "dp").astype(F32)
        all_qkv = jnp.stack(attn_blocks).astype(F32)
        out_qkv = all_qkv.reshape(2 * n_dp, shard, lanes).transpose(1, 0, 2)
        out_query = out_qkv[..., :q_w].reshape(shard, -1)
        out_key = out_qkv[..., q_w : q_w + k_w].reshape(shard, -1)
        out_value = out_qkv[..., q_w + k_w :].reshape(shard, -1)
        grad_gain_attn = (
            jnp.sum(w_query.astype(F32) * out_query, axis=1)
            + jnp.sum(w_key.astype(F32) * out_key, axis=1)
            + jnp.sum(w_value.astype(F32) * out_value, axis=1)
        ) / gain_attn.astype(F32)

    own = scatter_plane(*grad_in, at_first=(down_x, down_y))
    wide = tokens.astype(F32)
    own_inverse = lax.rsqrt(jnp.mean(wide * wide, axis=-1, keepdims=True) + EPS)
    scaled = own * full_gain_attn
    grad_tokens = (
        grad_middle
        + own_inverse * scaled
        - wide * own_inverse**3 * jnp.mean(scaled * wide, axis=-1, keepdims=True)
    )
    return (
        output,
        grad_tokens,
        grad_gain_attn.reshape(-1),
        out_query,
        out_key,
        out_value,
        out_out,
        grad_gain_mlp.reshape(-1),
        out_gate,
        out_up,
        out_down,
    )


def solution(mesh):
    return jax.shard_map(
        on_device,
        mesh=mesh,
        in_specs=(
            P(("dp", "seq"), None),
            P("dp", None),
            P(("dp", "seq"), None),
            P("seq"),
            P("seq", None),
            P("seq", None),
            P("seq", None),
            P("seq", None),
            P("seq"),
            P("seq", None),
            P("seq", None),
            P("seq", None),
        ),
        out_specs=(
            P(("dp", "seq"), None),
            P(("dp", "seq"), None),
            P("seq"),
            P("seq", None),
            P("seq", None),
            P("seq", None),
            P("seq", None),
            P("seq"),
            P("seq", None),
            P("seq", None),
            P("seq", None),
        ),
        check_vma=False,
    )
```
